32 devices in a mesh: groups: 2 (over x), node: 16 (over z, y, core).
Axes of the slice: x: 2, y: 2, z: 4, core: 2. Of those that a mesh axis runs over, the one named last changes fastest.
Arguments:
- hidden: bfloat16 [16384, 8192], P(('groups', 'node')), parts along dimension 0, may hold values from -60 to 60
- queries: bfloat16 [16384, 4096], P(('groups', 'node')), parts along dimension 0, may hold values from -240 to 240
- norm_gain: float32 [8192], replicated, may hold values from 0.5 to 2
- key_weight: bfloat16 [8192, 512], replicated, may hold values from -0.0625 to 0.0625
- value_weight: bfloat16 [8192, 512], replicated, may hold values from -0.0625 to 0.0625
- anc_ids: int32 [256, 7], P(('groups', 'node')), parts along dimension 0, may hold values from -1 to 111, as said below
- anc_cut: int32 [256, 7], P(('groups', 'node')), parts along dimension 0, may hold values from 0 to 64, as said below
Outputs:
- context: bfloat16 [16384, 4096], P(('groups', 'node')), parts along dimension 0
The draws below stay inside these ranges and needn't reach their ends.
There are 2 independent parts, one for each index of `groups`. The reference program is written for one: setup_inputs(seed, part) draws one part's arguments, and reference() takes and returns one part's arrays. A program takes and returns all parts, laid end to end along the dimension named above; an argument that names none is the same for every part. Nothing has to cross between parts.
Inputs may be any that keep to these rules, and one draw needn't show every extreme that they name: `anc_ids`: block g lies on node index g // 8 and has depth d = (g // 8) // 2. Column k of its row, for k < d, names its (k+1)-th nearest ancestor, which lies on node index g // 8 - (k+1) * 2; columns k >= d hold -1. The list of a block's parent is the block's list shifted by one column. `anc_cut`: 0 exactly where anc_ids is -1. Column k + 1 of a block equals column k of its parent.
All inputs are finite; a program needn't handle non-finite values.
Results may differ from the reference program's by a relative error of at most 0.012.
The reference program's roundings to bfloat16 on the way (of `normed` and `weights`) count: a program that leaves them out, or rounds other values in their place, can miss the bound.
Values may be sent and summed in bfloat16 or wider, within the bound.
No kernel may reach another device: no remote copies, remote signals or barrier semaphores. Data moves between devices by JAX's collectives and lax.ppermute only.
A program may use at most 256 MiB of HBM per device.

```python
import math
import jax
import jax.numpy as jnp
from jax import lax

D = 8192
HEADS = 32
KV_HEADS = 4
HEAD_DIM = 128
BLOCK = 64
LEVELS = 8
BLK_DEV = 8
CHAINS = 2
BLOCKS = 128
TOKENS = 8192
KW = 512


def forest_tables(key):
    key = jax.random.fold_in(key, 101)
    first_key, second_key = jax.random.split(key)
    blocks = jnp.arange(BLOCKS)
    device = blocks // BLK_DEV
    slot = blocks % BLK_DEV
    parent_slot = jax.random.randint(first_key, (BLOCKS,), 0, BLK_DEV)
    parent_slot = jnp.where(slot == 0, BLK_DEV - 1, parent_slot)
    first_cut = jax.random.randint(second_key, (BLOCKS,), 1, BLOCK + 1)
    first_cut = jnp.where(slot == 0, BLOCK, first_cut)
    has_parent = device >= CHAINS
    parent = jnp.where(has_parent, (device - CHAINS) * BLK_DEV + parent_slot, -1)
    parent_cut = jnp.where(has_parent, first_cut, 0)
    id_columns = [parent]
    cut_columns = [parent_cut]
    previous = parent
    for column in range(1, LEVELS - 1):
        safe = jnp.maximum(previous, 0)
        following = jnp.where(previous >= 0, jnp.take(parent, safe), -1)
        following_cut = jnp.where(previous >= 0, jnp.take(parent_cut, safe), 0)
        id_columns.append(following)
        cut_columns.append(following_cut)
        previous = following
    return (jnp.stack(id_columns, axis=1).astype(jnp.int32), jnp.stack(cut_columns, axis=1).astype(jnp.int32))


def draw_anc_ids(key, part):
    shared = forest_tables(key)
    return shared[0]


def draw_anc_cut(key, part):
    shared = forest_tables(key)
    return shared[1]


def draw_hidden(key, part):
    key = jax.random.fold_in(key, 3)
    row_key, col_key, base_key = jax.random.split(key, 3)
    row_scale = jnp.exp(jax.random.uniform(row_key, (TOKENS, 1), jnp.float32, 0.0, math.log(10.0)))
    col_scale = jnp.exp(jax.random.uniform(col_key, (1, D), jnp.float32, 0.0, math.log(10.0)))
    base = jax.random.normal(base_key, (TOKENS, D), jnp.float32)
    return jnp.clip(base * row_scale * col_scale / 10.0, -60.0, 60.0).astype(jnp.bfloat16)


def draw_queries(key, part):
    key = jax.random.fold_in(key, 4)
    row_key, base_key = jax.random.split(key)
    top = 4.0
    bottom = 0.5
    row_scale = jnp.exp(jax.random.uniform(row_key, (TOKENS, 1), jnp.float32, math.log(bottom), math.log(top)))
    base = jnp.clip(jax.random.normal(base_key, (TOKENS, HEADS * HEAD_DIM), jnp.float32), -6.0, 6.0)
    return jnp.clip(base * row_scale, -240.0, 240.0).astype(jnp.bfloat16)


def noise(key, shape, spread, limit, held_as=jnp.bfloat16):
    values = jax.random.normal(key, shape, jnp.float32) * spread
    return jnp.minimum(jnp.maximum(values, -limit), limit).astype(held_as)


def setup_inputs(seed: int = 0, part: int = 0) -> dict:
    key_list = jax.random.split(jax.random.key(seed), 8)
    part_splits = jax.random.split(jax.random.fold_in(key_list[7], part), 8)
    return {
        "hidden": draw_hidden(jax.random.fold_in(jax.random.fold_in(key_list[7], part), 71), part),
        "queries": draw_queries(jax.random.fold_in(jax.random.fold_in(key_list[7], part), 71), part),
        "norm_gain": jnp.clip(jnp.exp(jax.random.uniform(key_list[2], (D,), jnp.float32, math.log(0.5), math.log(2.0))), 0.5, 2.0),
        "key_weight": noise(key_list[3], (D, KW), D ** -0.5, 0.0625),
        "value_weight": noise(key_list[4], (D, KW), D ** -0.5, 0.0625),
        "anc_ids": draw_anc_ids(jax.random.fold_in(jax.random.fold_in(key_list[7], part), 71), part),
        "anc_cut": draw_anc_cut(jax.random.fold_in(jax.random.fold_in(key_list[7], part), 71), part),
    }


def visibility(cuts, block):
    offsets = jnp.arange(block)
    count, depth = cuts.shape
    seen = offsets[None, None, :] < cuts[:, :, None]
    seen = jnp.broadcast_to(seen.reshape(count, 1, depth * block), (count, block, depth * block))
    causal = offsets[None, :] <= offsets[:, None]
    causal = jnp.broadcast_to(causal[None], (count, block, block))
    return jnp.concatenate([seen, causal], axis=2).astype(jnp.int32)

def reference(hidden, queries, norm_gain, key_weight, value_weight, anc_ids, anc_cut):
    x = hidden.astype(jnp.float32)
    mean_sq = lax.optimization_barrier(jnp.mean(x * x, axis=-1, keepdims=True))
    inverse = lax.rsqrt(mean_sq + 1e-05)
    normed = (x * inverse * norm_gain).astype(jnp.bfloat16)
    keys = jnp.dot(normed, key_weight, preferred_element_type=jnp.float32).astype(jnp.bfloat16)
    values = jnp.dot(normed, value_weight, preferred_element_type=jnp.float32).astype(jnp.bfloat16)
    width = KV_HEADS * HEAD_DIM
    group = HEADS // KV_HEADS
    stacked = jnp.concatenate([keys, values], axis=1).reshape(BLOCKS, BLOCK, 2 * width)
    query_blocks = queries.reshape(BLOCKS, BLOCK, KV_HEADS, group, HEAD_DIM)

    def one_block(index):
        ids = anc_ids[index]
        safe = jnp.maximum(ids, 0)
        picked = stacked[safe]
        every = jnp.concatenate([picked, stacked[index][None]], axis=0).reshape(LEVELS * BLOCK, 2 * width)
        key_part = every[:, :width].astype(jnp.float32).reshape(LEVELS * BLOCK, KV_HEADS, HEAD_DIM)
        value_part = every[:, width:].astype(jnp.float32).reshape(LEVELS * BLOCK, KV_HEADS, HEAD_DIM)
        query_part = query_blocks[index].astype(jnp.float32)
        scores = jnp.einsum('qgrd,kgd->grqk', query_part, key_part) * HEAD_DIM ** (-0.5)
        visible = visibility(anc_cut[index][None], BLOCK)[0]
        scores = jnp.where(visible[None, None] > 0, scores, -1e+30)
        peak = lax.optimization_barrier(jnp.max(scores, axis=-1, keepdims=True))
        expd = jnp.exp(scores - peak)
        total = lax.optimization_barrier(jnp.sum(expd, axis=-1, keepdims=True))
        weights = (expd / total).astype(jnp.bfloat16)
        out = jnp.einsum('grqk,kgd->qgrd', weights.astype(jnp.float32), value_part)
        return out.astype(jnp.bfloat16).reshape(BLOCK, HEADS * HEAD_DIM)
    result = lax.map(one_block, jnp.arange(BLOCKS))
    return result.reshape(TOKENS, HEADS * HEAD_DIM)
```

```python
import functools
import jax
import jax.numpy as jnp
from jax import lax
from jax.experimental import pallas as pl
from jax.experimental.pallas import tpu as pltpu
from jax.sharding import PartitionSpec as P

HEAD_DIM = 128
EPS = 1e-05
LOG2E = 1.4426950408889634
MASKED = -1e30
VMEM_BYTES = 56 * 1024 * 1024


def norm_project_kernel(x_ref, gain_ref, key_ref, value_ref, normed_ref, kv_ref):
    rows, features = x_ref.shape
    chunk = 512

    def square(c, acc):
        cols = pl.ds(pl.multiple_of(c * chunk, chunk), chunk)
        x = x_ref[:, cols].astype(jnp.float32)
        return acc + x * x

    acc = lax.fori_loop(0, features // chunk, square, jnp.zeros((rows, chunk), jnp.float32))
    mean_sq = jnp.sum(acc, axis=-1, keepdims=True) / features
    inverse = lax.rsqrt(mean_sq + EPS)

    def scale(c, carry):
        cols = pl.ds(pl.multiple_of(c * chunk, chunk), chunk)
        x = x_ref[:, cols].astype(jnp.float32)
        normed_ref[:, cols] = (x * inverse * gain_ref[:, cols]).astype(jnp.bfloat16)
        return carry

    lax.fori_loop(0, features // chunk, scale, 0)
    normed = normed_ref[...]
    for col, weight in enumerate((key_ref, value_ref)):
        part = jnp.dot(normed, weight[...], preferred_element_type=jnp.float32)
        kv_ref[:, col * HEAD_DIM : (col + 1) * HEAD_DIM] = part.astype(jnp.bfloat16)


def norm_project(hidden, gain, key_weight, value_weight):
    rows, features = hidden.shape
    step = rows // 4
    weight = pl.BlockSpec((features, HEAD_DIM), lambda i: (0, 0), pipeline_mode=pl.Buffered(1))
    return pl.pallas_call(
        norm_project_kernel,
        grid=(rows // step,),
        in_specs=[
            pl.BlockSpec((step, features), lambda i: (i, 0)),
            pl.BlockSpec((1, features), lambda i: (0, 0), pipeline_mode=pl.Buffered(1)),
            weight,
            weight,
        ],
        out_specs=[
            pl.BlockSpec((step, features), lambda i: (i, 0)),
            pl.BlockSpec((step, 2 * HEAD_DIM), lambda i: (i, 0)),
        ],
        out_shape=[
            jax.ShapeDtypeStruct((rows, features), jnp.bfloat16),
            jax.ShapeDtypeStruct((rows, 2 * HEAD_DIM), jnp.bfloat16),
        ],
        compiler_params=pltpu.CompilerParams(vmem_limit_bytes=VMEM_BYTES),
        cost_estimate=pl.CostEstimate(
            flops=4 * rows * features * HEAD_DIM, bytes_accessed=20 << 20, transcendentals=0
        ),
        name="norm_project",
    )(hidden, gain.reshape(1, features), key_weight, value_weight)


def project_kernel(normed_ref, key_ref, value_ref, *kv_refs):
    head = pl.program_id(0)
    normed = normed_ref[...]
    for col, weight in enumerate((key_ref, value_ref)):
        part = jnp.dot(normed, weight[...], preferred_element_type=jnp.float32).astype(jnp.bfloat16)
        for index, kv_ref in enumerate(kv_refs):

            @pl.when(head == index)
            def _(kv_ref=kv_ref, part=part, col=col):
                kv_ref[:, col * HEAD_DIM : (col + 1) * HEAD_DIM] = part


def project(normed, key_weight, value_weight, heads):
    rows, features = normed.shape
    weight = pl.BlockSpec((features, HEAD_DIM), lambda h: (0, h + 1))
    return pl.pallas_call(
        project_kernel,
        grid=(heads,),
        in_specs=[
            pl.BlockSpec((rows, features), lambda h: (0, 0), pipeline_mode=pl.Buffered(1)),
            weight,
            weight,
        ],
        out_specs=[pl.BlockSpec((rows, 2 * HEAD_DIM), lambda h: (0, 0)) for _ in range(heads)],
        out_shape=[jax.ShapeDtypeStruct((rows, 2 * HEAD_DIM), jnp.bfloat16) for _ in range(heads)],
        compiler_params=pltpu.CompilerParams(vmem_limit_bytes=VMEM_BYTES),
        cost_estimate=pl.CostEstimate(
            flops=4 * heads * rows * features * HEAD_DIM, bytes_accessed=20 << 20, transcendentals=0
        ),
        name="project",
    )(normed, key_weight, value_weight)


def attention_kernel(block, per_group, near, slot_ref, cut_ref, odd_ref, q_ref, own_ref, *refs):
    out_ref = refs[-1]
    straight, crossed = refs[:near], refs[near : 2 * near + 1]
    depth = slot_ref.shape[1]
    here = pl.program_id(0)
    odd = odd_ref[0] == 1
    pieces = []
    for k in range(depth):
        rows = pl.ds(pl.multiple_of(slot_ref[here, k] * block, block), block)
        if k % 2 == 1:
            pieces.append(straight[k // 2][rows, :])
        else:
            low = crossed[k // 2][rows, :]
            high = crossed[min(k // 2 + 1, near)][rows, :]
            pieces.append(jnp.where(odd, low, high))
    pieces.append(own_ref[pl.ds(pl.multiple_of(here * block, block), block), :])
    every = jnp.concatenate(pieces, axis=0)
    width = (depth + 1) * block
    keys, values = every[:, :HEAD_DIM], every[:, HEAD_DIM:]
    lane = lax.broadcasted_iota(jnp.int32, (block, width), 1)
    token = lax.broadcasted_iota(jnp.int32, (block, width), 0)
    limit = jnp.where(lane >= depth * block, token + (depth * block + 1), 0)
    for k in range(depth):
        inside = (lane >= k * block) & (lane < (k + 1) * block)
        limit = jnp.where(inside, cut_ref[here, k] + k * block, limit)
    bias = jnp.where(lane < limit, 0.0, MASKED)
    queries = jnp.concatenate(
        [q_ref[:, r * HEAD_DIM : (r + 1) * HEAD_DIM] for r in range(per_group)], axis=0
    )
    scores = lax.dot_general(
        queries, keys, (((1,), (1,)), ((), ())), preferred_element_type=jnp.float32
    )
    scores = (scores.reshape(per_group, block, width) + bias[None]).reshape(per_group * block, width)
    peak = jnp.max(scores, axis=-1, keepdims=True)
    weights = jnp.exp2((scores - peak) * (HEAD_DIM**-0.5 * LOG2E)).astype(jnp.bfloat16)
    padded = jnp.concatenate([values, jnp.ones_like(values)], axis=1)
    both = jnp.dot(weights, padded, preferred_element_type=jnp.float32)
    context = (both[:, :HEAD_DIM] / both[:, HEAD_DIM:]).astype(jnp.bfloat16)
    for r in range(per_group):
        out_ref[:, r * HEAD_DIM : (r + 1) * HEAD_DIM] = context[r * block : (r + 1) * block]


def attention(slots, cuts, odd, queries, own, straight, crossed, head, heads, previous):
    rows, features = queries.shape
    blocks = slots.shape[0]
    block = rows // blocks
    wide = features // heads
    near = len(straight)
    whole = pl.BlockSpec(own.shape, lambda b, *_: (0, 0), pipeline_mode=pl.Buffered(1))
    part = pl.BlockSpec((block, wide), lambda b, *_: (b, head))
    operands = [slots, cuts, odd, queries, own, *straight, *crossed]
    in_specs = [part] + [whole] * (1 + near + len(crossed))
    aliases = {}
    if previous is not None:
        aliases = {len(operands): 0}
        operands.append(previous)
        in_specs.append(pl.BlockSpec(memory_space=pl.ANY))
    return pl.pallas_call(
        functools.partial(attention_kernel, block, wide // HEAD_DIM, near),
        grid_spec=pltpu.PrefetchScalarGridSpec(
            num_scalar_prefetch=3, grid=(blocks,), in_specs=in_specs, out_specs=part
        ),
        out_shape=jax.ShapeDtypeStruct((rows, features), jnp.bfloat16),
        input_output_aliases=aliases,
        compiler_params=pltpu.CompilerParams(vmem_limit_bytes=VMEM_BYTES),
        cost_estimate=pl.CostEstimate(
            flops=4 * rows * features // heads * 8 * block,
            bytes_accessed=4 << 20,
            transcendentals=rows * wide // HEAD_DIM * 8 * block,
        ),
        name="attention",
    )(*operands)


def shards(hidden, queries, norm_gain, key_weight, value_weight, anc_ids, anc_cut):
    blocks, depth = anc_ids.shape
    levels = depth + 1
    size = lax.axis_size("node")
    chains = size // levels
    heads = key_weight.shape[1] // HEAD_DIM
    near = depth // 2
    half = [index // chains // 2 for index in range(size)]
    even = [index // chains % 2 == 0 for index in range(size)]
    other = [index + chains if even[index] else index - chains for index in range(size)]
    odd = (lax.axis_index("node") // chains % 2).astype(jnp.int32).reshape(1)
    slots = jnp.where(anc_ids >= 0, anc_ids % blocks, 0)

    normed, first = norm_project(hidden, norm_gain, key_weight, value_weight)
    rest = project(normed, key_weight, value_weight, heads - 1)
    own = [first, *rest]
    result = None
    for head in range(heads):
        piece = own[head]
        straight = [
            lax.ppermute(
                piece,
                "node",
                [(i, i + 2 * s * chains) for i in range(size) if i + 2 * s * chains < size],
            )
            for s in range(1, near + 1)
        ]
        crossed = [lax.ppermute(piece, "node", [(i, other[i]) for i in range(size) if even[i]])]
        for s in range(1, near + 1):
            pairs = [(i, other[i]) for i in range(size) if half[i] >= s]
            crossed.append(lax.ppermute(straight[s - 1], "node", pairs))
        result = attention(
            slots, anc_cut, odd, queries, piece, straight, crossed, head, heads, result
        )
    return result


def solution(mesh):
    placed = (
        P(("groups", "node"), None),
        P(("groups", "node"), None),
        P(),
        P(),
        P(),
        P(("groups", "node"), None),
        P(("groups", "node"), None),
    )
    return jax.shard_map(
        shards, mesh=mesh, in_specs=placed, out_specs=P(("groups", "node"), None), check_vma=False
    )
```

```python
import functools
import jax
import jax.numpy as jnp
from jax import lax
from jax.experimental import pallas as pl
from jax.experimental.pallas import tpu as pltpu
from jax.sharding import PartitionSpec as P

HEAD_DIM = 128
EPS = 1e-05
LOG2E = 1.4426950408889634
MASKED = -1e30
MIB = 1024 * 1024
CHUNKS = 4
UNITS = 2


def norm_project_kernel(x_ref, gain_ref, key_ref, value_ref, normed_ref, kv_ref, x_scr, sq_scr, acc_scr):
    step = pl.program_id(0)
    rows, chunk = x_ref.shape
    features = chunk * CHUNKS
    width = key_ref.shape[1]
    lanes = 128

    @pl.when(step < CHUNKS)
    def _():
        acc = jnp.zeros((rows, lanes), jnp.float32)
        for c in range(chunk // lanes):
            x = x_ref[:, c * lanes : (c + 1) * lanes].astype(jnp.float32)
            acc += x * x
        x_scr[step] = x_ref[...]
        sq_scr[...] = jnp.where(step == 0, acc, sq_scr[...] + acc)

    @pl.when(step == CHUNKS)
    def _():
        mean_sq = jnp.sum(sq_scr[...], axis=-1, keepdims=True) / features
        sq_scr[...] = jnp.broadcast_to(lax.rsqrt(mean_sq + EPS), sq_scr.shape)

    @pl.when(step >= CHUNKS)
    def _():
        index = step - CHUNKS
        for c in range(chunk // lanes):
            cols = slice(c * lanes, (c + 1) * lanes)
            x = x_scr[index, :, cols].astype(jnp.float32)
            normed_ref[:, cols] = (x * sq_scr[...] * gain_ref[:, cols]).astype(jnp.bfloat16)
        normed = normed_ref[...]
        for part, weight in enumerate((key_ref, value_ref)):
            cols = slice(part * width, (part + 1) * width)
            term = jnp.dot(normed, weight[...], preferred_element_type=jnp.float32)
            total = jnp.where(index == 0, term, acc_scr[:, cols] + term)
            acc_scr[:, cols] = total

    @pl.when(step == 2 * CHUNKS - 1)
    def _():
        kv_ref[...] = acc_scr[...].astype(jnp.bfloat16)


def norm_project(hidden, gain, key_weight, value_weight):
    rows, features = hidden.shape
    chunk = features // CHUNKS
    width = key_weight.shape[1] // UNITS
    second = lambda i: jnp.maximum(i - CHUNKS, 0)
    weight = pl.BlockSpec((chunk, width), lambda i: (second(i), 0))
    return pl.pallas_call(
        norm_project_kernel,
        grid=(2 * CHUNKS,),
        in_specs=[
            pl.BlockSpec((rows, chunk), lambda i: (0, jnp.minimum(i, CHUNKS - 1))),
            pl.BlockSpec((1, chunk), lambda i: (0, second(i))),
            weight,
            weight,
        ],
        out_specs=[
            pl.BlockSpec((rows, chunk), lambda i: (0, second(i))),
            pl.BlockSpec((rows, 2 * width), lambda i: (0, 0)),
        ],
        out_shape=[
            jax.ShapeDtypeStruct((rows, features), jnp.bfloat16),
            jax.ShapeDtypeStruct((rows, 2 * width), jnp.bfloat16),
        ],
        scratch_shapes=[
            pltpu.VMEM((CHUNKS, rows, chunk), jnp.bfloat16),
            pltpu.VMEM((rows, 128), jnp.float32),
            pltpu.VMEM((rows, 2 * width), jnp.float32),
        ],
        compiler_params=pltpu.CompilerParams(vmem_limit_bytes=36 * MIB),
        cost_estimate=pl.CostEstimate(
            flops=4 * rows * features * width, bytes_accessed=24 * MIB, transcendentals=0
        ),
        name="norm_project",
    )(hidden, gain.reshape(1, features), key_weight, value_weight)


def project_kernel(normed_ref, key_ref, value_ref, kv_ref, acc_scr):
    step = pl.program_id(0)
    width = key_ref.shape[1]
    normed = normed_ref[...]
    for part, weight in enumerate((key_ref, value_ref)):
        cols = slice(part * width, (part + 1) * width)
        term = jnp.dot(normed, weight[...], preferred_element_type=jnp.float32)
        acc_scr[:, cols] = jnp.where(step == 0, term, acc_scr[:, cols] + term)

    @pl.when(step == CHUNKS - 1)
    def _():
        kv_ref[...] = acc_scr[...].astype(jnp.bfloat16)


def project(normed, key_weight, value_weight, unit):
    rows, features = normed.shape
    chunk = features // CHUNKS
    width = key_weight.shape[1] // UNITS
    weight = pl.BlockSpec((chunk, width), lambda i: (i, unit))
    return pl.pallas_call(
        project_kernel,
        grid=(CHUNKS,),
        in_specs=[pl.BlockSpec((rows, chunk), lambda i: (0, i)), weight, weight],
        out_specs=pl.BlockSpec((rows, 2 * width), lambda i: (0, 0)),
        out_shape=jax.ShapeDtypeStruct((rows, 2 * width), jnp.bfloat16),
        scratch_shapes=[pltpu.VMEM((rows, 2 * width), jnp.float32)],
        compiler_params=pltpu.CompilerParams(vmem_limit_bytes=24 * MIB),
        cost_estimate=pl.CostEstimate(
            flops=4 * rows * features * width, bytes_accessed=16 * MIB, transcendentals=0
        ),
        name="project",
    )(normed, key_weight, value_weight)


def attention_kernel(block, kv_heads, near, slot_ref, cut_ref, odd_ref, q_ref, own_ref, *refs):
    out_ref = refs[-1]
    straight, crossed = refs[:near], refs[near : 2 * near + 1]
    depth = slot_ref.shape[1]
    here = pl.program_id(0)
    odd = odd_ref[0] == 1
    per_group = q_ref.shape[1] // HEAD_DIM // kv_heads
    tile = 256
    together = tile // block
    scale = HEAD_DIM**-0.5 * LOG2E
    pieces = []
    for k in range(depth):
        rows = pl.ds(pl.multiple_of(slot_ref[here, k] * block, block), block)
        if k % 2 == 1:
            pieces.append(straight[k // 2][rows, :])
        else:
            low = crossed[k // 2][rows, :]
            high = crossed[min(k // 2 + 1, near)][rows, :]
            pieces.append(jnp.where(odd, low, high))
    pieces.append(own_ref[pl.ds(pl.multiple_of(here * block, block), block), :])
    every = jnp.concatenate(pieces, axis=0)
    token = lax.broadcasted_iota(jnp.int32, (block, 128), 0)
    lane = lax.broadcasted_iota(jnp.int32, (block, 128), 1)
    bias = []
    for k in range(depth):
        bias.append(jnp.where(token < cut_ref[here, k], 0.0, MASKED))
    bias.append(jnp.where(token <= lane % block, 0.0, MASKED))
    bias = [jnp.concatenate([b] * (tile // 128), axis=1) for b in bias]
    for head in range(kv_heads):
        keys = every[:, head * HEAD_DIM : (head + 1) * HEAD_DIM]
        values = every[:, (kv_heads + head) * HEAD_DIM : (kv_heads + head + 1) * HEAD_DIM]
        flipped = jnp.concatenate(
            [values.T, jnp.ones((16, values.shape[0]), jnp.bfloat16)], axis=0
        )
        for first in range(head * per_group, (head + 1) * per_group, together):
            queries = jnp.concatenate(
                [
                    q_ref[:, r * HEAD_DIM : (r + 1) * HEAD_DIM]
                    for r in range(first, first + together)
                ],
                axis=0,
            )
            scores = lax.dot_general(
                keys, queries, (((1,), (1,)), ((), ())), preferred_element_type=jnp.float32
            )
            parts = [scores[k * block : (k + 1) * block] + bias[k] for k in range(depth + 1)]
            peak = functools.reduce(jnp.maximum, parts)
            peak = jnp.max(peak, axis=0, keepdims=True)
            weights = jnp.concatenate(
                [jnp.exp2((part - peak) * scale).astype(jnp.bfloat16) for part in parts], axis=0
            )
            both = jnp.dot(flipped, weights, preferred_element_type=jnp.float32)
            context = both[:HEAD_DIM] * (1.0 / both[HEAD_DIM : HEAD_DIM + 1])
            context = context.T.astype(jnp.bfloat16)
            for r in range(together):
                cols = slice((first + r) * HEAD_DIM, (first + r + 1) * HEAD_DIM)
                out_ref[:, cols] = context[r * block : (r + 1) * block]


def attention(slots, cuts, odd, queries, own, straight, crossed, unit, previous):
    rows, features = queries.shape
    blocks, depth = slots.shape
    block = rows // blocks
    wide = features // UNITS
    near = len(straight)
    kv_heads = own.shape[1] // (2 * HEAD_DIM)
    whole = pl.BlockSpec(own.shape, lambda b, *_: (0, 0), pipeline_mode=pl.Buffered(1))
    part = pl.BlockSpec((block, wide), lambda b, *_: (b, unit))
    operands = [slots, cuts, odd, queries, own, *straight, *crossed]
    in_specs = [part] + [whole] * (1 + near + len(crossed))
    aliases = {}
    if previous is not None:
        aliases = {len(operands): 0}
        operands.append(previous)
        in_specs.append(pl.BlockSpec(memory_space=pl.ANY))
    return pl.pallas_call(
        functools.partial(attention_kernel, block, kv_heads, near),
        grid_spec=pltpu.PrefetchScalarGridSpec(
            num_scalar_prefetch=3, grid=(blocks,), in_specs=in_specs, out_specs=part
        ),
        out_shape=jax.ShapeDtypeStruct((rows, features), jnp.bfloat16),
        input_output_aliases=aliases,
        compiler_params=pltpu.CompilerParams(vmem_limit_bytes=24 * MIB),
        cost_estimate=pl.CostEstimate(
            flops=4 * rows * wide * (depth + 1) * block,
            bytes_accessed=8 * MIB,
            transcendentals=rows * wide // HEAD_DIM * (depth + 1) * block,
        ),
        name="attention",
    )(*operands)


def shards(hidden, queries, norm_gain, key_weight, value_weight, anc_ids, anc_cut):
    blocks, depth = anc_ids.shape
    levels = depth + 1
    size = lax.axis_size("node")
    chains = size // levels
    near = depth // 2
    half = [index // chains // 2 for index in range(size)]
    even = [index // chains % 2 == 0 for index in range(size)]
    other = [index + chains if even[index] else index - chains for index in range(size)]
    odd = (lax.axis_index("node") // chains % 2).astype(jnp.int32).reshape(1)
    slots = jnp.where(anc_ids >= 0, anc_ids % blocks, 0)

    def shifted(array, distance, least=0):
        shift = 2 * distance * chains
        pairs = [(i, i + shift) for i in range(size) if i + shift < size and half[i] >= least]
        return lax.ppermute(array, "node", pairs)

    normed, first = norm_project(hidden, norm_gain, key_weight, value_weight)
    own = [first] + [project(normed, key_weight, value_weight, unit) for unit in range(1, UNITS)]
    result = None
    for unit in range(UNITS):
        piece = own[unit]
        straight = []
        for s in range(1, near + 1):
            straight.append(shifted(piece, s) if s <= 2 else shifted(straight[-1], 1, s - 1))
        crossed = [lax.ppermute(piece, "node", [(i, other[i]) for i in range(size) if even[i]])]
        for s in range(1, near + 1):
            pairs = [(i, other[i]) for i in range(size) if half[i] >= s]
            crossed.append(lax.ppermute(straight[s - 1], "node", pairs))
        result = attention(slots, anc_cut, odd, queries, piece, straight, crossed, unit, result)
    return result


def solution(mesh):
    placed = (
        P(("groups", "node"), None),
        P(("groups", "node"), None),
        P(),
        P(),
        P(),
        P(("groups", "node"), None),
        P(("groups", "node"), None),
    )
    return jax.shard_map(
        shards, mesh=mesh, in_specs=placed, out_specs=P(("groups", "node"), None), check_vma=False
    )
```

```python
import functools
import jax
import jax.numpy as jnp
from jax import lax
from jax.experimental import pallas as pl
from jax.experimental.pallas import tpu as pltpu
from jax.sharding import PartitionSpec as P

HEAD_DIM = 128
EPS = 1e-05
LOG2E = 1.4426950408889634
MASKED = -1e30
MIB = 1024 * 1024
CHUNKS = 4
NORM_CHUNKS = 8
UNITS = 2
BLOCKS_PER_STEP = 2


def norm_project_kernel(
    x_hbm, gain_ref, key_hbm, value_hbm, normed_hbm, kv_ref,
    x_scr, key_scr, value_scr, normed_scr, acc_scr, x_sem, key_sem, value_sem, normed_sem,
):
    rows, features = x_scr.shape
    width = key_scr.shape[1]
    chunk = features // NORM_CHUNKS
    lanes = 128

    def columns(c):
        return slice(c * chunk, (c + 1) * chunk)

    def load_x(c):
        return pltpu.make_async_copy(
            x_hbm.at[:, columns(c)], x_scr.at[:, columns(c)], x_sem.at[c]
        )

    def load_weights(c):
        return [
            pltpu.make_async_copy(
                hbm.at[columns(c), pl.ds(0, width)], scr.at[columns(c), :], sem.at[c]
            )
            for hbm, scr, sem in ((key_hbm, key_scr, key_sem), (value_hbm, value_scr, value_sem))
        ]

    def store_normed(c):
        return pltpu.make_async_copy(
            normed_scr.at[:, columns(c)], normed_hbm.at[:, columns(c)], normed_sem.at[c]
        )

    for c in range(NORM_CHUNKS):
        load_x(c).start()
    for c in range(NORM_CHUNKS):
        for copy in load_weights(c):
            copy.start()

    squares = jnp.zeros((rows, lanes), jnp.float32)
    for c in range(NORM_CHUNKS):
        load_x(c).wait()
        for first in range(c * chunk, (c + 1) * chunk, lanes):
            x = x_scr[:, first : first + lanes].astype(jnp.float32)
            squares += x * x
    mean_sq = jnp.sum(squares, axis=-1, keepdims=True) / features
    inverse = jnp.broadcast_to(lax.rsqrt(mean_sq + EPS), (rows, lanes))

    def normalise(c):
        for first in range(c * chunk, (c + 1) * chunk, lanes):
            cols = slice(first, first + lanes)
            x = x_scr[:, cols].astype(jnp.float32)
            normed_scr[:, cols] = (x * inverse * gain_ref[:, cols]).astype(jnp.bfloat16)

    normalise(0)
    for c in range(NORM_CHUNKS):
        for copy in load_weights(c):
            copy.wait()
        store_normed(c).start()
        for part, weight in enumerate((key_scr, value_scr)):
            cols = slice(part * width, (part + 1) * width)
            term = jnp.dot(
                normed_scr[:, columns(c)], weight[columns(c), :], preferred_element_type=jnp.float32
            )
            if c == 0:
                acc_scr[:, cols] = term
            elif c < NORM_CHUNKS - 1:
                acc_scr[:, cols] += term
            else:
                kv_ref[:, cols] = (acc_scr[:, cols] + term).astype(jnp.bfloat16)
        if c < NORM_CHUNKS - 1:
            normalise(c + 1)
    for c in range(NORM_CHUNKS):
        store_normed(c).wait()


def norm_project(hidden, gain, key_weight, value_weight):
    rows, features = hidden.shape
    width = key_weight.shape[1] // UNITS
    whole = pl.BlockSpec(memory_space=pltpu.VMEM)
    remote = pl.BlockSpec(memory_space=pl.ANY)
    return pl.pallas_call(
        norm_project_kernel,
        in_specs=[remote, whole, remote, remote],
        out_specs=[remote, whole],
        out_shape=[
            jax.ShapeDtypeStruct((rows, features), jnp.bfloat16),
            jax.ShapeDtypeStruct((rows, 2 * width), jnp.bfloat16),
        ],
        scratch_shapes=[
            pltpu.VMEM((rows, features), jnp.bfloat16),
            pltpu.VMEM((features, width), jnp.bfloat16),
            pltpu.VMEM((features, width), jnp.bfloat16),
            pltpu.VMEM((rows, features), jnp.bfloat16),
            pltpu.VMEM((rows, 2 * width), jnp.float32),
            pltpu.SemaphoreType.DMA((NORM_CHUNKS,)),
            pltpu.SemaphoreType.DMA((NORM_CHUNKS,)),
            pltpu.SemaphoreType.DMA((NORM_CHUNKS,)),
            pltpu.SemaphoreType.DMA((NORM_CHUNKS,)),
        ],
        compiler_params=pltpu.CompilerParams(vmem_limit_bytes=57 * MIB),
        cost_estimate=pl.CostEstimate(
            flops=4 * rows * features * width, bytes_accessed=24 * MIB, transcendentals=0
        ),
        name="norm_project",
    )(hidden, gain.reshape(1, features), key_weight, value_weight)


def project_kernel(normed_ref, key_ref, value_ref, kv_ref, acc_scr):
    step = pl.program_id(0)
    width = key_ref.shape[1]
    normed = normed_ref[...]
    for part, weight in enumerate((key_ref, value_ref)):
        cols = slice(part * width, (part + 1) * width)
        term = jnp.dot(normed, weight[...], preferred_element_type=jnp.float32)
        acc_scr[:, cols] = jnp.where(step == 0, term, acc_scr[:, cols] + term)

    @pl.when(step == CHUNKS - 1)
    def _():
        kv_ref[...] = acc_scr[...].astype(jnp.bfloat16)


def project(normed, key_weight, value_weight, unit):
    rows, features = normed.shape
    chunk = features // CHUNKS
    width = key_weight.shape[1] // UNITS
    weight = pl.BlockSpec((chunk, width), lambda i: (i, unit))
    return pl.pallas_call(
        project_kernel,
        grid=(CHUNKS,),
        in_specs=[pl.BlockSpec((rows, chunk), lambda i: (0, i)), weight, weight],
        out_specs=pl.BlockSpec((rows, 2 * width), lambda i: (0, 0)),
        out_shape=jax.ShapeDtypeStruct((rows, 2 * width), jnp.bfloat16),
        scratch_shapes=[pltpu.VMEM((rows, 2 * width), jnp.float32)],
        compiler_params=pltpu.CompilerParams(vmem_limit_bytes=57 * MIB),
        cost_estimate=pl.CostEstimate(
            flops=4 * rows * features * width, bytes_accessed=16 * MIB, transcendentals=0
        ),
        name="project",
    )(normed, key_weight, value_weight)


def attention_kernel(block, kv_heads, near, slot_ref, cut_ref, odd_ref, q_ref, own_ref, *refs):
    out_ref = refs[-1]
    straight, crossed = refs[:near], refs[near : 2 * near + 1]
    depth = slot_ref.shape[1]
    odd = odd_ref[0] == 1
    per_group = q_ref.shape[1] // HEAD_DIM // kv_heads
    tile = 256
    together = tile // block
    scale = HEAD_DIM**-0.5 * LOG2E
    token = lax.broadcasted_iota(jnp.int32, (block, HEAD_DIM), 0)
    lane = lax.broadcasted_iota(jnp.int32, (block, HEAD_DIM), 1)
    hidden_later = jnp.where((lane >= block) & (lane - block > token), MASKED, 0.0)
    query_mask = jnp.where(lane == 0, 1.0, hidden_later).astype(jnp.bfloat16)
    query_mask = jnp.concatenate([query_mask] * together, axis=0)
    own_mask = jnp.where(lane - block == token, 1.0, 0.0).astype(jnp.bfloat16)

    def gather(local):
        here = pl.program_id(0) * BLOCKS_PER_STEP + local
        pieces, masks = [], []
        for k in range(depth):
            rows = pl.ds(pl.multiple_of(slot_ref[here, k] * block, block), block)
            if k % 2 == 1:
                pieces.append(straight[k // 2][rows, :])
            else:
                low = crossed[k // 2][rows, :]
                high = crossed[min(k // 2 + 1, near)][rows, :]
                pieces.append(jnp.where(odd, low, high))
            unseen = (lane == 0) & (token >= cut_ref[here, k])
            masks.append(jnp.where(unseen, MASKED, 0.0).astype(jnp.bfloat16))
        pieces.append(own_ref[pl.ds(pl.multiple_of(here * block, block), block), :])
        masks.append(own_mask)
        return jnp.concatenate(pieces, axis=0), jnp.concatenate(masks, axis=0)

    def score(local, head, first, every, mask):
        keys = jnp.concatenate([every[:, head * HEAD_DIM : (head + 1) * HEAD_DIM], mask], axis=1)
        rows = slice(local * block, (local + 1) * block)
        queries = jnp.concatenate(
            [
                q_ref[rows, r * HEAD_DIM : (r + 1) * HEAD_DIM]
                for r in range(first, first + together)
            ],
            axis=0,
        )
        queries = jnp.concatenate([queries, query_mask], axis=1)
        return lax.dot_general(
            keys, queries, (((1,), (1,)), ((), ())), preferred_element_type=jnp.float32
        )

    def finish(local, first, scores, flipped):
        peak = jnp.max(scores, axis=0, keepdims=True)
        weights = jnp.exp2((scores - peak) * scale).astype(jnp.bfloat16)
        both = jnp.dot(flipped, weights, preferred_element_type=jnp.float32)
        context = both[:HEAD_DIM] * (1.0 / both[HEAD_DIM : HEAD_DIM + 1])
        context = context.T.astype(jnp.bfloat16)
        for r in range(together):
            cols = slice((first + r) * HEAD_DIM, (first + r + 1) * HEAD_DIM)
            out_ref[local * block : (local + 1) * block, cols] = context[r * block : (r + 1) * block]

    waiting = None
    for local in range(BLOCKS_PER_STEP):
        every, mask = gather(local)
        for head in range(kv_heads):
            start = (kv_heads + head) * HEAD_DIM
            values = every[:, start : start + HEAD_DIM]
            flipped = jnp.concatenate(
                [values.T, jnp.ones((16, values.shape[0]), jnp.bfloat16)], axis=0
            )
            for first in range(head * per_group, (head + 1) * per_group, together):
                scores = score(local, head, first, every, mask)
                if waiting is not None:
                    finish(*waiting)
                waiting = (local, first, scores, flipped)
    finish(*waiting)


def attention(slots, cuts, odd, queries, own, straight, crossed, unit, previous):
    rows, features = queries.shape
    blocks, depth = slots.shape
    block = rows // blocks
    wide = features // UNITS
    near = len(straight)
    kv_heads = own.shape[1] // (2 * HEAD_DIM)
    whole = pl.BlockSpec(own.shape, lambda b, *_: (0, 0), pipeline_mode=pl.Buffered(1))
    part = pl.BlockSpec((BLOCKS_PER_STEP * block, wide), lambda b, *_: (b, unit))
    operands = [slots, cuts, odd, queries, own, *straight, *crossed]
    in_specs = [part] + [whole] * (1 + near + len(crossed))
    aliases = {}
    if previous is not None:
        aliases = {len(operands): 0}
        operands.append(previous)
        in_specs.append(pl.BlockSpec(memory_space=pl.ANY))
    return pl.pallas_call(
        functools.partial(attention_kernel, block, kv_heads, near),
        grid_spec=pltpu.PrefetchScalarGridSpec(
            num_scalar_prefetch=3, grid=(blocks // BLOCKS_PER_STEP,), in_specs=in_specs, out_specs=part
        ),
        out_shape=jax.ShapeDtypeStruct((rows, features), jnp.bfloat16),
        input_output_aliases=aliases,
        compiler_params=pltpu.CompilerParams(vmem_limit_bytes=24 * MIB),
        cost_estimate=pl.CostEstimate(
            flops=4 * rows * wide * (depth + 1) * block,
            bytes_accessed=8 * MIB,
            transcendentals=rows * wide // HEAD_DIM * (depth + 1) * block,
        ),
        name="attention",
    )(*operands)


def shards(hidden, queries, norm_gain, key_weight, value_weight, anc_ids, anc_cut):
    blocks, depth = anc_ids.shape
    levels = depth + 1
    size = lax.axis_size("node")
    chains = size // levels
    near = depth // 2
    half = [index // chains // 2 for index in range(size)]
    even = [index // chains % 2 == 0 for index in range(size)]
    other = [index + chains if even[index] else index - chains for index in range(size)]
    odd = (lax.axis_index("node") // chains % 2).astype(jnp.int32).reshape(1)
    slots = jnp.where(anc_ids >= 0, anc_ids % blocks, 0)

    def shifted(array, distance, least=0):
        shift = 2 * distance * chains
        pairs = [(i, i + shift) for i in range(size) if i + shift < size and half[i] >= least]
        return lax.ppermute(array, "node", pairs)

    normed, first = norm_project(hidden, norm_gain, key_weight, value_weight)
    own = [first] + [project(normed, key_weight, value_weight, unit) for unit in range(1, UNITS)]
    def after(array, *earlier):
        return lax.optimization_barrier((array, *earlier))[0]

    straight = [[] for _ in range(UNITS)]
    crossed = [[] for _ in range(UNITS)]
    waves = []
    for s in range(near + 1):
        for unit in range(UNITS):
            settled = waves[-2] if len(waves) >= 2 else ()
            source = own[unit] if s == 0 else straight[unit][s - 1]
            pairs = [(i, other[i]) for i in range(size) if (half[i] >= s if s else even[i])]
            crossed[unit].append(lax.ppermute(after(source, *settled), "node", pairs))
            wave = [crossed[unit][-1]]
            if s < near:
                ahead = after(own[unit] if s < 2 else straight[unit][-1], *settled)
                straight[unit].append(
                    shifted(ahead, s + 1) if s < 2 else shifted(ahead, 1, s)
                )
                wave.append(straight[unit][-1])
            waves.append(wave)
    result = None
    for unit in range(UNITS):
        result = attention(
            slots, anc_cut, odd, queries, own[unit], straight[unit], crossed[unit], unit, result
        )
    return result


def solution(mesh):
    placed = (
        P(("groups", "node"), None),
        P(("groups", "node"), None),
        P(),
        P(),
        P(),
        P(("groups", "node"), None),
        P(("groups", "node"), None),
    )
    return jax.shard_map(
        shards, mesh=mesh, in_specs=placed, out_specs=P(("groups", "node"), None), check_vma=False
    )
```

```python
import functools
import jax
import jax.numpy as jnp
from jax import lax
from jax.experimental import pallas as pl
from jax.experimental.pallas import tpu as pltpu
from jax.sharding import PartitionSpec as P

HEAD_DIM = 128
EPS = 1e-05
LOG2E = 1.4426950408889634
MASKED = -1e30
MIB = 1024 * 1024
CHUNKS = 4
NORM_CHUNKS = 8
UNITS = 2
BLOCKS_PER_STEP = 2


def norm_project_kernel(
    x_hbm, gain_ref, key_hbm, value_hbm, normed_hbm, kv_ref,
    x_scr, key_scr, value_scr, normed_scr, acc_scr, x_sem, key_sem, value_sem, normed_sem,
):
    rows, features = x_scr.shape
    width = key_scr.shape[1]
    chunk = features // NORM_CHUNKS
    lanes = 128

    def columns(c):
        return slice(c * chunk, (c + 1) * chunk)

    def load_x(c):
        return pltpu.make_async_copy(
            x_hbm.at[:, columns(c)], x_scr.at[:, columns(c)], x_sem.at[c]
        )

    def load_weights(c):
        return [
            pltpu.make_async_copy(
                hbm.at[columns(c), pl.ds(0, width)], scr.at[columns(c), :], sem.at[c]
            )
            for hbm, scr, sem in ((key_hbm, key_scr, key_sem), (value_hbm, value_scr, value_sem))
        ]

    def store_normed(c):
        return pltpu.make_async_copy(
            normed_scr.at[:, columns(c)], normed_hbm.at[:, columns(c)], normed_sem.at[c]
        )

    def start_weights(c):
        for copy in load_weights(c):
            copy.start()

    for c in range(NORM_CHUNKS):
        load_x(c).start()
    band = 128
    bands = [slice(first, first + band) for first in range(0, rows, band)]
    ahead = NORM_CHUNKS // 2
    squares = [jnp.zeros((band, lanes), jnp.float32) for _ in bands]
    for c in range(NORM_CHUNKS):
        load_x(c).wait()
        if c >= ahead:
            start_weights(c - ahead)
        for index, row in enumerate(bands):
            for first in range(c * chunk, (c + 1) * chunk, lanes):
                x = x_scr[row, first : first + lanes].astype(jnp.float32)
                squares[index] += x * x
    for c in range(NORM_CHUNKS - ahead, NORM_CHUNKS):
        start_weights(c)
    inverse = []
    for total in squares:
        mean_sq = jnp.sum(total, axis=-1, keepdims=True) / features
        inverse.append(jnp.broadcast_to(lax.rsqrt(mean_sq + EPS), (band, lanes)))

    def normalise(c):
        for index, row in enumerate(bands):
            for first in range(c * chunk, (c + 1) * chunk, lanes):
                cols = slice(first, first + lanes)
                x = x_scr[row, cols].astype(jnp.float32)
                normed_scr[row, cols] = (x * inverse[index] * gain_ref[:, cols]).astype(jnp.bfloat16)

    normalise(0)
    for c in range(NORM_CHUNKS):
        for copy in load_weights(c):
            copy.wait()
        store_normed(c).start()
        for part, weight in enumerate((key_scr, value_scr)):
            cols = slice(part * width, (part + 1) * width)
            term = jnp.dot(
                normed_scr[:, columns(c)], weight[columns(c), :], preferred_element_type=jnp.float32
            )
            if c == 0:
                acc_scr[:, cols] = term
            elif c < NORM_CHUNKS - 1:
                acc_scr[:, cols] += term
            else:
                kv_ref[:, cols] = (acc_scr[:, cols] + term).astype(jnp.bfloat16)
        if c < NORM_CHUNKS - 1:
            normalise(c + 1)
    for c in range(NORM_CHUNKS):
        store_normed(c).wait()


def norm_project(hidden, gain, key_weight, value_weight):
    rows, features = hidden.shape
    width = key_weight.shape[1] // UNITS
    whole = pl.BlockSpec(memory_space=pltpu.VMEM)
    remote = pl.BlockSpec(memory_space=pl.ANY)
    return pl.pallas_call(
        norm_project_kernel,
        in_specs=[remote, whole, remote, remote],
        out_specs=[remote, whole],
        out_shape=[
            jax.ShapeDtypeStruct((rows, features), jnp.bfloat16),
            jax.ShapeDtypeStruct((rows, 2 * width), jnp.bfloat16),
        ],
        scratch_shapes=[
            pltpu.VMEM((rows, features), jnp.bfloat16),
            pltpu.VMEM((features, width), jnp.bfloat16),
            pltpu.VMEM((features, width), jnp.bfloat16),
            pltpu.VMEM((rows, features), jnp.bfloat16),
            pltpu.VMEM((rows, 2 * width), jnp.float32),
            pltpu.SemaphoreType.DMA((NORM_CHUNKS,)),
            pltpu.SemaphoreType.DMA((NORM_CHUNKS,)),
            pltpu.SemaphoreType.DMA((NORM_CHUNKS,)),
            pltpu.SemaphoreType.DMA((NORM_CHUNKS,)),
        ],
        compiler_params=pltpu.CompilerParams(vmem_limit_bytes=57 * MIB),
        cost_estimate=pl.CostEstimate(
            flops=4 * rows * features * width, bytes_accessed=24 * MIB, transcendentals=0
        ),
        name="norm_project",
    )(hidden, gain.reshape(1, features), key_weight, value_weight)


def project_kernel(normed_ref, key_ref, value_ref, kv_ref, acc_scr):
    step = pl.program_id(0)
    width = key_ref.shape[1]
    normed = normed_ref[...]
    for part, weight in enumerate((key_ref, value_ref)):
        cols = slice(part * width, (part + 1) * width)
        term = jnp.dot(normed, weight[...], preferred_element_type=jnp.float32)
        acc_scr[:, cols] = jnp.where(step == 0, term, acc_scr[:, cols] + term)

    @pl.when(step == CHUNKS - 1)
    def _():
        kv_ref[...] = acc_scr[...].astype(jnp.bfloat16)


def project(normed, key_weight, value_weight, unit):
    rows, features = normed.shape
    chunk = features // CHUNKS
    width = key_weight.shape[1] // UNITS
    weight = pl.BlockSpec((chunk, width), lambda i: (i, unit))
    return pl.pallas_call(
        project_kernel,
        grid=(CHUNKS,),
        in_specs=[pl.BlockSpec((rows, chunk), lambda i: (0, i)), weight, weight],
        out_specs=pl.BlockSpec((rows, 2 * width), lambda i: (0, 0)),
        out_shape=jax.ShapeDtypeStruct((rows, 2 * width), jnp.bfloat16),
        scratch_shapes=[pltpu.VMEM((rows, 2 * width), jnp.float32)],
        compiler_params=pltpu.CompilerParams(vmem_limit_bytes=57 * MIB),
        cost_estimate=pl.CostEstimate(
            flops=4 * rows * features * width, bytes_accessed=16 * MIB, transcendentals=0
        ),
        name="project",
    )(normed, key_weight, value_weight)


def attention_kernel(block, near, slot_ref, cut_ref, odd_ref, q_ref, *refs):
    own_hbm, straight, crossed = refs[0], refs[1 : near + 1], refs[near + 1 : 2 * near + 2]
    out_ref, kv_scr, sems = refs[-3:]
    depth = slot_ref.shape[1]
    kv_heads = kv_scr.shape[2] // (2 * HEAD_DIM)

    @pl.when(pl.program_id(0) == 0)
    def _():
        copies = [pltpu.make_async_copy(own_hbm, kv_scr.at[depth], sems.at[0])]
        for s, ref in enumerate(straight):
            copies.append(pltpu.make_async_copy(ref, kv_scr.at[2 * s + 1], sems.at[s + 1]))
        for s, ref in enumerate(crossed):
            level = 2 * lax.rem(s + odd_ref[0] + near, near + 1)
            copies.append(pltpu.make_async_copy(ref, kv_scr.at[level], sems.at[near + s + 1]))
        for copy in copies:
            copy.start()
        for copy in copies:
            copy.wait()

    per_group = q_ref.shape[1] // HEAD_DIM // kv_heads
    tile = 256
    together = tile // block
    scale = HEAD_DIM**-0.5 * LOG2E
    token = lax.broadcasted_iota(jnp.int32, (block, HEAD_DIM), 0)
    lane = lax.broadcasted_iota(jnp.int32, (block, HEAD_DIM), 1)
    hidden_later = jnp.where((lane >= block) & (lane - block > token), MASKED, 0.0)
    query_mask = jnp.where(lane == 0, 1.0, hidden_later).astype(jnp.bfloat16)
    query_mask = jnp.concatenate([query_mask] * together, axis=0)
    own_mask = jnp.where(lane - block == token, 1.0, 0.0).astype(jnp.bfloat16)

    def gather(local):
        here = pl.program_id(0) * BLOCKS_PER_STEP + local
        pieces, masks = [], []
        for k in range(depth):
            rows = pl.ds(pl.multiple_of(slot_ref[here, k] * block, block), block)
            pieces.append(kv_scr[k, rows, :])
            unseen = (lane == 0) & (token >= cut_ref[here, k])
            masks.append(jnp.where(unseen, MASKED, 0.0).astype(jnp.bfloat16))
        pieces.append(kv_scr[depth, pl.ds(pl.multiple_of(here * block, block), block), :])
        masks.append(own_mask)
        return jnp.concatenate(pieces, axis=0), jnp.concatenate(masks, axis=0)

    def score(local, head, first, every, mask):
        keys = jnp.concatenate([every[:, head * HEAD_DIM : (head + 1) * HEAD_DIM], mask], axis=1)
        rows = slice(local * block, (local + 1) * block)
        queries = jnp.concatenate(
            [
                q_ref[rows, r * HEAD_DIM : (r + 1) * HEAD_DIM]
                for r in range(first, first + together)
            ],
            axis=0,
        )
        queries = jnp.concatenate([queries, query_mask], axis=1)
        return lax.dot_general(
            keys, queries, (((1,), (1,)), ((), ())), preferred_element_type=jnp.float32
        )

    def finish(local, first, scores, flipped):
        peak = jnp.max(scores, axis=0, keepdims=True)
        weights = jnp.exp2((scores - peak) * scale).astype(jnp.bfloat16)
        both = jnp.dot(flipped, weights, preferred_element_type=jnp.float32)
        context = both[:HEAD_DIM] * (1.0 / both[HEAD_DIM : HEAD_DIM + 1])
        context = context.T.astype(jnp.bfloat16)
        for r in range(together):
            cols = slice((first + r) * HEAD_DIM, (first + r + 1) * HEAD_DIM)
            out_ref[local * block : (local + 1) * block, cols] = context[r * block : (r + 1) * block]

    waiting = None
    for local in range(BLOCKS_PER_STEP):
        every, mask = gather(local)
        for head in range(kv_heads):
            start = (kv_heads + head) * HEAD_DIM
            values = every[:, start : start + HEAD_DIM]
            flipped = jnp.concatenate(
                [values.T, jnp.ones((16, values.shape[0]), jnp.bfloat16)], axis=0
            )
            for first in range(head * per_group, (head + 1) * per_group, together):
                scores = score(local, head, first, every, mask)
                if waiting is not None:
                    finish(*waiting)
                waiting = (local, first, scores, flipped)
    finish(*waiting)


def attention(slots, cuts, odd, queries, own, straight, crossed, unit, previous):
    rows, features = queries.shape
    blocks, depth = slots.shape
    block = rows // blocks
    wide = features // UNITS
    near = len(straight)
    held = pl.BlockSpec(memory_space=pltpu.HBM)
    part = pl.BlockSpec((BLOCKS_PER_STEP * block, wide), lambda b, *_: (b, unit))
    operands = [slots, cuts, odd, queries, own, *straight, *crossed]
    in_specs = [part] + [held] * (1 + near + len(crossed))
    aliases = {}
    if previous is not None:
        aliases = {len(operands): 0}
        operands.append(previous)
        in_specs.append(held)
    return pl.pallas_call(
        functools.partial(attention_kernel, block, near),
        grid_spec=pltpu.PrefetchScalarGridSpec(
            num_scalar_prefetch=3,
            grid=(blocks // BLOCKS_PER_STEP,),
            in_specs=in_specs,
            out_specs=part,
            scratch_shapes=[
                pltpu.VMEM((depth + 1, *own.shape), own.dtype),
                pltpu.SemaphoreType.DMA((depth + 1,)),
            ],
        ),
        out_shape=jax.ShapeDtypeStruct((rows, features), jnp.bfloat16),
        input_output_aliases=aliases,
        compiler_params=pltpu.CompilerParams(vmem_limit_bytes=57 * MIB),
        cost_estimate=pl.CostEstimate(
            flops=4 * rows * wide * (depth + 1) * block,
            bytes_accessed=8 * MIB,
            transcendentals=rows * wide // HEAD_DIM * (depth + 1) * block,
        ),
        name="attention",
    )(*operands)


def shards(hidden, queries, norm_gain, key_weight, value_weight, anc_ids, anc_cut):
    blocks, depth = anc_ids.shape
    levels = depth + 1
    size = lax.axis_size("node")
    chains = size // levels
    near = depth // 2
    half = [index // chains // 2 for index in range(size)]
    even = [index // chains % 2 == 0 for index in range(size)]
    other = [index + chains if even[index] else index - chains for index in range(size)]
    odd = (lax.axis_index("node") // chains % 2).astype(jnp.int32).reshape(1)
    slots = jnp.where(anc_ids >= 0, anc_ids % blocks, 0)

    normed, first = norm_project(hidden, norm_gain, key_weight, value_weight)
    own = [first] + [project(normed, key_weight, value_weight, unit) for unit in range(1, UNITS)]
    def after(array, *earlier):
        return lax.optimization_barrier((array, *earlier))[0]

    straight = [{} for _ in range(UNITS)]
    crossed = [{} for _ in range(UNITS)]

    def step_across(s, unit, settled):
        source = own[unit] if s == 0 else straight[unit][s]
        both_ways = unit == UNITS - 1 and s == 0
        pairs = [
            (i, other[i])
            for i in range(size)
            if half[i] >= s and (s > 0 or even[i] or (both_ways and half[i] == 0))
        ]
        crossed[unit][s] = lax.ppermute(after(source, *settled), "node", pairs)
        return crossed[unit][s]

    def step_along(s, unit, settled):
        source = own[unit] if s == 1 else straight[unit][s - 1]
        shift = 2 * chains
        pairs = [(i, i + shift) for i in range(size - shift) if half[i] >= s - 1]
        straight[unit][s] = lax.ppermute(after(source, *settled), "node", pairs)
        return straight[unit][s]

    def step_down(unit, settled):
        shift = 2 * near * chains
        pairs = [(i, i + shift) for i in range(size - shift)]
        crossed[unit][near] = lax.ppermute(after(crossed[unit][0], *settled), "node", pairs)
        return crossed[unit][near]

    early, late = range(UNITS)
    across = [(s, unit) for s in range(near - 1) for unit in (early, late)]
    across += [(near - 1, early), (near, early), (near - 1, late)]
    along = [(s, unit) for s in range(1, near + 1) for unit in (early, late)]
    waves = []
    for index, (s, unit) in enumerate(across):
        settled = waves[-2] if len(waves) >= 2 else ()
        wave = [step_across(s, unit, settled)]
        if index < len(along):
            wave.append(step_along(*along[index], settled))
        else:
            wave.append(step_down(late, settled))
        waves.append(wave)
    result = None
    for unit in range(UNITS):
        result = attention(
            slots,
            anc_cut,
            odd,
            queries,
            own[unit],
            [straight[unit][s] for s in range(1, near + 1)],
            [crossed[unit][s] for s in range(near + 1)],
            unit,
            result,
        )
    return result


def solution(mesh):
    placed = (
        P(("groups", "node"), None),
        P(("groups", "node"), None),
        P(),
        P(),
        P(),
        P(("groups", "node"), None),
        P(("groups", "node"), None),
    )
    return jax.shard_map(
        shards, mesh=mesh, in_specs=placed, out_specs=P(("groups", "node"), None), check_vma=False
    )
```

```python
import functools
import jax
import jax.numpy as jnp
from jax import lax
from jax.experimental import pallas as pl
from jax.experimental.pallas import tpu as pltpu
from jax.sharding import PartitionSpec as P

HEAD_DIM = 128
EPS = 1e-05
LOG2E = 1.4426950408889634
MASKED = -1e30
MIB = 1024 * 1024
CHUNKS = 4
LOADS = 8
BLOCKS_PER_STEP = 4


def norm_project_kernel(
    x_hbm, gain_ref, key_hbm, value_hbm, normed_hbm, kv_ref,
    x_scr, weight_scr, normed_scr, x_sem, key_sem, value_sem, normed_sem,
):
    rows, features = x_scr.shape
    piece = features // LOADS
    chunk = features // CHUNKS
    lanes = 128

    def load_x(c):
        cols = slice(c * piece, (c + 1) * piece)
        return pltpu.make_async_copy(x_hbm.at[:, cols], x_scr.at[:, cols], x_sem.at[c])

    def load_weights(c):
        span = slice(c * chunk, (c + 1) * chunk)
        head = pl.ds(0, HEAD_DIM)
        return [
            pltpu.make_async_copy(
                key_hbm.at[span, head], weight_scr.at[span, :HEAD_DIM], key_sem.at[c]
            ),
            pltpu.make_async_copy(
                value_hbm.at[span, head], weight_scr.at[span, HEAD_DIM:], value_sem.at[c]
            ),
        ]

    def store_normed(c):
        cols = slice(c * chunk, (c + 1) * chunk)
        return pltpu.make_async_copy(
            normed_scr.at[:, cols], normed_hbm.at[:, cols], normed_sem.at[c]
        )

    for c in range(LOADS):
        load_x(c).start()
    band = 128
    bands = [slice(first, first + band) for first in range(0, rows, band)]
    squares = [jnp.zeros((band, lanes), jnp.float32) for _ in bands]
    for c in range(LOADS):
        load_x(c).wait()
        if c >= LOADS - CHUNKS:
            for copy in load_weights(c - LOADS + CHUNKS):
                copy.start()
        for index, row in enumerate(bands):
            for first in range(c * piece, (c + 1) * piece, lanes):
                x = x_scr[row, first : first + lanes].astype(jnp.float32)
                squares[index] += x * x
    inverse = []
    for total in squares:
        mean_sq = jnp.sum(total, axis=-1, keepdims=True) / features
        inverse.append(jnp.broadcast_to(lax.rsqrt(mean_sq + EPS), (band, lanes)))

    def normalise(c):
        for index, row in enumerate(bands):
            for first in range(c * chunk, (c + 1) * chunk, lanes):
                cols = slice(first, first + lanes)
                x = x_scr[row, cols].astype(jnp.float32)
                normed_scr[row, cols] = (x * inverse[index] * gain_ref[:, cols]).astype(jnp.bfloat16)

    normalise(0)
    total = None
    for c in range(CHUNKS):
        for copy in load_weights(c):
            copy.wait()
        store_normed(c).start()
        span = slice(c * chunk, (c + 1) * chunk)
        term = jnp.dot(
            normed_scr[:, span], weight_scr[span, :], preferred_element_type=jnp.float32
        )
        total = term if total is None else total + term
        if c < CHUNKS - 1:
            normalise(c + 1)
    kv_ref[...] = total.astype(jnp.bfloat16)
    for c in range(CHUNKS):
        store_normed(c).wait()


def norm_project(hidden, gain, key_weight, value_weight):
    rows, features = hidden.shape
    whole = pl.BlockSpec(memory_space=pltpu.VMEM)
    held = pl.BlockSpec(memory_space=pltpu.HBM)
    return pl.pallas_call(
        norm_project_kernel,
        in_specs=[held, whole, held, held],
        out_specs=[held, whole],
        out_shape=[
            jax.ShapeDtypeStruct((rows, features), jnp.bfloat16),
            jax.ShapeDtypeStruct((rows, 2 * HEAD_DIM), jnp.bfloat16),
        ],
        scratch_shapes=[
            pltpu.VMEM((rows, features), jnp.bfloat16),
            pltpu.VMEM((features, 2 * HEAD_DIM), jnp.bfloat16),
            pltpu.VMEM((rows, features), jnp.bfloat16),
            pltpu.SemaphoreType.DMA((LOADS,)),
            pltpu.SemaphoreType.DMA((CHUNKS,)),
            pltpu.SemaphoreType.DMA((CHUNKS,)),
            pltpu.SemaphoreType.DMA((CHUNKS,)),
        ],
        compiler_params=pltpu.CompilerParams(vmem_limit_bytes=57 * MIB),
        cost_estimate=pl.CostEstimate(
            flops=4 * rows * features * HEAD_DIM, bytes_accessed=24 * MIB, transcendentals=0
        ),
        name="norm_project",
    )(hidden, gain.reshape(1, features), key_weight, value_weight)


def project_kernel(normed_ref, key_ref, value_ref, *refs):
    acc_scr = refs[-1]
    step = pl.program_id(0)
    normed = normed_ref[...]
    for index in range(len(refs) - 1):
        head = slice(index * HEAD_DIM, (index + 1) * HEAD_DIM)
        weight = jnp.concatenate([key_ref[:, head], value_ref[:, head]], axis=1)
        term = jnp.dot(normed, weight, preferred_element_type=jnp.float32)
        acc_scr[index] = jnp.where(step == 0, term, acc_scr[index] + term)

    @pl.when(step == CHUNKS - 1)
    def _():
        for index in range(len(refs) - 1):
            refs[index][...] = acc_scr[index].astype(jnp.bfloat16)


def project(normed, key_weight, value_weight, first, heads):
    rows, features = normed.shape
    chunk = features // CHUNKS
    weight = pl.BlockSpec((chunk, heads * HEAD_DIM), lambda i: (i, first // heads))
    return pl.pallas_call(
        project_kernel,
        grid=(CHUNKS,),
        in_specs=[pl.BlockSpec((rows, chunk), lambda i: (0, i)), weight, weight],
        out_specs=[pl.BlockSpec((rows, 2 * HEAD_DIM), lambda i: (0, 0)) for _ in range(heads)],
        out_shape=[
            jax.ShapeDtypeStruct((rows, 2 * HEAD_DIM), jnp.bfloat16) for _ in range(heads)
        ],
        scratch_shapes=[pltpu.VMEM((heads, rows, 2 * HEAD_DIM), jnp.float32)],
        compiler_params=pltpu.CompilerParams(vmem_limit_bytes=57 * MIB),
        cost_estimate=pl.CostEstimate(
            flops=4 * heads * rows * features * HEAD_DIM,
            bytes_accessed=(8 + 4 * heads) * MIB,
            transcendentals=0,
        ),
        name="project",
    )(normed, key_weight, value_weight)


def attention_kernel(block, near, slot_ref, cut_ref, odd_ref, q_ref, *refs):
    own_hbm, straight, crossed = refs[0], refs[1 : near + 1], refs[near + 1 : 2 * near + 2]
    out_ref, kv_scr, sems = refs[-3:]
    depth = slot_ref.shape[1]
    kv_heads = kv_scr.shape[2] // (2 * HEAD_DIM)

    @pl.when(pl.program_id(0) == 0)
    def _():
        copies = [pltpu.make_async_copy(own_hbm, kv_scr.at[depth], sems.at[0])]
        for s, ref in enumerate(straight):
            copies.append(pltpu.make_async_copy(ref, kv_scr.at[2 * s + 1], sems.at[s + 1]))
        for s, ref in enumerate(crossed):
            level = 2 * lax.rem(s + odd_ref[0] + near, near + 1)
            copies.append(pltpu.make_async_copy(ref, kv_scr.at[level], sems.at[near + s + 1]))
        for copy in copies:
            copy.start()
        for copy in copies:
            copy.wait()

    per_group = q_ref.shape[1] // HEAD_DIM // kv_heads
    tile = 256
    together = tile // block
    scale = HEAD_DIM**-0.5 * LOG2E
    token = lax.broadcasted_iota(jnp.int32, (block, HEAD_DIM), 0)
    lane = lax.broadcasted_iota(jnp.int32, (block, HEAD_DIM), 1)
    hidden_later = jnp.where((lane >= block) & (lane - block > token), MASKED, 0.0)
    query_mask = jnp.where(lane == 0, 1.0, hidden_later).astype(jnp.bfloat16)
    query_mask = jnp.concatenate([query_mask] * together, axis=0)
    own_mask = jnp.where(lane - block == token, 1.0, 0.0).astype(jnp.bfloat16)

    def gather(local):
        here = pl.program_id(0) * BLOCKS_PER_STEP + local
        pieces, masks = [], []
        for k in range(depth):
            rows = pl.ds(pl.multiple_of(slot_ref[here, k] * block, block), block)
            pieces.append(kv_scr[k, rows, :])
            unseen = (lane == 0) & (token >= cut_ref[here, k])
            masks.append(jnp.where(unseen, MASKED, 0.0).astype(jnp.bfloat16))
        pieces.append(kv_scr[depth, pl.ds(pl.multiple_of(here * block, block), block), :])
        masks.append(own_mask)
        return jnp.concatenate(pieces, axis=0), jnp.concatenate(masks, axis=0)

    def score(local, head, first, every, mask):
        keys = jnp.concatenate([every[:, head * HEAD_DIM : (head + 1) * HEAD_DIM], mask], axis=1)
        rows = slice(local * block, (local + 1) * block)
        queries = jnp.concatenate(
            [
                q_ref[rows, r * HEAD_DIM : (r + 1) * HEAD_DIM]
                for r in range(first, first + together)
            ],
            axis=0,
        )
        queries = jnp.concatenate([queries, query_mask], axis=1)
        return lax.dot_general(
            keys, queries, (((1,), (1,)), ((), ())), preferred_element_type=jnp.float32
        )

    def finish(local, first, scores, flipped):
        peak = jnp.max(scores, axis=0, keepdims=True)
        weights = jnp.exp2((scores - peak) * scale).astype(jnp.bfloat16)
        both = jnp.dot(flipped, weights, preferred_element_type=jnp.float32)
        context = both[:HEAD_DIM] * (1.0 / both[HEAD_DIM : HEAD_DIM + 1])
        context = context.T.astype(jnp.bfloat16)
        for r in range(together):
            cols = slice((first + r) * HEAD_DIM, (first + r + 1) * HEAD_DIM)
            out_ref[local * block : (local + 1) * block, cols] = context[r * block : (r + 1) * block]

    waiting = None
    for local in range(BLOCKS_PER_STEP):
        every, mask = gather(local)
        for head in range(kv_heads):
            start = (kv_heads + head) * HEAD_DIM
            values = every[:, start : start + HEAD_DIM]
            flipped = jnp.concatenate(
                [values.T, jnp.ones((16, values.shape[0]), jnp.bfloat16)], axis=0
            )
            for first in range(head * per_group, (head + 1) * per_group, together):
                scores = score(local, head, first, every, mask)
                if waiting is not None:
                    finish(*waiting)
                waiting = (local, first, scores, flipped)
    finish(*waiting)


def attention(slots, cuts, odd, queries, own, straight, crossed, unit, units, previous):
    rows, features = queries.shape
    blocks, depth = slots.shape
    block = rows // blocks
    wide = features // units
    near = len(straight)
    held = pl.BlockSpec(memory_space=pltpu.HBM)
    part = pl.BlockSpec((BLOCKS_PER_STEP * block, wide), lambda b, *_: (b, unit))
    operands = [slots, cuts, odd, queries, own, *straight, *crossed]
    in_specs = [part] + [held] * (1 + near + len(crossed))
    aliases = {}
    if previous is not None:
        aliases = {len(operands): 0}
        operands.append(previous)
        in_specs.append(held)
    return pl.pallas_call(
        functools.partial(attention_kernel, block, near),
        grid_spec=pltpu.PrefetchScalarGridSpec(
            num_scalar_prefetch=3,
            grid=(blocks // BLOCKS_PER_STEP,),
            in_specs=in_specs,
            out_specs=part,
            scratch_shapes=[
                pltpu.VMEM((depth + 1, *own.shape), own.dtype),
                pltpu.SemaphoreType.DMA((depth + 1,)),
            ],
        ),
        out_shape=jax.ShapeDtypeStruct((rows, features), jnp.bfloat16),
        input_output_aliases=aliases,
        compiler_params=pltpu.CompilerParams(vmem_limit_bytes=57 * MIB),
        cost_estimate=pl.CostEstimate(
            flops=4 * rows * wide * (depth + 1) * block,
            bytes_accessed=8 * MIB,
            transcendentals=rows * wide // HEAD_DIM * (depth + 1) * block,
        ),
        name="attention",
    )(*operands)


def shards(hidden, queries, norm_gain, key_weight, value_weight, anc_ids, anc_cut):
    blocks, depth = anc_ids.shape
    levels = depth + 1
    size = lax.axis_size("node")
    chains = size // levels
    near = depth // 2
    heads = key_weight.shape[1] // HEAD_DIM
    half = [index // chains // 2 for index in range(size)]
    even = [index // chains % 2 == 0 for index in range(size)]
    other = [index + chains if even[index] else index - chains for index in range(size)]
    odd = (lax.axis_index("node") // chains % 2).astype(jnp.int32).reshape(1)
    slots = jnp.where(anc_ids >= 0, anc_ids % blocks, 0)

    normed, first = norm_project(hidden, norm_gain, key_weight, value_weight)
    own = [first]
    own += project(normed, key_weight, value_weight, 1, 1)
    own += project(normed, key_weight, value_weight, 2, heads - 2)
    straight = [{} for _ in range(heads)]
    crossed = [{} for _ in range(heads)]
    early, late = range(heads // 2), range(heads // 2, heads)

    def after(array, settled):
        return lax.optimization_barrier((array, *settled))[0]

    def step_across(s, head, settled):
        source = own[head] if s == 0 else straight[head][s]
        pairs = [
            (i, other[i])
            for i in range(size)
            if half[i] >= s and (s > 0 or even[i] or (head in late and half[i] == 0))
        ]
        crossed[head][s] = lax.ppermute(after(source, settled), "node", pairs)
        return crossed[head][s]

    def step_along(s, head, settled):
        source = own[head] if s == 1 else straight[head][s - 1]
        shift = 2 * chains
        pairs = [(i, i + shift) for i in range(size - shift) if half[i] >= s - 1]
        straight[head][s] = lax.ppermute(after(source, settled), "node", pairs)
        return straight[head][s]

    def step_down(head, settled):
        shift = 2 * near * chains
        pairs = [(i, i + shift) for i in range(size - shift)]
        crossed[head][near] = lax.ppermute(after(crossed[head][0], settled), "node", pairs)
        return crossed[head][near]

    across = [functools.partial(step_across, s, h) for s in range(near + 1) for h in early]
    across += [functools.partial(step_across, s, h) for s in range(near) for h in late]
    along = [functools.partial(step_along, s, h) for s in range(1, near + 1) for h in early]
    along += [functools.partial(step_along, s, h) for s in range(1, near + 1) for h in late]
    along += [functools.partial(step_down, h) for h in late]
    waves = []
    result = None

    def attend(head):
        return attention(
            slots,
            anc_cut,
            odd,
            queries,
            own[head],
            [straight[head][s] for s in range(1, near + 1)],
            [crossed[head][s] for s in range(near + 1)],
            head,
            heads,
            result,
        )

    free = len(early) * (near + 1)
    for index, (one, two) in enumerate(zip(across, along, strict=True)):
        lag = 2 if index < free // 2 else 3
        settled = list(waves[-lag]) if len(waves) >= lag else []
        head = (index - free - 2) // 2
        if index >= free + 2 and index % 2 == free % 2 and head in early:
            result = attend(head)
            settled.append(result)
        waves.append([one(settled), two(settled)])
    for head in late:
        result = attend(head)
    return result


def solution(mesh):
    placed = (
        P(("groups", "node"), None),
        P(("groups", "node"), None),
        P(),
        P(),
        P(),
        P(("groups", "node"), None),
        P(("groups", "node"), None),
    )
    return jax.shard_map(
        shards, mesh=mesh, in_specs=placed, out_specs=P(("groups", "node"), None), check_vma=False
    )
```

```python
import functools
import jax
import jax.numpy as jnp
from jax import lax
from jax.experimental import pallas as pl
from jax.experimental.pallas import tpu as pltpu
from jax.sharding import PartitionSpec as P

HEAD_DIM = 128
EPS = 1e-05
LOG2E = 1.4426950408889634
MASKED = -1e30
MIB = 1024 * 1024
CHUNKS = 4
LOADS = 8
UNITS = 2
BLOCKS_PER_STEP = 2


def norm_project_kernel(
    x_hbm, gain_ref, key_hbm, value_hbm, normed_hbm, kv_ref,
    x_scr, weight_scr, normed_scr, acc_scr, scale_scr, x_sem, key_sem, value_sem, normed_sem,
):
    loads, rows, chunk = x_scr.shape
    width = weight_scr.shape[2] // 2
    lanes = 128
    band = 128

    def span(c):
        return pl.ds(pl.multiple_of(c * chunk, chunk), chunk)

    def load_x(c):
        return pltpu.make_async_copy(x_hbm.at[:, span(c)], x_scr.at[c], x_sem.at[c])

    def load_weights(c):
        head = pl.ds(0, width)
        return [
            pltpu.make_async_copy(
                key_hbm.at[span(c), head], weight_scr.at[c, :, pl.ds(0, width)], key_sem.at[c]
            ),
            pltpu.make_async_copy(
                value_hbm.at[span(c), head], weight_scr.at[c, :, pl.ds(width, width)], value_sem.at[c]
            ),
        ]

    def store_normed(c):
        return pltpu.make_async_copy(normed_scr.at[c], normed_hbm.at[:, span(c)], normed_sem.at[c])

    for c in range(loads):
        load_x(c).start()
    scale_scr[...] = jnp.zeros_like(scale_scr)

    def square(c, carry):
        load_x(c).wait()

        @pl.when(c >= loads // 2)
        def _():
            for part in range(2):
                for copy in load_weights(2 * (c - loads // 2) + part):
                    copy.start()

        for first in range(0, rows, band):
            row = slice(first, first + band)
            total = scale_scr[row, :]
            for lane in range(0, chunk, lanes):
                x = x_scr[c, row, lane : lane + lanes].astype(jnp.float32)
                total += x * x
            scale_scr[row, :] = total
        return carry

    lax.fori_loop(0, loads, square, 0)
    mean_sq = jnp.sum(scale_scr[...], axis=-1, keepdims=True) / (loads * chunk)
    scale_scr[...] = jnp.broadcast_to(lax.rsqrt(mean_sq + EPS), scale_scr.shape)

    def normalise(c):
        for first in range(0, rows, band):
            row = slice(first, first + band)
            inverse = scale_scr[row, :]
            for lane in range(0, chunk, lanes):
                cols = slice(lane, lane + lanes)
                x = x_scr[c, row, cols].astype(jnp.float32)
                gain = gain_ref[c, :, cols]
                normed_scr[c, row, cols] = (x * inverse * gain).astype(jnp.bfloat16)

    normalise(0)
    acc_scr[...] = jnp.zeros_like(acc_scr)

    def multiply(c, carry):
        for copy in load_weights(c):
            copy.wait()
        store_normed(c).start()
        acc_scr[...] += jnp.dot(normed_scr[c], weight_scr[c], preferred_element_type=jnp.float32)

        @pl.when(c < loads - 1)
        def _():
            normalise(c + 1)

        return carry

    lax.fori_loop(0, loads, multiply, 0)
    kv_ref[...] = acc_scr[...].astype(jnp.bfloat16)
    for c in range(loads):
        store_normed(c).wait()


def norm_project(hidden, gain, key_weight, value_weight):
    rows, features = hidden.shape
    width = key_weight.shape[1] // UNITS
    chunk = features // LOADS
    whole = pl.BlockSpec(memory_space=pltpu.VMEM)
    held = pl.BlockSpec(memory_space=pltpu.HBM)
    return pl.pallas_call(
        norm_project_kernel,
        in_specs=[held, whole, held, held],
        out_specs=[held, whole],
        out_shape=[
            jax.ShapeDtypeStruct((rows, features), jnp.bfloat16),
            jax.ShapeDtypeStruct((rows, 2 * width), jnp.bfloat16),
        ],
        scratch_shapes=[
            pltpu.VMEM((LOADS, rows, chunk), jnp.bfloat16),
            pltpu.VMEM((LOADS, chunk, 2 * width), jnp.bfloat16),
            pltpu.VMEM((LOADS, rows, chunk), jnp.bfloat16),
            pltpu.VMEM((rows, 2 * width), jnp.float32),
            pltpu.VMEM((rows, 128), jnp.float32),
            pltpu.SemaphoreType.DMA((LOADS,)),
            pltpu.SemaphoreType.DMA((LOADS,)),
            pltpu.SemaphoreType.DMA((LOADS,)),
            pltpu.SemaphoreType.DMA((LOADS,)),
        ],
        compiler_params=pltpu.CompilerParams(vmem_limit_bytes=57 * MIB),
        cost_estimate=pl.CostEstimate(
            flops=4 * rows * features * width, bytes_accessed=24 * MIB, transcendentals=0
        ),
        name="norm_project",
    )(hidden, gain.reshape(LOADS, 1, chunk), key_weight, value_weight)


def project_kernel(normed_ref, key_ref, value_ref, kv_ref, acc_scr):
    step = pl.program_id(0)
    width = key_ref.shape[1]
    normed = normed_ref[...]
    for part, weight in enumerate((key_ref, value_ref)):
        cols = slice(part * width, (part + 1) * width)
        term = jnp.dot(normed, weight[...], preferred_element_type=jnp.float32)
        acc_scr[:, cols] = jnp.where(step == 0, term, acc_scr[:, cols] + term)

    @pl.when(step == CHUNKS - 1)
    def _():
        kv_ref[...] = acc_scr[...].astype(jnp.bfloat16)


def project(normed, key_weight, value_weight, unit):
    rows, features = normed.shape
    chunk = features // CHUNKS
    width = key_weight.shape[1] // UNITS
    weight = pl.BlockSpec((chunk, width), lambda i: (i, unit))
    return pl.pallas_call(
        project_kernel,
        grid=(CHUNKS,),
        in_specs=[pl.BlockSpec((rows, chunk), lambda i: (0, i)), weight, weight],
        out_specs=pl.BlockSpec((rows, 2 * width), lambda i: (0, 0)),
        out_shape=jax.ShapeDtypeStruct((rows, 2 * width), jnp.bfloat16),
        scratch_shapes=[pltpu.VMEM((rows, 2 * width), jnp.float32)],
        compiler_params=pltpu.CompilerParams(vmem_limit_bytes=57 * MIB),
        cost_estimate=pl.CostEstimate(
            flops=4 * rows * features * width, bytes_accessed=16 * MIB, transcendentals=0
        ),
        name="project",
    )(normed, key_weight, value_weight)


def attention_kernel(block, near, slot_ref, cut_ref, odd_ref, q_ref, *refs):
    own_hbm, straight, crossed = refs[0], refs[1 : near + 1], refs[near + 1 : 2 * near + 2]
    out_ref, kv_scr, sems = refs[-3:]
    depth = slot_ref.shape[1]
    kv_heads = kv_scr.shape[2] // (2 * HEAD_DIM)

    @pl.when(pl.program_id(0) == 0)
    def _():
        copies = [pltpu.make_async_copy(own_hbm, kv_scr.at[depth], sems.at[0])]
        for s, ref in enumerate(straight):
            copies.append(pltpu.make_async_copy(ref, kv_scr.at[2 * s + 1], sems.at[s + 1]))
        for s, ref in enumerate(crossed):
            level = 2 * lax.rem(s + odd_ref[0] + near, near + 1)
            copies.append(pltpu.make_async_copy(ref, kv_scr.at[level], sems.at[near + s + 1]))
        for copy in copies:
            copy.start()
        for copy in copies:
            copy.wait()

    per_group = q_ref.shape[1] // HEAD_DIM // kv_heads
    scale = HEAD_DIM**-0.5 * LOG2E
    token = lax.broadcasted_iota(jnp.int32, (block, HEAD_DIM), 0)
    lane = lax.broadcasted_iota(jnp.int32, (block, HEAD_DIM), 1)
    hidden_later = jnp.where((lane >= block) & (lane - block > token), MASKED, 0.0)
    query_mask = jnp.where(lane == 0, 1.0, hidden_later).astype(jnp.bfloat16)
    query_mask = jnp.concatenate([query_mask] * per_group, axis=0)
    own_mask = jnp.where(lane - block == token, 1.0, 0.0).astype(jnp.bfloat16)

    def gather(local):
        here = pl.program_id(0) * BLOCKS_PER_STEP + local
        pieces, masks = [], []
        for k in range(depth):
            rows = pl.ds(pl.multiple_of(slot_ref[here, k] * block, block), block)
            pieces.append(kv_scr[k, rows, :])
            unseen = (lane == 0) & (token >= cut_ref[here, k])
            masks.append(jnp.where(unseen, MASKED, 0.0).astype(jnp.bfloat16))
        pieces.append(kv_scr[depth, pl.ds(pl.multiple_of(here * block, block), block), :])
        masks.append(own_mask)
        return jnp.concatenate(pieces, axis=0), jnp.concatenate(masks, axis=0)

    def score(local, head, every, mask):
        keys = jnp.concatenate([every[:, head * HEAD_DIM : (head + 1) * HEAD_DIM], mask], axis=1)
        rows = slice(local * block, (local + 1) * block)
        first = head * per_group
        queries = jnp.concatenate(
            [
                q_ref[rows, r * HEAD_DIM : (r + 1) * HEAD_DIM]
                for r in range(first, first + per_group)
            ],
            axis=0,
        )
        queries = jnp.concatenate([queries, query_mask], axis=1)
        return lax.dot_general(
            queries, keys, (((1,), (1,)), ((), ())), preferred_element_type=jnp.float32
        )

    def finish(local, head, scores, values):
        peak = jnp.max(scores, axis=-1, keepdims=True)
        weights = jnp.exp2((scores - peak) * scale).astype(jnp.bfloat16)
        padded = jnp.concatenate([values, jnp.ones_like(values)], axis=1)
        both = jnp.dot(weights, padded, preferred_element_type=jnp.float32)
        context = (both[:, :HEAD_DIM] * (1.0 / both[:, HEAD_DIM:])).astype(jnp.bfloat16)
        for r in range(per_group):
            first = (head * per_group + r) * HEAD_DIM
            out_ref[local * block : (local + 1) * block, first : first + HEAD_DIM] = context[
                r * block : (r + 1) * block
            ]

    waiting = None
    for local in range(BLOCKS_PER_STEP):
        every, mask = gather(local)
        for head in range(kv_heads):
            start = (kv_heads + head) * HEAD_DIM
            scores = score(local, head, every, mask)
            if waiting is not None:
                finish(*waiting)
            waiting = (local, head, scores, every[:, start : start + HEAD_DIM])
    finish(*waiting)


def attention(slots, cuts, odd, queries, own, straight, crossed, unit, previous):
    rows, features = queries.shape
    blocks, depth = slots.shape
    block = rows // blocks
    wide = features // UNITS
    near = len(straight)
    held = pl.BlockSpec(memory_space=pltpu.HBM)
    part = pl.BlockSpec((BLOCKS_PER_STEP * block, wide), lambda b, *_: (b, unit))
    operands = [slots, cuts, odd, queries, own, *straight, *crossed]
    in_specs = [part] + [held] * (1 + near + len(crossed))
    aliases = {}
    if previous is not None:
        aliases = {len(operands): 0}
        operands.append(previous)
        in_specs.append(held)
    return pl.pallas_call(
        functools.partial(attention_kernel, block, near),
        grid_spec=pltpu.PrefetchScalarGridSpec(
            num_scalar_prefetch=3,
            grid=(blocks // BLOCKS_PER_STEP,),
            in_specs=in_specs,
            out_specs=part,
            scratch_shapes=[
                pltpu.VMEM((depth + 1, *own.shape), own.dtype),
                pltpu.SemaphoreType.DMA((depth + 1,)),
            ],
        ),
        out_shape=jax.ShapeDtypeStruct((rows, features), jnp.bfloat16),
        input_output_aliases=aliases,
        compiler_params=pltpu.CompilerParams(vmem_limit_bytes=57 * MIB),
        cost_estimate=pl.CostEstimate(
            flops=4 * rows * wide * (depth + 1) * block,
            bytes_accessed=8 * MIB,
            transcendentals=rows * wide // HEAD_DIM * (depth + 1) * block,
        ),
        name="attention",
    )(*operands)


def shards(hidden, queries, norm_gain, key_weight, value_weight, anc_ids, anc_cut):
    blocks, depth = anc_ids.shape
    levels = depth + 1
    size = lax.axis_size("node")
    chains = size // levels
    near = depth // 2
    half = [index // chains // 2 for index in range(size)]
    even = [index // chains % 2 == 0 for index in range(size)]
    other = [index + chains if even[index] else index - chains for index in range(size)]
    odd = (lax.axis_index("node") // chains % 2).astype(jnp.int32).reshape(1)
    slots = jnp.where(anc_ids >= 0, anc_ids % blocks, 0)

    normed, first = norm_project(hidden, norm_gain, key_weight, value_weight)
    own = [first] + [project(normed, key_weight, value_weight, unit) for unit in range(1, UNITS)]
    def after(array, *earlier):
        return lax.optimization_barrier((array, *earlier))[0]

    straight = [{} for _ in range(UNITS)]
    crossed = [{} for _ in range(UNITS)]

    def step_across(s, unit, settled):
        source = own[unit] if s == 0 else straight[unit][s]
        both_ways = unit == UNITS - 1 and s == 0
        pairs = [
            (i, other[i])
            for i in range(size)
            if half[i] >= s and (s > 0 or even[i] or (both_ways and half[i] == 0))
        ]
        crossed[unit][s] = lax.ppermute(after(source, *settled), "node", pairs)
        return crossed[unit][s]

    def step_along(s, unit, settled):
        source = own[unit] if s == 1 else straight[unit][s - 1]
        shift = 2 * chains
        pairs = [(i, i + shift) for i in range(size - shift) if half[i] >= s - 1]
        straight[unit][s] = lax.ppermute(after(source, *settled), "node", pairs)
        return straight[unit][s]

    def step_down(unit, settled):
        shift = 2 * near * chains
        pairs = [(i, i + shift) for i in range(size - shift)]
        crossed[unit][near] = lax.ppermute(after(crossed[unit][0], *settled), "node", pairs)
        return crossed[unit][near]

    early, late = range(UNITS)
    across = [(s, unit) for s in range(near - 1) for unit in (early, late)]
    across += [(near - 1, early), (near, early), (near - 1, late)]
    along = [(1, early), (1, late)]
    along += [(s, early) for s in range(2, near + 1)] + [(s, late) for s in range(2, near + 1)]
    y_chain, z_chain = [], []
    for (s, unit), step in zip(across, [*along, None], strict=True):
        y_chain.append(step_across(s, unit, y_chain[-2:-1]))
        if step is not None:
            z_chain.append(step_along(*step, z_chain[-2:-1]))
        else:
            z_chain.append(step_down(late, z_chain[-2:-1]))
    result = None
    for unit in range(UNITS):
        result = attention(
            slots,
            anc_cut,
            odd,
            queries,
            own[unit],
            [straight[unit][s] for s in range(1, near + 1)],
            [crossed[unit][s] for s in range(near + 1)],
            unit,
            result,
        )
    return result


def solution(mesh):
    placed = (
        P(("groups", "node"), None),
        P(("groups", "node"), None),
        P(),
        P(),
        P(),
        P(("groups", "node"), None),
        P(("groups", "node"), None),
    )
    return jax.shard_map(
        shards, mesh=mesh, in_specs=placed, out_specs=P(("groups", "node"), None), check_vma=False
    )
```

```python
import functools
import jax
import jax.numpy as jnp
from jax import lax
from jax.experimental import pallas as pl
from jax.experimental.pallas import tpu as pltpu
from jax.sharding import PartitionSpec as P

HEAD_DIM = 128
EPS = 1e-05
LOG2E = 1.4426950408889634
MASKED = -1e30
MIB = 1024 * 1024
CHUNKS = 4
LOADS = 8
UNITS = 2
BLOCKS_PER_STEP = 4


def norm_project_kernel(
    x_hbm, gain_ref, key_hbm, value_hbm, normed_hbm, kv_ref,
    x_scr, weight_scr, even_scr, odd_scr, acc_scr, scale_scr, x_sem, key_sem, value_sem, normed_sem,
):
    loads, rows, chunk = x_scr.shape
    width = weight_scr.shape[2] // 2
    lanes = 128
    band = 128

    def span(c):
        return pl.ds(pl.multiple_of(c * chunk, chunk), chunk)

    def load_x(c):
        return pltpu.make_async_copy(x_hbm.at[:, span(c)], x_scr.at[c], x_sem.at[c])

    def load_weights(c):
        head = pl.ds(0, width)
        return [
            pltpu.make_async_copy(
                key_hbm.at[span(c), head], weight_scr.at[c, :, pl.ds(0, width)], key_sem.at[c]
            ),
            pltpu.make_async_copy(
                value_hbm.at[span(c), head], weight_scr.at[c, :, pl.ds(width, width)], value_sem.at[c]
            ),
        ]

    def store_normed(normed_scr, c):
        return pltpu.make_async_copy(
            normed_scr.at[c // 2], normed_hbm.at[:, span(c)], normed_sem.at[c]
        )

    for c in range(loads):
        load_x(c).start()
    scale_scr[...] = jnp.zeros_like(scale_scr)

    def square(c, carry):
        load_x(c).wait()

        @pl.when(c >= loads // 2)
        def _():
            for part in range(2):
                for copy in load_weights(2 * (c - loads // 2) + part):
                    copy.start()

        for first in range(0, rows, band):
            row = slice(first, first + band)
            total = scale_scr[row, :]
            for lane in range(0, chunk, lanes):
                x = x_scr[c, row, lane : lane + lanes].astype(jnp.float32)
                total += x * x
            scale_scr[row, :] = total
        return carry

    lax.fori_loop(0, loads, square, 0)
    mean_sq = jnp.sum(scale_scr[...], axis=-1, keepdims=True) / (loads * chunk)
    scale_scr[...] = jnp.broadcast_to(lax.rsqrt(mean_sq + EPS), scale_scr.shape)

    def normalise(normed_scr, c):
        for first in range(0, rows, band):
            row = slice(first, first + band)
            inverse = scale_scr[row, :]
            for lane in range(0, chunk, lanes):
                cols = slice(lane, lane + lanes)
                x = x_scr[c, row, cols].astype(jnp.float32)
                gain = gain_ref[c, :, cols]
                normed_scr[c // 2, row, cols] = (x * inverse * gain).astype(jnp.bfloat16)

    def multiply(normed_scr, c):
        for copy in load_weights(c):
            copy.wait()
        store_normed(normed_scr, c).start()
        acc_scr[...] += jnp.dot(
            normed_scr[c // 2], weight_scr[c], preferred_element_type=jnp.float32
        )

    normalise(even_scr, 0)
    acc_scr[...] = jnp.zeros_like(acc_scr)

    def pair(p, carry):
        multiply(even_scr, 2 * p)
        normalise(odd_scr, 2 * p + 1)
        multiply(odd_scr, 2 * p + 1)
        normalise(even_scr, 2 * p + 2)
        return carry

    lax.fori_loop(0, loads // 2 - 1, pair, 0)
    multiply(even_scr, loads - 2)
    normalise(odd_scr, loads - 1)
    multiply(odd_scr, loads - 1)
    for head in range(width // HEAD_DIM):
        for part in range(2):
            source = slice(part * width + head * HEAD_DIM, part * width + (head + 1) * HEAD_DIM)
            target = slice((2 * head + part) * HEAD_DIM, (2 * head + part + 1) * HEAD_DIM)
            kv_ref[:, target] = acc_scr[:, source].astype(jnp.bfloat16)
    for c in range(loads):
        store_normed(odd_scr if c % 2 else even_scr, c).wait()


def norm_project(hidden, gain, key_weight, value_weight):
    rows, features = hidden.shape
    width = key_weight.shape[1] // UNITS
    chunk = features // LOADS
    whole = pl.BlockSpec(memory_space=pltpu.VMEM)
    held = pl.BlockSpec(memory_space=pltpu.HBM)
    return pl.pallas_call(
        norm_project_kernel,
        in_specs=[held, whole, held, held],
        out_specs=[held, whole],
        out_shape=[
            jax.ShapeDtypeStruct((rows, features), jnp.bfloat16),
            jax.ShapeDtypeStruct((rows, 2 * width), jnp.bfloat16),
        ],
        scratch_shapes=[
            pltpu.VMEM((LOADS, rows, chunk), jnp.bfloat16),
            pltpu.VMEM((LOADS, chunk, 2 * width), jnp.bfloat16),
            pltpu.VMEM((LOADS // 2, rows, chunk), jnp.bfloat16),
            pltpu.VMEM((LOADS // 2, rows, chunk), jnp.bfloat16),
            pltpu.VMEM((rows, 2 * width), jnp.float32),
            pltpu.VMEM((rows, 128), jnp.float32),
            pltpu.SemaphoreType.DMA((LOADS,)),
            pltpu.SemaphoreType.DMA((LOADS,)),
            pltpu.SemaphoreType.DMA((LOADS,)),
            pltpu.SemaphoreType.DMA((LOADS,)),
        ],
        compiler_params=pltpu.CompilerParams(vmem_limit_bytes=57 * MIB),
        cost_estimate=pl.CostEstimate(
            flops=4 * rows * features * width, bytes_accessed=24 * MIB, transcendentals=0
        ),
        name="norm_project",
    )(hidden, gain.reshape(LOADS, 1, chunk), key_weight, value_weight)


def project_kernel(normed_ref, key_ref, value_ref, kv_ref, acc_scr):
    step = pl.program_id(0)
    width = key_ref.shape[1]
    normed = normed_ref[...]
    for part, weight in enumerate((key_ref, value_ref)):
        cols = slice(part * width, (part + 1) * width)
        term = jnp.dot(normed, weight[...], preferred_element_type=jnp.float32)
        acc_scr[:, cols] = jnp.where(step == 0, term, acc_scr[:, cols] + term)

    @pl.when(step == CHUNKS - 1)
    def _():
        for head in range(width // HEAD_DIM):
            for part in range(2):
                source = slice(part * width + head * HEAD_DIM, part * width + (head + 1) * HEAD_DIM)
                target = slice((2 * head + part) * HEAD_DIM, (2 * head + part + 1) * HEAD_DIM)
                kv_ref[:, target] = acc_scr[:, source].astype(jnp.bfloat16)


def project(normed, key_weight, value_weight, unit):
    rows, features = normed.shape
    chunk = features // CHUNKS
    width = key_weight.shape[1] // UNITS
    weight = pl.BlockSpec((chunk, width), lambda i: (i, unit))
    return pl.pallas_call(
        project_kernel,
        grid=(CHUNKS,),
        in_specs=[pl.BlockSpec((rows, chunk), lambda i: (0, i)), weight, weight],
        out_specs=pl.BlockSpec((rows, 2 * width), lambda i: (0, 0)),
        out_shape=jax.ShapeDtypeStruct((rows, 2 * width), jnp.bfloat16),
        scratch_shapes=[pltpu.VMEM((rows, 2 * width), jnp.float32)],
        compiler_params=pltpu.CompilerParams(vmem_limit_bytes=57 * MIB),
        cost_estimate=pl.CostEstimate(
            flops=4 * rows * features * width, bytes_accessed=16 * MIB, transcendentals=0
        ),
        name="project",
    )(normed, key_weight, value_weight)


def attention_kernel(block, near, slot_ref, cut_ref, odd_ref, q_ref, *refs):
    own_hbm, straight, crossed = refs[0], refs[1 : near + 1], refs[near + 1 : 2 * near + 2]
    out_ref, kv_scr, sems = refs[-3:]
    kv_heads, levels = kv_scr.shape[:2]
    depth = levels - 1
    width = kv_scr.shape[3]
    per_group = q_ref.shape[1] // HEAD_DIM
    head, step = pl.program_id(0), pl.program_id(1)
    scale = HEAD_DIM**-0.5 * LOG2E

    def fetch(index):
        def copy(ref, level, number):
            return pltpu.make_async_copy(
                ref.at[:, pl.ds(pl.multiple_of(index * width, width), width)],
                kv_scr.at[index, level],
                sems.at[index, number],
            )

        copies = [copy(own_hbm, depth, 0)]
        for s, ref in enumerate(straight):
            copies.append(copy(ref, 2 * s + 1, s + 1))
        for s, ref in enumerate(crossed):
            level = 2 * lax.rem(s + odd_ref[0] + near, near + 1)
            copies.append(copy(ref, level, near + s + 1))
        return copies

    @pl.when((head == 0) & (step == 0))
    def _():
        for index in range(kv_heads):
            for copy in fetch(index):
                copy.start()

    @pl.when(step == 0)
    def _():
        for copy in fetch(head):
            copy.wait()

    token = lax.broadcasted_iota(jnp.int32, (block, HEAD_DIM), 0)
    lane = lax.broadcasted_iota(jnp.int32, (block, HEAD_DIM), 1)
    hidden_later = jnp.where((lane >= block) & (lane - block > token), MASKED, 0.0)
    query_mask = jnp.where(lane == 0, 1.0, hidden_later).astype(jnp.bfloat16)
    query_mask = jnp.concatenate([query_mask] * per_group, axis=0)
    own_mask = jnp.where(lane - block == token, 1.0, 0.0).astype(jnp.bfloat16)

    def score(local):
        here = step * BLOCKS_PER_STEP + local
        pieces, masks = [], []
        for k in range(depth):
            rows = pl.ds(pl.multiple_of(slot_ref[here, k] * block, block), block)
            pieces.append(kv_scr[head, k, rows, :])
            unseen = (lane == 0) & (token >= cut_ref[here, k])
            masks.append(jnp.where(unseen, MASKED, 0.0).astype(jnp.bfloat16))
        rows = pl.ds(pl.multiple_of(here * block, block), block)
        pieces.append(kv_scr[head, depth, rows, :])
        masks.append(own_mask)
        every = jnp.concatenate(pieces, axis=0)
        keys = jnp.concatenate([every[:, :HEAD_DIM], jnp.concatenate(masks, axis=0)], axis=1)
        rows = slice(local * block, (local + 1) * block)
        queries = jnp.concatenate(
            [q_ref[rows, r * HEAD_DIM : (r + 1) * HEAD_DIM] for r in range(per_group)], axis=0
        )
        queries = jnp.concatenate([queries, query_mask], axis=1)
        scores = lax.dot_general(
            queries, keys, (((1,), (1,)), ((), ())), preferred_element_type=jnp.float32
        )
        return scores, every[:, HEAD_DIM:]

    def finish(local, scores, values):
        peak = jnp.max(scores, axis=-1, keepdims=True)
        weights = jnp.exp2((scores - peak) * scale).astype(jnp.bfloat16)
        padded = jnp.concatenate([values, jnp.ones_like(values)], axis=1)
        both = jnp.dot(weights, padded, preferred_element_type=jnp.float32)
        context = (both[:, :HEAD_DIM] * (1.0 / both[:, HEAD_DIM:])).astype(jnp.bfloat16)
        for r in range(per_group):
            out_ref[local * block : (local + 1) * block, r * HEAD_DIM : (r + 1) * HEAD_DIM] = context[
                r * block : (r + 1) * block
            ]

    waiting = None
    for local in range(BLOCKS_PER_STEP):
        scores, values = score(local)
        if waiting is not None:
            finish(*waiting)
        waiting = (local, scores, values)
    finish(*waiting)


def attention(slots, cuts, odd, queries, own, straight, crossed, unit, previous):
    rows, features = queries.shape
    blocks, depth = slots.shape
    block = rows // blocks
    wide = features // UNITS
    near = len(straight)
    held = pl.BlockSpec(memory_space=pltpu.HBM)
    kv_heads = own.shape[1] // (2 * HEAD_DIM)
    per_head = wide // kv_heads
    part = pl.BlockSpec(
        (BLOCKS_PER_STEP * block, per_head), lambda h, b, *_: (b, unit * kv_heads + h)
    )
    operands = [slots, cuts, odd, queries, own, *straight, *crossed]
    in_specs = [part] + [held] * (1 + near + len(crossed))
    aliases = {}
    if previous is not None:
        aliases = {len(operands): 0}
        operands.append(previous)
        in_specs.append(held)
    return pl.pallas_call(
        functools.partial(attention_kernel, block, near),
        grid_spec=pltpu.PrefetchScalarGridSpec(
            num_scalar_prefetch=3,
            grid=(kv_heads, blocks // BLOCKS_PER_STEP),
            in_specs=in_specs,
            out_specs=part,
            scratch_shapes=[
                pltpu.VMEM((kv_heads, depth + 1, rows, 2 * HEAD_DIM), own.dtype),
                pltpu.SemaphoreType.DMA((kv_heads, depth + 1)),
            ],
        ),
        out_shape=jax.ShapeDtypeStruct((rows, features), jnp.bfloat16),
        input_output_aliases=aliases,
        compiler_params=pltpu.CompilerParams(vmem_limit_bytes=57 * MIB),
        cost_estimate=pl.CostEstimate(
            flops=4 * rows * wide * (depth + 1) * block,
            bytes_accessed=8 * MIB,
            transcendentals=rows * wide // HEAD_DIM * (depth + 1) * block,
        ),
        name="attention",
    )(*operands)


def shards(hidden, queries, norm_gain, key_weight, value_weight, anc_ids, anc_cut):
    blocks, depth = anc_ids.shape
    levels = depth + 1
    size = lax.axis_size("node")
    chains = size // levels
    near = depth // 2
    half = [index // chains // 2 for index in range(size)]
    even = [index // chains % 2 == 0 for index in range(size)]
    other = [index + chains if even[index] else index - chains for index in range(size)]
    odd = (lax.axis_index("node") // chains % 2).astype(jnp.int32).reshape(1)
    slots = jnp.where(anc_ids >= 0, anc_ids % blocks, 0)

    normed, first = norm_project(hidden, norm_gain, key_weight, value_weight)
    own = [first] + [project(normed, key_weight, value_weight, unit) for unit in range(1, UNITS)]
    def after(array, *earlier):
        return lax.optimization_barrier((array, *earlier))[0]

    straight = [{} for _ in range(UNITS)]
    crossed = [{} for _ in range(UNITS)]

    def step_across(s, unit, settled):
        source = own[unit] if s == 0 else straight[unit][s]
        both_ways = unit == UNITS - 1 and s == 0
        pairs = [
            (i, other[i])
            for i in range(size)
            if half[i] >= s and (s > 0 or even[i] or (both_ways and half[i] == 0))
        ]
        crossed[unit][s] = lax.ppermute(after(source, *settled), "node", pairs)
        return crossed[unit][s]

    def step_along(s, unit, settled):
        source = straight[unit][1] if s == 2 else own[unit]
        shift = 2 * (1 if s == 2 else s) * chains
        pairs = [(i, i + shift) for i in range(size - shift) if half[i] >= (s == 2)]
        straight[unit][s] = lax.ppermute(after(source, *settled), "node", pairs)
        return straight[unit][s]

    def step_down(unit, settled):
        shift = 2 * near * chains
        pairs = [(i, i + shift) for i in range(size - shift)]
        crossed[unit][near] = lax.ppermute(after(crossed[unit][0], *settled), "node", pairs)
        return crossed[unit][near]

    early, late = range(UNITS)
    across = [(s, unit) for s in range(near - 1) for unit in (early, late)]
    across += [(near - 1, early), (near, early), (near - 1, late)]
    along = [(1, early), (1, late)]
    along += [(s, early) for s in range(2, near + 1)] + [(2, late), None]
    along += [(s, late) for s in range(3, near + 1)]
    y_chain, z_chain = [], []
    for (s, unit), step in zip(across, along, strict=True):
        y_chain.append(step_across(s, unit, y_chain[-2:-1]))
        if step is not None:
            z_chain.append(step_along(*step, z_chain[-2:-1]))
        else:
            z_chain.append(step_down(late, z_chain[-2:-1]))
    result = None
    for unit in range(UNITS):
        result = attention(
            slots,
            anc_cut,
            odd,
            queries,
            own[unit],
            [straight[unit][s] for s in range(1, near + 1)],
            [crossed[unit][s] for s in range(near + 1)],
            unit,
            result,
        )
    return result


def solution(mesh):
    placed = (
        P(("groups", "node"), None),
        P(("groups", "node"), None),
        P(),
        P(),
        P(),
        P(("groups", "node"), None),
        P(("groups", "node"), None),
    )
    return jax.shard_map(
        shards, mesh=mesh, in_specs=placed, out_specs=P(("groups", "node"), None), check_vma=False
    )
```

```python
import functools
import jax
import jax.numpy as jnp
from jax import lax
from jax.experimental import pallas as pl
from jax.experimental.pallas import tpu as pltpu
from jax.sharding import PartitionSpec as P

HEAD_DIM = 128
EPS = 1e-05
LOG2E = 1.4426950408889634
MASKED = -1e30
MIB = 1024 * 1024
CHUNKS = 4
LOADS = 8
UNITS = 2
BLOCKS_PER_STEP = 4


def norm_project_kernel(
    x_hbm, gain_ref, key_hbm, value_hbm, normed_hbm, kv_ref,
    x_scr, key_scr, value_scr, even_scr, odd_scr, acc_scr, scale_scr, x_sem, key_sem, value_sem, normed_sem,
):
    loads, rows, chunk = x_scr.shape
    width = key_scr.shape[2] // UNITS
    lanes = 128
    band = 128

    def span(c):
        return pl.ds(pl.multiple_of(c * chunk, chunk), chunk)

    def load_x(c):
        return pltpu.make_async_copy(x_hbm.at[:, span(c)], x_scr.at[c], x_sem.at[c])

    def load_weights(c):
        return [
            pltpu.make_async_copy(hbm.at[span(c)], scr.at[c], sem.at[c])
            for hbm, scr, sem in ((key_hbm, key_scr, key_sem), (value_hbm, value_scr, value_sem))
        ]

    def store_normed(normed_scr, c):
        return pltpu.make_async_copy(
            normed_scr.at[c // 2], normed_hbm.at[:, span(c)], normed_sem.at[c]
        )

    for c in range(loads):
        load_x(c).start()
    scale_scr[...] = jnp.zeros_like(scale_scr)

    def square(c, carry):
        load_x(c).wait()

        @pl.when(c >= loads // 2)
        def _():
            for part in range(2):
                for copy in load_weights(2 * (c - loads // 2) + part):
                    copy.start()

        for first in range(0, rows, band):
            row = slice(first, first + band)
            total = scale_scr[row, :]
            for lane in range(0, chunk, lanes):
                x = x_scr[c, row, lane : lane + lanes].astype(jnp.float32)
                total += x * x
            scale_scr[row, :] = total
        return carry

    lax.fori_loop(0, loads, square, 0)
    mean_sq = jnp.sum(scale_scr[...], axis=-1, keepdims=True) / (loads * chunk)
    scale_scr[...] = jnp.broadcast_to(lax.rsqrt(mean_sq + EPS), scale_scr.shape)

    def normalise(normed_scr, c):
        for first in range(0, rows, band):
            row = slice(first, first + band)
            inverse = scale_scr[row, :]
            for lane in range(0, chunk, lanes):
                cols = slice(lane, lane + lanes)
                x = x_scr[c, row, cols].astype(jnp.float32)
                gain = gain_ref[c, :, cols]
                normed_scr[c // 2, row, cols] = (x * inverse * gain).astype(jnp.bfloat16)

    def multiply(normed_scr, c):
        for copy in load_weights(c):
            copy.wait()
        store_normed(normed_scr, c).start()
        normed = normed_scr[c // 2]
        for part, weight in enumerate((key_scr, value_scr)):
            acc_scr[:, part * width : (part + 1) * width] += jnp.dot(
                normed, weight[c, :, :width], preferred_element_type=jnp.float32
            )

    normalise(even_scr, 0)
    acc_scr[...] = jnp.zeros_like(acc_scr)

    def pair(p, carry):
        multiply(even_scr, 2 * p)
        normalise(odd_scr, 2 * p + 1)
        multiply(odd_scr, 2 * p + 1)
        normalise(even_scr, 2 * p + 2)
        return carry

    lax.fori_loop(0, loads // 2 - 1, pair, 0)
    multiply(even_scr, loads - 2)
    normalise(odd_scr, loads - 1)
    multiply(odd_scr, loads - 1)
    for head in range(width // HEAD_DIM):
        for part in range(2):
            source = slice(part * width + head * HEAD_DIM, part * width + (head + 1) * HEAD_DIM)
            target = slice((2 * head + part) * HEAD_DIM, (2 * head + part + 1) * HEAD_DIM)
            kv_ref[:, target] = acc_scr[:, source].astype(jnp.bfloat16)
    for c in range(loads):
        store_normed(odd_scr if c % 2 else even_scr, c).wait()


def norm_project(hidden, gain, key_weight, value_weight):
    rows, features = hidden.shape
    width = key_weight.shape[1] // UNITS
    chunk = features // LOADS
    whole = pl.BlockSpec(memory_space=pltpu.VMEM)
    held = pl.BlockSpec(memory_space=pltpu.HBM)
    return pl.pallas_call(
        norm_project_kernel,
        in_specs=[held, whole, held, held],
        out_specs=[held, whole],
        out_shape=[
            jax.ShapeDtypeStruct((rows, features), jnp.bfloat16),
            jax.ShapeDtypeStruct((rows, 2 * width), jnp.bfloat16),
        ],
        scratch_shapes=[
            pltpu.VMEM((LOADS, rows, chunk), jnp.bfloat16),
            pltpu.VMEM((LOADS, chunk, key_weight.shape[1]), jnp.bfloat16),
            pltpu.VMEM((LOADS, chunk, key_weight.shape[1]), jnp.bfloat16),
            pltpu.VMEM((LOADS // 2, rows, chunk), jnp.bfloat16),
            pltpu.VMEM((LOADS // 2, rows, chunk), jnp.bfloat16),
            pltpu.VMEM((rows, 2 * width), jnp.float32),
            pltpu.VMEM((rows, 128), jnp.float32),
            pltpu.SemaphoreType.DMA((LOADS,)),
            pltpu.SemaphoreType.DMA((LOADS,)),
            pltpu.SemaphoreType.DMA((LOADS,)),
            pltpu.SemaphoreType.DMA((LOADS,)),
        ],
        compiler_params=pltpu.CompilerParams(vmem_limit_bytes=57 * MIB),
        cost_estimate=pl.CostEstimate(
            flops=4 * rows * features * width, bytes_accessed=24 * MIB, transcendentals=0
        ),
        name="norm_project",
    )(hidden, gain.reshape(LOADS, 1, chunk), key_weight, value_weight)


def project_kernel(unit, normed_ref, key_ref, value_ref, kv_ref, acc_scr):
    step = pl.program_id(0)
    width = key_ref.shape[1] // UNITS
    mine = slice(unit * width, (unit + 1) * width)
    normed = normed_ref[...]
    for part, weight in enumerate((key_ref, value_ref)):
        cols = slice(part * width, (part + 1) * width)
        term = jnp.dot(normed, weight[:, mine], preferred_element_type=jnp.float32)
        acc_scr[:, cols] = jnp.where(step == 0, term, acc_scr[:, cols] + term)

    @pl.when(step == CHUNKS - 1)
    def _():
        for head in range(width // HEAD_DIM):
            for part in range(2):
                source = slice(part * width + head * HEAD_DIM, part * width + (head + 1) * HEAD_DIM)
                target = slice((2 * head + part) * HEAD_DIM, (2 * head + part + 1) * HEAD_DIM)
                kv_ref[:, target] = acc_scr[:, source].astype(jnp.bfloat16)


def project(normed, key_weight, value_weight, unit):
    rows, features = normed.shape
    chunk = features // CHUNKS
    width = key_weight.shape[1] // UNITS
    weight = pl.BlockSpec((chunk, key_weight.shape[1]), lambda i: (i, 0))
    return pl.pallas_call(
        functools.partial(project_kernel, unit),
        grid=(CHUNKS,),
        in_specs=[pl.BlockSpec((rows, chunk), lambda i: (0, i)), weight, weight],
        out_specs=pl.BlockSpec((rows, 2 * width), lambda i: (0, 0)),
        out_shape=jax.ShapeDtypeStruct((rows, 2 * width), jnp.bfloat16),
        scratch_shapes=[pltpu.VMEM((rows, 2 * width), jnp.float32)],
        compiler_params=pltpu.CompilerParams(vmem_limit_bytes=57 * MIB),
        cost_estimate=pl.CostEstimate(
            flops=4 * rows * features * width, bytes_accessed=16 * MIB, transcendentals=0
        ),
        name="project",
    )(normed, key_weight, value_weight)


def attention_kernel(block, near, slot_ref, cut_ref, odd_ref, q_ref, *refs):
    own_hbm, straight, crossed = refs[0], refs[1 : near + 1], refs[near + 1 : 2 * near + 2]
    out_ref, kv_scr, sems = refs[-3:]
    kv_heads, levels = kv_scr.shape[:2]
    depth = levels - 1
    width = kv_scr.shape[3]
    per_group = q_ref.shape[1] // HEAD_DIM
    head, step = pl.program_id(0), pl.program_id(1)
    scale = HEAD_DIM**-0.5 * LOG2E

    def fetch(index):
        def copy(ref, level, number):
            return pltpu.make_async_copy(
                ref.at[:, pl.ds(pl.multiple_of(index * width, width), width)],
                kv_scr.at[index, level],
                sems.at[index, number],
            )

        copies = [copy(own_hbm, depth, 0)]
        for s, ref in enumerate(straight):
            copies.append(copy(ref, 2 * s + 1, s + 1))
        for s, ref in enumerate(crossed):
            level = 2 * lax.rem(s + odd_ref[0] + near, near + 1)
            copies.append(copy(ref, level, near + s + 1))
        return copies

    @pl.when((head == 0) & (step == 0))
    def _():
        for index in range(kv_heads):
            for copy in fetch(index):
                copy.start()

    @pl.when(step == 0)
    def _():
        for copy in fetch(head):
            copy.wait()

    token = lax.broadcasted_iota(jnp.int32, (block, HEAD_DIM), 0)
    lane = lax.broadcasted_iota(jnp.int32, (block, HEAD_DIM), 1)
    hidden_later = jnp.where((lane >= block) & (lane - block > token), MASKED, 0.0)
    query_mask = jnp.where(lane == 0, 1.0, hidden_later).astype(jnp.bfloat16)
    query_mask = jnp.concatenate([query_mask] * per_group, axis=0)
    own_mask = jnp.where(lane - block == token, 1.0, 0.0).astype(jnp.bfloat16)

    def score(local):
        here = step * BLOCKS_PER_STEP + local
        pieces, masks = [], []
        for k in range(depth):
            rows = pl.ds(pl.multiple_of(slot_ref[here, k] * block, block), block)
            pieces.append(kv_scr[head, k, rows, :])
            unseen = (lane == 0) & (token >= cut_ref[here, k])
            masks.append(jnp.where(unseen, MASKED, 0.0).astype(jnp.bfloat16))
        rows = pl.ds(pl.multiple_of(here * block, block), block)
        pieces.append(kv_scr[head, depth, rows, :])
        masks.append(own_mask)
        every = jnp.concatenate(pieces, axis=0)
        keys = jnp.concatenate([every[:, :HEAD_DIM], jnp.concatenate(masks, axis=0)], axis=1)
        rows = slice(local * block, (local + 1) * block)
        queries = jnp.concatenate(
            [q_ref[rows, r * HEAD_DIM : (r + 1) * HEAD_DIM] for r in range(per_group)], axis=0
        )
        queries = jnp.concatenate([queries, query_mask], axis=1)
        scores = lax.dot_general(
            queries, keys, (((1,), (1,)), ((), ())), preferred_element_type=jnp.float32
        )
        return scores, every[:, HEAD_DIM:]

    def finish(local, scores, values):
        peak = jnp.max(scores, axis=-1, keepdims=True)
        weights = jnp.exp2((scores - peak) * scale).astype(jnp.bfloat16)
        padded = jnp.concatenate([values, jnp.ones_like(values)], axis=1)
        both = jnp.dot(weights, padded, preferred_element_type=jnp.float32)
        context = (both[:, :HEAD_DIM] * (1.0 / both[:, HEAD_DIM:])).astype(jnp.bfloat16)
        for r in range(per_group):
            out_ref[local * block : (local + 1) * block, r * HEAD_DIM : (r + 1) * HEAD_DIM] = context[
                r * block : (r + 1) * block
            ]

    waiting = None
    for local in range(BLOCKS_PER_STEP):
        scores, values = score(local)
        if waiting is not None:
            finish(*waiting)
        waiting = (local, scores, values)
    finish(*waiting)


def attention(slots, cuts, odd, queries, own, straight, crossed, unit, previous):
    rows, features = queries.shape
    blocks, depth = slots.shape
    block = rows // blocks
    wide = features // UNITS
    near = len(straight)
    held = pl.BlockSpec(memory_space=pltpu.HBM)
    kv_heads = own.shape[1] // (2 * HEAD_DIM)
    per_head = wide // kv_heads
    part = pl.BlockSpec(
        (BLOCKS_PER_STEP * block, per_head), lambda h, b, *_: (b, unit * kv_heads + h)
    )
    operands = [slots, cuts, odd, queries, own, *straight, *crossed]
    in_specs = [part] + [held] * (1 + near + len(crossed))
    aliases = {}
    if previous is not None:
        aliases = {len(operands): 0}
        operands.append(previous)
        in_specs.append(held)
    return pl.pallas_call(
        functools.partial(attention_kernel, block, near),
        grid_spec=pltpu.PrefetchScalarGridSpec(
            num_scalar_prefetch=3,
            grid=(kv_heads, blocks // BLOCKS_PER_STEP),
            in_specs=in_specs,
            out_specs=part,
            scratch_shapes=[
                pltpu.VMEM((kv_heads, depth + 1, rows, 2 * HEAD_DIM), own.dtype),
                pltpu.SemaphoreType.DMA((kv_heads, depth + 1)),
            ],
        ),
        out_shape=jax.ShapeDtypeStruct((rows, features), jnp.bfloat16),
        input_output_aliases=aliases,
        compiler_params=pltpu.CompilerParams(vmem_limit_bytes=57 * MIB),
        cost_estimate=pl.CostEstimate(
            flops=4 * rows * wide * (depth + 1) * block,
            bytes_accessed=8 * MIB,
            transcendentals=rows * wide // HEAD_DIM * (depth + 1) * block,
        ),
        name="attention",
    )(*operands)


def shards(hidden, queries, norm_gain, key_weight, value_weight, anc_ids, anc_cut):
    blocks, depth = anc_ids.shape
    levels = depth + 1
    size = lax.axis_size("node")
    chains = size // levels
    near = depth // 2
    half = [index // chains // 2 for index in range(size)]
    even = [index // chains % 2 == 0 for index in range(size)]
    other = [index + chains if even[index] else index - chains for index in range(size)]
    odd = (lax.axis_index("node") // chains % 2).astype(jnp.int32).reshape(1)
    slots = jnp.where(anc_ids >= 0, anc_ids % blocks, 0)

    normed, first = norm_project(hidden, norm_gain, key_weight, value_weight)
    own = [first] + [project(normed, key_weight, value_weight, unit) for unit in range(1, UNITS)]
    def after(array, *earlier):
        return lax.optimization_barrier((array, *earlier))[0]

    straight = [{} for _ in range(UNITS)]
    crossed = [{} for _ in range(UNITS)]

    def step_across(s, unit, settled):
        source = own[unit] if s == 0 else straight[unit][s]
        both_ways = unit == UNITS - 1 and s == 0
        pairs = [
            (i, other[i])
            for i in range(size)
            if half[i] >= s and (s > 0 or even[i] or (both_ways and half[i] == 0))
        ]
        crossed[unit][s] = lax.ppermute(after(source, *settled), "node", pairs)
        return crossed[unit][s]

    def step_along(s, unit, settled):
        source = own[unit] if s == 1 else straight[unit][s - 1]
        shift = 2 * chains
        pairs = [(i, i + shift) for i in range(size - shift) if half[i] >= s - 1]
        straight[unit][s] = lax.ppermute(after(source, *settled), "node", pairs)
        return straight[unit][s]

    def step_down(unit, settled):
        shift = 2 * near * chains
        pairs = [(i, i + shift) for i in range(size - shift)]
        crossed[unit][near] = lax.ppermute(after(crossed[unit][0], *settled), "node", pairs)
        return crossed[unit][near]

    early, late = range(UNITS)
    across = [(s, unit) for s in range(near - 1) for unit in (early, late)]
    across += [(near - 1, early), (near, early), (near - 1, late)]
    along = [(1, early), (1, late)]
    along += [(s, early) for s in range(2, near + 1)] + [(s, late) for s in range(2, near)]
    y_chain, z_chain = [], []
    for index, (s, unit) in enumerate(across):
        second = [own[late]] if index == 2 else []
        y_chain.append(step_across(s, unit, y_chain[-2:-1] + second))
        if index < len(along):
            z_chain.append(step_along(*along[index], z_chain[-2:-1] + second))
    down = step_down(late, [z_chain[-2], y_chain[-3]])
    step_along(near, late, [down])
    result = None
    for unit in range(UNITS):
        result = attention(
            slots,
            anc_cut,
            odd,
            queries,
            own[unit],
            [straight[unit][s] for s in range(1, near + 1)],
            [crossed[unit][s] for s in range(near + 1)],
            unit,
            result,
        )
    return result


def solution(mesh):
    placed = (
        P(("groups", "node"), None),
        P(("groups", "node"), None),
        P(),
        P(),
        P(),
        P(("groups", "node"), None),
        P(("groups", "node"), None),
    )
    return jax.shard_map(
        shards, mesh=mesh, in_specs=placed, out_specs=P(("groups", "node"), None), check_vma=False
    )
```

```python
import functools
import jax
import jax.numpy as jnp
from jax import lax
from jax.experimental import pallas as pl
from jax.experimental.pallas import tpu as pltpu
from jax.sharding import PartitionSpec as P

HEAD_DIM = 128
EPS = 1e-05
LOG2E = 1.4426950408889634
MASKED = -1e30
MIB = 1024 * 1024
CHUNKS = 8
LOADS = 8
UNITS = 2
BLOCKS_PER_STEP = 4


def norm_project_kernel(
    x_hbm, gain_ref, key_hbm, value_hbm, normed_hbm, kv_ref,
    x_scr, wide_scr, weight_scr, even_scr, odd_scr, acc_scr, scale_scr, x_sem, key_sem, value_sem, normed_sem,
):
    loads, rows, chunk = x_scr.shape
    width = weight_scr.shape[2] // 2
    lanes = 128
    band = 128

    def span(c):
        return pl.ds(pl.multiple_of(c * chunk, chunk), chunk)

    def load_x(c):
        return pltpu.make_async_copy(x_hbm.at[:, span(c)], x_scr.at[c], x_sem.at[c])

    def load_weights(c):
        head = pl.ds(0, width)
        return [
            pltpu.make_async_copy(
                key_hbm.at[span(c), head], weight_scr.at[c, :, pl.ds(0, width)], key_sem.at[c]
            ),
            pltpu.make_async_copy(
                value_hbm.at[span(c), head], weight_scr.at[c, :, pl.ds(width, width)], value_sem.at[c]
            ),
        ]

    def store_normed(normed_scr, c):
        return pltpu.make_async_copy(
            normed_scr.at[c // 2], normed_hbm.at[:, span(c)], normed_sem.at[c]
        )

    for c in range(loads):
        load_x(c).start()
    scale_scr[...] = jnp.zeros_like(scale_scr)

    def square(c, carry):
        load_x(c).wait()

        @pl.when(c >= loads // 2)
        def _():
            for part in range(2):
                for copy in load_weights(2 * (c - loads // 2) + part):
                    copy.start()

        for first in range(0, rows, band):
            row = slice(first, first + band)
            total = scale_scr[row, :]
            for lane in range(0, chunk, lanes):
                x = x_scr[c, row, lane : lane + lanes].astype(jnp.float32)
                wide_scr[c, row, lane : lane + lanes] = x
                total += x * x
            scale_scr[row, :] = total
        return carry

    lax.fori_loop(0, loads, square, 0)
    mean_sq = jnp.sum(scale_scr[...], axis=-1, keepdims=True) / (loads * chunk)
    scale_scr[...] = jnp.broadcast_to(lax.rsqrt(mean_sq + EPS), scale_scr.shape)

    def normalise(normed_scr, c):
        for first in range(0, rows, band):
            row = slice(first, first + band)
            inverse = scale_scr[row, :]
            for lane in range(0, chunk, lanes):
                cols = slice(lane, lane + lanes)
                x = wide_scr[c, row, cols]
                gain = gain_ref[c, :, cols]
                normed_scr[c // 2, row, cols] = (x * inverse * gain).astype(jnp.bfloat16)

    def multiply(normed_scr, c):
        for copy in load_weights(c):
            copy.wait()
        store_normed(normed_scr, c).start()
        acc_scr[...] += jnp.dot(
            normed_scr[c // 2], weight_scr[c], preferred_element_type=jnp.float32
        )

    normalise(even_scr, 0)
    acc_scr[...] = jnp.zeros_like(acc_scr)

    def pair(p, carry):
        multiply(even_scr, 2 * p)
        normalise(odd_scr, 2 * p + 1)
        multiply(odd_scr, 2 * p + 1)
        normalise(even_scr, 2 * p + 2)
        return carry

    lax.fori_loop(0, loads // 2 - 1, pair, 0)
    multiply(even_scr, loads - 2)
    normalise(odd_scr, loads - 1)
    multiply(odd_scr, loads - 1)
    for head in range(width // HEAD_DIM):
        for part in range(2):
            source = slice(part * width + head * HEAD_DIM, part * width + (head + 1) * HEAD_DIM)
            target = slice((2 * head + part) * HEAD_DIM, (2 * head + part + 1) * HEAD_DIM)
            kv_ref[:, target] = acc_scr[:, source].astype(jnp.bfloat16)
    for c in range(loads):
        store_normed(odd_scr if c % 2 else even_scr, c).wait()


def norm_project(hidden, gain, key_weight, value_weight):
    rows, features = hidden.shape
    width = key_weight.shape[1] // UNITS
    chunk = features // LOADS
    whole = pl.BlockSpec(memory_space=pltpu.VMEM)
    held = pl.BlockSpec(memory_space=pltpu.HBM)
    return pl.pallas_call(
        norm_project_kernel,
        in_specs=[held, whole, held, held],
        out_specs=[held, whole],
        out_shape=[
            jax.ShapeDtypeStruct((rows, features), jnp.bfloat16),
            jax.ShapeDtypeStruct((rows, 2 * width), jnp.bfloat16),
        ],
        scratch_shapes=[
            pltpu.VMEM((LOADS, rows, chunk), jnp.bfloat16),
            pltpu.VMEM((LOADS, rows, chunk), jnp.float32),
            pltpu.VMEM((LOADS, chunk, 2 * width), jnp.bfloat16),
            pltpu.VMEM((LOADS // 2, rows, chunk), jnp.bfloat16),
            pltpu.VMEM((LOADS // 2, rows, chunk), jnp.bfloat16),
            pltpu.VMEM((rows, 2 * width), jnp.float32),
            pltpu.VMEM((rows, 128), jnp.float32),
            pltpu.SemaphoreType.DMA((LOADS,)),
            pltpu.SemaphoreType.DMA((LOADS,)),
            pltpu.SemaphoreType.DMA((LOADS,)),
            pltpu.SemaphoreType.DMA((LOADS,)),
        ],
        compiler_params=pltpu.CompilerParams(vmem_limit_bytes=57 * MIB),
        cost_estimate=pl.CostEstimate(
            flops=4 * rows * features * width, bytes_accessed=24 * MIB, transcendentals=0
        ),
        name="norm_project",
    )(hidden, gain.reshape(LOADS, 1, chunk), key_weight, value_weight)


def project_kernel(normed_ref, key_ref, value_ref, kv_ref, acc_scr):
    step = pl.program_id(0)
    width = key_ref.shape[1]
    normed = normed_ref[...]
    for part, weight in enumerate((key_ref, value_ref)):
        cols = slice(part * width, (part + 1) * width)
        term = jnp.dot(normed, weight[...], preferred_element_type=jnp.float32)
        acc_scr[:, cols] = jnp.where(step == 0, term, acc_scr[:, cols] + term)

    @pl.when(step == CHUNKS - 1)
    def _():
        for head in range(width // HEAD_DIM):
            for part in range(2):
                source = slice(part * width + head * HEAD_DIM, part * width + (head + 1) * HEAD_DIM)
                target = slice((2 * head + part) * HEAD_DIM, (2 * head + part + 1) * HEAD_DIM)
                kv_ref[:, target] = acc_scr[:, source].astype(jnp.bfloat16)


def project(normed, key_weight, value_weight, unit):
    rows, features = normed.shape
    chunk = features // CHUNKS
    width = key_weight.shape[1] // UNITS
    weight = pl.BlockSpec((chunk, width), lambda i: (i, unit))
    return pl.pallas_call(
        project_kernel,
        grid=(CHUNKS,),
        in_specs=[pl.BlockSpec((rows, chunk), lambda i: (0, i)), weight, weight],
        out_specs=pl.BlockSpec((rows, 2 * width), lambda i: (0, 0)),
        out_shape=jax.ShapeDtypeStruct((rows, 2 * width), jnp.bfloat16),
        scratch_shapes=[pltpu.VMEM((rows, 2 * width), jnp.float32)],
        compiler_params=pltpu.CompilerParams(vmem_limit_bytes=57 * MIB),
        cost_estimate=pl.CostEstimate(
            flops=4 * rows * features * width, bytes_accessed=16 * MIB, transcendentals=0
        ),
        name="project",
    )(normed, key_weight, value_weight)


def attention_kernel(block, near, slot_ref, cut_ref, odd_ref, q_ref, *refs):
    own_hbm, straight, crossed = refs[0], refs[1 : near + 1], refs[near + 1 : 2 * near + 2]
    out_ref, kv_scr, sems = refs[-3:]
    kv_heads, levels = kv_scr.shape[:2]
    depth = levels - 1
    width = kv_scr.shape[3]
    per_group = q_ref.shape[1] // HEAD_DIM
    head, step = pl.program_id(0), pl.program_id(1)
    scale = HEAD_DIM**-0.5 * LOG2E

    def fetch(index):
        def copy(ref, level, number):
            return pltpu.make_async_copy(
                ref.at[:, pl.ds(pl.multiple_of(index * width, width), width)],
                kv_scr.at[index, level],
                sems.at[index, number],
            )

        copies = [copy(own_hbm, depth, 0)]
        for s, ref in enumerate(straight):
            copies.append(copy(ref, 2 * s + 1, s + 1))
        for s, ref in enumerate(crossed):
            level = 2 * lax.rem(s + odd_ref[0] + near, near + 1)
            copies.append(copy(ref, level, near + s + 1))
        return copies

    @pl.when((head == 0) & (step == 0))
    def _():
        for index in range(kv_heads):
            for copy in fetch(index):
                copy.start()

    @pl.when(step == 0)
    def _():
        for copy in fetch(head):
            copy.wait()

    token = lax.broadcasted_iota(jnp.int32, (block, HEAD_DIM), 0)
    lane = lax.broadcasted_iota(jnp.int32, (block, HEAD_DIM), 1)
    hidden_later = jnp.where((lane >= block) & (lane - block > token), MASKED, 0.0)
    query_mask = jnp.where(lane == 0, 1.0, hidden_later).astype(jnp.bfloat16)
    query_mask = jnp.concatenate([query_mask] * per_group, axis=0)
    own_mask = jnp.where(lane - block == token, 1.0, 0.0).astype(jnp.bfloat16)

    def score(local):
        here = step * BLOCKS_PER_STEP + local
        pieces, masks = [], []
        for k in range(depth):
            rows = pl.ds(pl.multiple_of(slot_ref[here, k] * block, block), block)
            pieces.append(kv_scr[head, k, rows, :])
            unseen = (lane == 0) & (token >= cut_ref[here, k])
            masks.append(jnp.where(unseen, MASKED, 0.0).astype(jnp.bfloat16))
        rows = pl.ds(pl.multiple_of(here * block, block), block)
        pieces.append(kv_scr[head, depth, rows, :])
        masks.append(own_mask)
        every = jnp.concatenate(pieces, axis=0)
        keys = jnp.concatenate([every[:, :HEAD_DIM], jnp.concatenate(masks, axis=0)], axis=1)
        rows = slice(local * block, (local + 1) * block)
        queries = jnp.concatenate(
            [q_ref[rows, r * HEAD_DIM : (r + 1) * HEAD_DIM] for r in range(per_group)], axis=0
        )
        queries = jnp.concatenate([queries, query_mask], axis=1)
        scores = lax.dot_general(
            queries, keys, (((1,), (1,)), ((), ())), preferred_element_type=jnp.float32
        )
        return scores, every[:, HEAD_DIM:]

    def finish(local, scores, values):
        peak = jnp.max(scores, axis=-1, keepdims=True)
        weights = jnp.exp2((scores - peak) * scale).astype(jnp.bfloat16)
        padded = jnp.concatenate([values, jnp.ones_like(values)], axis=1)
        both = jnp.dot(weights, padded, preferred_element_type=jnp.float32)
        context = (both[:, :HEAD_DIM] * (1.0 / both[:, HEAD_DIM:])).astype(jnp.bfloat16)
        for r in range(per_group):
            out_ref[local * block : (local + 1) * block, r * HEAD_DIM : (r + 1) * HEAD_DIM] = context[
                r * block : (r + 1) * block
            ]

    waiting = None
    for local in range(BLOCKS_PER_STEP):
        scores, values = score(local)
        if waiting is not None:
            finish(*waiting)
        waiting = (local, scores, values)
    finish(*waiting)


def attention(slots, cuts, odd, queries, own, straight, crossed, unit, previous):
    rows, features = queries.shape
    blocks, depth = slots.shape
    block = rows // blocks
    wide = features // UNITS
    near = len(straight)
    held = pl.BlockSpec(memory_space=pltpu.HBM)
    kv_heads = own.shape[1] // (2 * HEAD_DIM)
    per_head = wide // kv_heads
    part = pl.BlockSpec(
        (BLOCKS_PER_STEP * block, per_head), lambda h, b, *_: (b, unit * kv_heads + h)
    )
    operands = [slots, cuts, odd, queries, own, *straight, *crossed]
    in_specs = [part] + [held] * (1 + near + len(crossed))
    aliases = {}
    if previous is not None:
        aliases = {len(operands): 0}
        operands.append(previous)
        in_specs.append(held)
    return pl.pallas_call(
        functools.partial(attention_kernel, block, near),
        grid_spec=pltpu.PrefetchScalarGridSpec(
            num_scalar_prefetch=3,
            grid=(kv_heads, blocks // BLOCKS_PER_STEP),
            in_specs=in_specs,
            out_specs=part,
            scratch_shapes=[
                pltpu.VMEM((kv_heads, depth + 1, rows, 2 * HEAD_DIM), own.dtype),
                pltpu.SemaphoreType.DMA((kv_heads, depth + 1)),
            ],
        ),
        out_shape=jax.ShapeDtypeStruct((rows, features), jnp.bfloat16),
        input_output_aliases=aliases,
        compiler_params=pltpu.CompilerParams(vmem_limit_bytes=57 * MIB),
        cost_estimate=pl.CostEstimate(
            flops=4 * rows * wide * (depth + 1) * block,
            bytes_accessed=8 * MIB,
            transcendentals=rows * wide // HEAD_DIM * (depth + 1) * block,
        ),
        name="attention",
    )(*operands)


def shards(hidden, queries, norm_gain, key_weight, value_weight, anc_ids, anc_cut):
    blocks, depth = anc_ids.shape
    levels = depth + 1
    size = lax.axis_size("node")
    chains = size // levels
    near = depth // 2
    half = [index // chains // 2 for index in range(size)]
    even = [index // chains % 2 == 0 for index in range(size)]
    other = [index + chains if even[index] else index - chains for index in range(size)]
    odd = (lax.axis_index("node") // chains % 2).astype(jnp.int32).reshape(1)
    slots = jnp.where(anc_ids >= 0, anc_ids % blocks, 0)

    normed, first = norm_project(hidden, norm_gain, key_weight, value_weight)
    own = [first] + [project(normed, key_weight, value_weight, unit) for unit in range(1, UNITS)]
    def after(array, *earlier):
        return lax.optimization_barrier((array, *earlier))[0]

    straight = [{} for _ in range(UNITS)]
    crossed = [{} for _ in range(UNITS)]

    def step_across(s, unit, settled):
        source = own[unit] if s == 0 else straight[unit][s]
        both_ways = unit == UNITS - 1 and s == 0
        pairs = [
            (i, other[i])
            for i in range(size)
            if half[i] >= s and (s > 0 or even[i] or (both_ways and half[i] == 0))
        ]
        crossed[unit][s] = lax.ppermute(after(source, *settled), "node", pairs)
        return crossed[unit][s]

    def step_along(s, unit, settled):
        source = own[unit] if s == 1 else straight[unit][s - 1]
        shift = 2 * chains
        pairs = [(i, i + shift) for i in range(size - shift) if half[i] >= s - 1]
        straight[unit][s] = lax.ppermute(after(source, *settled), "node", pairs)
        return straight[unit][s]

    def step_down(unit, settled):
        shift = 2 * near * chains
        pairs = [(i, i + shift) for i in range(size - shift)]
        crossed[unit][near] = lax.ppermute(after(crossed[unit][0], *settled), "node", pairs)
        return crossed[unit][near]

    early, late = range(UNITS)
    across = [(s, unit) for s in range(near - 1) for unit in (early, late)]
    across += [(near - 1, early), (near, early), (near - 1, late)]
    along = [(1, early), (1, late)]
    along += [(s, early) for s in range(2, near + 1)] + [(s, late) for s in range(2, near)]
    y_chain, z_chain = [], []
    for index, (s, unit) in enumerate(across):
        y_chain.append(step_across(s, unit, y_chain[-2:-1]))
        if index < len(along):
            z_chain.append(step_along(*along[index], z_chain[-2:-1]))
    step_down(late, [z_chain[-2], y_chain[-3]])
    step_along(near, late, [z_chain[-1]])
    result = None
    for unit in range(UNITS):
        result = attention(
            slots,
            anc_cut,
            odd,
            queries,
            own[unit],
            [straight[unit][s] for s in range(1, near + 1)],
            [crossed[unit][s] for s in range(near + 1)],
            unit,
            result,
        )
    return result


def solution(mesh):
    placed = (
        P(("groups", "node"), None),
        P(("groups", "node"), None),
        P(),
        P(),
        P(),
        P(("groups", "node"), None),
        P(("groups", "node"), None),
    )
    return jax.shard_map(
        shards, mesh=mesh, in_specs=placed, out_specs=P(("groups", "node"), None), check_vma=False
    )
```

```python
import functools
import jax
import jax.numpy as jnp
from jax import lax
from jax.experimental import pallas as pl
from jax.experimental.pallas import tpu as pltpu
from jax.sharding import PartitionSpec as P

HEAD_DIM = 128
EPS = 1e-05
LOG2E = 1.4426950408889634
MASKED = -1e30
MIB = 1024 * 1024
CHUNKS = 4
LOADS = 8
UNITS = 2


PLAN = (
    ("across", 0, 0, ()),
    ("along", 1, 0, ()),
    ("across", 0, 1, ()),
    ("along", 1, 1, ()),
    ("across", 1, 0, (("across", 0, 0),)),
    ("along", 2, 0, (("along", 1, 0),)),
    ("across", 1, 1, (("across", 0, 1),)),
    ("along", 3, 0, (("along", 1, 1),)),
    ("across", 2, 0, (("across", 1, 0),)),
    ("along", 2, 1, (("along", 2, 0),)),
    ("across", 3, 0, (("across", 1, 1),)),
    ("across", 2, 1, (("across", 2, 0),)),
    ("down", 3, 1, (("along", 3, 0), ("across", 2, 0))),
    ("along", 3, 1, (("along", 2, 1),)),
)


def norm_project_kernel(
    x_hbm, gain_ref, key_hbm, value_hbm, scale_ref, kv_ref,
    x_scr, weight_scr, even_scr, odd_scr, acc_scr, x_sem, key_sem, value_sem,
):
    loads, rows, chunk = x_scr.shape
    width = weight_scr.shape[2] // 2
    lanes = 128
    band = 128

    def span(c):
        return pl.ds(pl.multiple_of(c * chunk, chunk), chunk)

    def load_x(c):
        return pltpu.make_async_copy(x_hbm.at[:, span(c)], x_scr.at[c], x_sem.at[c])

    def load_weights(c):
        head = pl.ds(0, width)
        return [
            pltpu.make_async_copy(
                key_hbm.at[span(c), head], weight_scr.at[c, :, pl.ds(0, width)], key_sem.at[c]
            ),
            pltpu.make_async_copy(
                value_hbm.at[span(c), head], weight_scr.at[c, :, pl.ds(width, width)], value_sem.at[c]
            ),
        ]

    for c in range(loads):
        load_x(c).start()
    scale_ref[...] = jnp.zeros_like(scale_ref)

    def square(c, carry):
        load_x(c).wait()

        @pl.when(c >= loads // 2)
        def _():
            for part in range(2):
                for copy in load_weights(2 * (c - loads // 2) + part):
                    copy.start()

        for first in range(0, rows, band):
            row = slice(first, first + band)
            total = scale_ref[row, :]
            for lane in range(0, chunk, lanes):
                x = x_scr[c, row, lane : lane + lanes].astype(jnp.float32)
                total += x * x
            scale_ref[row, :] = total
        return carry

    lax.fori_loop(0, loads, square, 0)
    mean_sq = jnp.sum(scale_ref[...], axis=-1, keepdims=True) / (loads * chunk)
    scale_ref[...] = jnp.broadcast_to(lax.rsqrt(mean_sq + EPS), scale_ref.shape)

    def normalise(normed_scr, c):
        for first in range(0, rows, band):
            row = slice(first, first + band)
            inverse = scale_ref[row, :]
            for lane in range(0, chunk, lanes):
                cols = slice(lane, lane + lanes)
                x = x_scr[c, row, cols].astype(jnp.float32)
                gain = gain_ref[c, :, cols]
                normed_scr[row, cols] = (x * inverse * gain).astype(jnp.bfloat16)

    def multiply(normed_scr, c):
        for copy in load_weights(c):
            copy.wait()
        acc_scr[...] += jnp.dot(
            normed_scr[...], weight_scr[c], preferred_element_type=jnp.float32
        )

    normalise(even_scr, 0)
    acc_scr[...] = jnp.zeros_like(acc_scr)

    def pair(p, carry):
        multiply(even_scr, 2 * p)
        normalise(odd_scr, 2 * p + 1)
        multiply(odd_scr, 2 * p + 1)
        normalise(even_scr, 2 * p + 2)
        return carry

    lax.fori_loop(0, loads // 2 - 1, pair, 0)
    multiply(even_scr, loads - 2)
    normalise(odd_scr, loads - 1)
    multiply(odd_scr, loads - 1)
    write_heads(kv_ref, acc_scr)


def write_heads(kv_ref, acc_scr):
    width = kv_ref.shape[1] // 2
    for head in range(width // HEAD_DIM):
        for part in range(2):
            source = slice(part * width + head * HEAD_DIM, part * width + (head + 1) * HEAD_DIM)
            target = slice((2 * head + part) * HEAD_DIM, (2 * head + part + 1) * HEAD_DIM)
            kv_ref[:, target] = acc_scr[:, source].astype(jnp.bfloat16)


def norm_project(hidden, gain, key_weight, value_weight):
    rows, features = hidden.shape
    width = key_weight.shape[1] // UNITS
    chunk = features // LOADS
    whole = pl.BlockSpec(memory_space=pltpu.VMEM)
    held = pl.BlockSpec(memory_space=pltpu.HBM)
    return pl.pallas_call(
        norm_project_kernel,
        in_specs=[held, whole, held, held],
        out_specs=[whole, whole],
        out_shape=[
            jax.ShapeDtypeStruct((rows, 128), jnp.float32),
            jax.ShapeDtypeStruct((rows, 2 * width), jnp.bfloat16),
        ],
        scratch_shapes=[
            pltpu.VMEM((LOADS, rows, chunk), jnp.bfloat16),
            pltpu.VMEM((LOADS, chunk, 2 * width), jnp.bfloat16),
            pltpu.VMEM((rows, chunk), jnp.bfloat16),
            pltpu.VMEM((rows, chunk), jnp.bfloat16),
            pltpu.VMEM((rows, 2 * width), jnp.float32),
            pltpu.SemaphoreType.DMA((LOADS,)),
            pltpu.SemaphoreType.DMA((LOADS,)),
            pltpu.SemaphoreType.DMA((LOADS,)),
        ],
        compiler_params=pltpu.CompilerParams(vmem_limit_bytes=57 * MIB),
        cost_estimate=pl.CostEstimate(
            flops=4 * rows * features * width, bytes_accessed=16 * MIB, transcendentals=0
        ),
        name="norm_project",
    )(hidden, gain.reshape(LOADS, 1, chunk), key_weight, value_weight)


def project_kernel(x_ref, scale_ref, gain_ref, key_ref, value_ref, kv_ref, acc_scr):
    step = pl.program_id(0)
    rows, chunk = x_ref.shape
    width = key_ref.shape[1]
    lanes = 128
    inverse = scale_ref[...]
    parts = []
    for lane in range(0, chunk, lanes):
        cols = slice(lane, lane + lanes)
        x = x_ref[:, cols].astype(jnp.float32)
        parts.append((x * inverse * gain_ref[:, cols]).astype(jnp.bfloat16))
    normed = jnp.concatenate(parts, axis=1)
    for part, weight in enumerate((key_ref, value_ref)):
        cols = slice(part * width, (part + 1) * width)
        term = jnp.dot(normed, weight[...], preferred_element_type=jnp.float32)
        acc_scr[:, cols] = jnp.where(step == 0, term, acc_scr[:, cols] + term)

    @pl.when(step == CHUNKS - 1)
    def _():
        write_heads(kv_ref, acc_scr)


def project(hidden, scale, gain, key_weight, value_weight, unit):
    rows, features = hidden.shape
    chunk = features // CHUNKS
    width = key_weight.shape[1] // UNITS
    weight = pl.BlockSpec((chunk, width), lambda i: (i, unit))
    return pl.pallas_call(
        project_kernel,
        grid=(CHUNKS,),
        in_specs=[
            pl.BlockSpec((rows, chunk), lambda i: (0, i)),
            pl.BlockSpec(scale.shape, lambda i: (0, 0)),
            pl.BlockSpec((1, chunk), lambda i: (0, i)),
            weight,
            weight,
        ],
        out_specs=pl.BlockSpec((rows, 2 * width), lambda i: (0, 0)),
        out_shape=jax.ShapeDtypeStruct((rows, 2 * width), jnp.bfloat16),
        scratch_shapes=[pltpu.VMEM((rows, 2 * width), jnp.float32)],
        compiler_params=pltpu.CompilerParams(vmem_limit_bytes=57 * MIB),
        cost_estimate=pl.CostEstimate(
            flops=4 * rows * features * width, bytes_accessed=16 * MIB, transcendentals=0
        ),
        name="project",
    )(hidden, scale, gain.reshape(1, features), key_weight, value_weight)


def attention_kernel(block, unit, near, slot_ref, cut_ref, odd_ref, q_hbm, *refs):
    own_hbm, straight, crossed = refs[0], refs[1 : near + 1], refs[near + 1 : 2 * near + 2]
    out_hbm, kv_scr, q_scr, out_scr, even_scr, odd_scr, kv_sem, q_sem, out_sem = refs[-9:]
    kv_heads, levels, _, width = kv_scr.shape
    depth = levels - 1
    blocks, wide = q_scr.shape[0] // kv_heads, q_scr.shape[2]
    per_group = wide // HEAD_DIM
    items = kv_heads * blocks
    scale = HEAD_DIM**-0.5 * LOG2E

    def load_kv(head):
        def copy(ref, level, number):
            return pltpu.make_async_copy(
                ref.at[:, head * width : (head + 1) * width],
                kv_scr.at[head, level],
                kv_sem.at[head, number],
            )

        copies = [copy(own_hbm, depth, 0)]
        for s, ref in enumerate(straight):
            copies.append(copy(ref, 2 * s + 1, s + 1))
        for s, ref in enumerate(crossed):
            level = 2 * lax.rem(s + odd_ref[0] + near, near + 1)
            copies.append(copy(ref, level, near + s + 1))
        return copies

    def place(ref, item):
        head, here = lax.div(item, blocks), lax.rem(item, blocks)
        rows = pl.ds(pl.multiple_of(here * block, block), block)
        cols = pl.ds(pl.multiple_of((unit * kv_heads + head) * wide, wide), wide)
        return ref.at[rows, cols]

    def load_q(item):
        return pltpu.make_async_copy(place(q_hbm, item), q_scr.at[item], q_sem.at[item])

    def store(item):
        return pltpu.make_async_copy(out_scr.at[item], place(out_hbm, item), out_sem.at[item])

    for head in range(kv_heads):
        for copy in load_kv(head):
            copy.start()
        for item in range(head * blocks, (head + 1) * blocks):
            load_q(item).start()

    token = lax.broadcasted_iota(jnp.int32, (block, HEAD_DIM), 0)
    lane = lax.broadcasted_iota(jnp.int32, (block, HEAD_DIM), 1)
    hidden_later = jnp.where((lane >= block) & (lane - block > token), MASKED, 0.0)
    query_mask = jnp.where(lane == 0, 1.0, hidden_later).astype(jnp.bfloat16)
    query_mask = jnp.concatenate([query_mask] * per_group, axis=0)
    own_mask = jnp.where(lane - block == token, 1.0, 0.0).astype(jnp.bfloat16)

    def gather(item, cols):
        head, here = lax.div(item, blocks), lax.rem(item, blocks)
        pieces = []
        for k in range(levels):
            slot = slot_ref[here, k] if k < depth else here
            rows = pl.ds(pl.multiple_of(slot * block, block), block)
            pieces.append(kv_scr[head, k, rows, cols])
        return jnp.concatenate(pieces, axis=0)

    def score(item, score_scr):
        here = lax.rem(item, blocks)
        masks = []
        for k in range(depth):
            unseen = (lane == 0) & (token >= cut_ref[here, k])
            masks.append(jnp.where(unseen, MASKED, 0.0).astype(jnp.bfloat16))
        masks.append(own_mask)
        keys = jnp.concatenate(
            [gather(item, slice(0, HEAD_DIM)), jnp.concatenate(masks, axis=0)], axis=1
        )
        queries = jnp.concatenate(
            [q_scr[item, :, r * HEAD_DIM : (r + 1) * HEAD_DIM] for r in range(per_group)], axis=0
        )
        queries = jnp.concatenate([queries, query_mask], axis=1)
        score_scr[...] = lax.dot_general(
            queries, keys, (((1,), (1,)), ((), ())), preferred_element_type=jnp.float32
        )

    def finish(item, score_scr):
        scores = score_scr[...]
        peak = jnp.max(scores, axis=-1, keepdims=True)
        weights = jnp.exp2((scores - peak) * scale).astype(jnp.bfloat16)
        values = gather(item, slice(HEAD_DIM, 2 * HEAD_DIM))
        padded = jnp.concatenate([values, jnp.ones_like(values)], axis=1)
        both = jnp.dot(weights, padded, preferred_element_type=jnp.float32)
        context = (both[:, :HEAD_DIM] * (1.0 / both[:, HEAD_DIM:])).astype(jnp.bfloat16)
        for r in range(per_group):
            out_scr[item, :, r * HEAD_DIM : (r + 1) * HEAD_DIM] = context[
                r * block : (r + 1) * block
            ]

    def arrive(item):
        @pl.when(item < items)
        def _():
            load_q(item).wait()

        for head in range(1, kv_heads):

            @pl.when(item == head * blocks)
            def _(head=head):
                for copy in load_kv(head):
                    copy.wait()

    for copy in load_kv(0):
        copy.wait()
    load_q(0).wait()
    score(0, even_scr)

    def pair(j, carry):
        item = 2 * j
        arrive(item + 1)
        score(item + 1, odd_scr)
        finish(item, even_scr)
        store(item).start()
        arrive(item + 2)
        score(jnp.minimum(item + 2, items - 1), even_scr)
        finish(item + 1, odd_scr)
        store(item + 1).start()
        return carry

    lax.fori_loop(0, items // 2, pair, 0)
    for item in range(items):
        store(item).wait()


def attention(slots, cuts, odd, queries, own, straight, crossed, unit, previous):
    rows, features = queries.shape
    blocks, depth = slots.shape
    block = rows // blocks
    near = len(straight)
    kv_heads = own.shape[1] // (2 * HEAD_DIM)
    wide = features // UNITS // kv_heads
    keys = (depth + 1) * block
    tall = wide // HEAD_DIM * block
    items = kv_heads * blocks
    held = pl.BlockSpec(memory_space=pltpu.HBM)
    table = pl.BlockSpec(memory_space=pltpu.SMEM)
    operands = [slots, cuts, odd, queries, own, *straight, *crossed]
    aliases = {}
    if previous is not None:
        aliases = {len(operands): 0}
        operands.append(previous)
    return pl.pallas_call(
        functools.partial(attention_kernel, block, unit, near),
        in_specs=[table] * 3 + [held] * (len(operands) - 3),
        out_specs=held,
        out_shape=jax.ShapeDtypeStruct((rows, features), jnp.bfloat16),
        input_output_aliases=aliases,
        scratch_shapes=[
            pltpu.VMEM((kv_heads, depth + 1, rows, 2 * HEAD_DIM), own.dtype),
            pltpu.VMEM((items, block, wide), jnp.bfloat16),
            pltpu.VMEM((items, block, wide), jnp.bfloat16),
            pltpu.VMEM((tall, keys), jnp.float32),
            pltpu.VMEM((tall, keys), jnp.float32),
            pltpu.SemaphoreType.DMA((kv_heads, depth + 1)),
            pltpu.SemaphoreType.DMA((items,)),
            pltpu.SemaphoreType.DMA((items,)),
        ],
        compiler_params=pltpu.CompilerParams(vmem_limit_bytes=57 * MIB),
        cost_estimate=pl.CostEstimate(
            flops=4 * items * tall * keys * HEAD_DIM,
            bytes_accessed=8 * MIB,
            transcendentals=items * tall * keys,
        ),
        name="attention",
    )(*operands)


def shards(hidden, queries, norm_gain, key_weight, value_weight, anc_ids, anc_cut):
    blocks, depth = anc_ids.shape
    levels = depth + 1
    size = lax.axis_size("node")
    chains = size // levels
    near = depth // 2
    half = [index // chains // 2 for index in range(size)]
    even = [index // chains % 2 == 0 for index in range(size)]
    other = [index + chains if even[index] else index - chains for index in range(size)]
    odd = (lax.axis_index("node") // chains % 2).astype(jnp.int32).reshape(1)
    slots = jnp.where(anc_ids >= 0, anc_ids % blocks, 0)

    scale, first = norm_project(hidden, norm_gain, key_weight, value_weight)
    own = [first, project(hidden, scale, norm_gain, key_weight, value_weight, 1)]
    def after(array, *earlier):
        return lax.optimization_barrier((array, *earlier))[0]

    column = 2 * chains
    moved = {("own", 0, 0): own[0], ("own", 0, 1): own[1]}

    def step(kind, s, unit, waits):
        if kind == "across":
            source = ("along", s, unit) if s else ("own", 0, unit)
            exchange = s > 0 or unit == UNITS - 1
            pairs = [
                (i, other[i])
                for i in range(size)
                if half[i] >= s and (even[i] or (exchange and half[i] == 0) or s > 0)
            ]
        elif kind == "along":
            source = ("along", s - 1, unit) if s > 1 else ("own", 0, unit)
            pairs = [(i, i + column) for i in range(size - column) if half[i] >= s - 1]
        else:
            source = ("across" if kind == "down" else "own", 0, unit)
            pairs = [(i, i + s * column) for i in range(size - s * column)]
        array = lax.optimization_barrier((moved[source], *[moved[w] for w in waits]))[0]
        key = "along" if kind == "direct" else kind
        moved[key, s, unit] = lax.ppermute(array, "node", pairs)

    for kind, s, unit, waits in PLAN:
        step(kind, s, unit, waits)
    result = None
    for unit in range(UNITS):
        result = attention(
            slots,
            anc_cut,
            odd,
            queries,
            own[unit],
            [moved["along", s, unit] for s in range(1, near + 1)],
            [moved["across", s, unit] for s in range(near)]
            + [moved["across" if unit == 0 else "down", near, unit]],
            unit,
            result,
        )
    return result


def solution(mesh):
    placed = (
        P(("groups", "node"), None),
        P(("groups", "node"), None),
        P(),
        P(),
        P(),
        P(("groups", "node"), None),
        P(("groups", "node"), None),
    )
    return jax.shard_map(
        shards, mesh=mesh, in_specs=placed, out_specs=P(("groups", "node"), None), check_vma=False
    )
```

```python
import functools
import jax
import jax.numpy as jnp
from jax import lax
from jax.experimental import pallas as pl
from jax.experimental.pallas import tpu as pltpu
from jax.sharding import PartitionSpec as P

HEAD_DIM = 128
EPS = 1e-05
LOG2E = 1.4426950408889634
MASKED = -1e30
MIB = 1024 * 1024
CHUNKS = 4
LOADS = 8
UNITS = 2
BLOCKS_PER_STEP = 4


PLAN = (
    ("across", 0, 0, ()),
    ("along", 1, 0, ()),
    ("across", 0, 1, ()),
    ("along", 1, 1, (("across", 0, 0),)),
    ("along", 2, 0, (("across", 0, 0),)),
    ("across", 1, 0, ()),
    ("across", 1, 1, (("across", 1, 0),)),
    ("direct", 3, 0, (("across", 0, 0),)),
    ("across", 2, 0, (("across", 1, 0),)),
    ("along", 2, 1, (("across", 2, 0), ("across", 0, 1), ("along", 1, 1))),
    ("across", 3, 0, ()),
    ("across", 2, 1, (("along", 1, 1), ("across", 1, 1))),
    ("down", 3, 1, (("across", 0, 0),)),
    ("along", 3, 1, (("across", 0, 1),)),
)


def norm_project_kernel(
    x_hbm, gain_ref, key_hbm, value_hbm, scale_ref, kv_ref,
    x_scr, weight_scr, even_scr, odd_scr, acc_scr, x_sem, key_sem, value_sem,
):
    loads, rows, chunk = x_scr.shape
    width = weight_scr.shape[2] // 2
    lanes = 128
    band = 128

    def span(c):
        return pl.ds(pl.multiple_of(c * chunk, chunk), chunk)

    def load_x(c):
        return pltpu.make_async_copy(x_hbm.at[:, span(c)], x_scr.at[c], x_sem.at[c])

    def load_weights(c):
        head = pl.ds(0, width)
        return [
            pltpu.make_async_copy(
                key_hbm.at[span(c), head], weight_scr.at[c, :, pl.ds(0, width)], key_sem.at[c]
            ),
            pltpu.make_async_copy(
                value_hbm.at[span(c), head], weight_scr.at[c, :, pl.ds(width, width)], value_sem.at[c]
            ),
        ]

    for c in range(loads):
        load_x(c).start()
    scale_ref[...] = jnp.zeros_like(scale_ref)

    def square(c, carry):
        load_x(c).wait()

        @pl.when(c >= loads // 2)
        def _():
            for part in range(2):
                for copy in load_weights(2 * (c - loads // 2) + part):
                    copy.start()

        for first in range(0, rows, band):
            row = slice(first, first + band)
            total = scale_ref[row, :]
            for lane in range(0, chunk, lanes):
                x = x_scr[c, row, lane : lane + lanes].astype(jnp.float32)
                total += x * x
            scale_ref[row, :] = total
        return carry

    lax.fori_loop(0, loads, square, 0)
    mean_sq = jnp.sum(scale_ref[...], axis=-1, keepdims=True) / (loads * chunk)
    scale_ref[...] = jnp.broadcast_to(lax.rsqrt(mean_sq + EPS), scale_ref.shape)

    def normalise(normed_scr, c, first_lane=0, last_lane=chunk):
        for first in range(0, rows, band):
            row = slice(first, first + band)
            inverse = scale_ref[row, :]
            for lane in range(first_lane, last_lane, lanes):
                cols = slice(lane, lane + lanes)
                x = x_scr[c, row, cols].astype(jnp.float32)
                gain = gain_ref[c, :, cols]
                normed_scr[row, cols] = (x * inverse * gain).astype(jnp.bfloat16)

    def multiply(normed_scr, c, later_scr):
        for copy in load_weights(c):
            copy.wait()
        for part in range(2):
            cols = slice(part * width, (part + 1) * width)
            acc_scr[:, cols] += jnp.dot(
                normed_scr[...], weight_scr[c, :, cols], preferred_element_type=jnp.float32
            )
            if later_scr is not None:
                normalise(later_scr, c + 1, part * chunk // 2, (part + 1) * chunk // 2)

    normalise(even_scr, 0)
    acc_scr[...] = jnp.zeros_like(acc_scr)

    def pair(p, carry):
        multiply(even_scr, 2 * p, odd_scr)
        multiply(odd_scr, 2 * p + 1, even_scr)
        return carry

    lax.fori_loop(0, loads // 2 - 1, pair, 0)
    multiply(even_scr, loads - 2, odd_scr)
    multiply(odd_scr, loads - 1, None)
    write_heads(kv_ref, acc_scr)


def write_heads(kv_ref, acc_scr):
    width = kv_ref.shape[1] // 2
    for head in range(width // HEAD_DIM):
        for part in range(2):
            source = slice(part * width + head * HEAD_DIM, part * width + (head + 1) * HEAD_DIM)
            target = slice((2 * head + part) * HEAD_DIM, (2 * head + part + 1) * HEAD_DIM)
            kv_ref[:, target] = acc_scr[:, source].astype(jnp.bfloat16)


def norm_project(hidden, gain, key_weight, value_weight):
    rows, features = hidden.shape
    width = key_weight.shape[1] // UNITS
    chunk = features // LOADS
    whole = pl.BlockSpec(memory_space=pltpu.VMEM)
    held = pl.BlockSpec(memory_space=pltpu.HBM)
    return pl.pallas_call(
        norm_project_kernel,
        in_specs=[held, whole, held, held],
        out_specs=[whole, whole],
        out_shape=[
            jax.ShapeDtypeStruct((rows, 128), jnp.float32),
            jax.ShapeDtypeStruct((rows, 2 * width), jnp.bfloat16),
        ],
        scratch_shapes=[
            pltpu.VMEM((LOADS, rows, chunk), jnp.bfloat16),
            pltpu.VMEM((LOADS, chunk, 2 * width), jnp.bfloat16),
            pltpu.VMEM((rows, chunk), jnp.bfloat16),
            pltpu.VMEM((rows, chunk), jnp.bfloat16),
            pltpu.VMEM((rows, 2 * width), jnp.float32),
            pltpu.SemaphoreType.DMA((LOADS,)),
            pltpu.SemaphoreType.DMA((LOADS,)),
            pltpu.SemaphoreType.DMA((LOADS,)),
        ],
        compiler_params=pltpu.CompilerParams(vmem_limit_bytes=57 * MIB),
        cost_estimate=pl.CostEstimate(
            flops=4 * rows * features * width, bytes_accessed=16 * MIB, transcendentals=0
        ),
        name="norm_project",
    )(hidden, gain.reshape(LOADS, 1, chunk), key_weight, value_weight)


def project_kernel(x_ref, scale_ref, gain_ref, key_ref, value_ref, kv_ref, acc_scr):
    step = pl.program_id(0)
    rows, chunk = x_ref.shape
    width = key_ref.shape[1]
    lanes = 128
    inverse = scale_ref[...]
    parts = []
    for lane in range(0, chunk, lanes):
        cols = slice(lane, lane + lanes)
        x = x_ref[:, cols].astype(jnp.float32)
        parts.append((x * inverse * gain_ref[:, cols]).astype(jnp.bfloat16))
    normed = jnp.concatenate(parts, axis=1)
    for part, weight in enumerate((key_ref, value_ref)):
        cols = slice(part * width, (part + 1) * width)
        term = jnp.dot(normed, weight[...], preferred_element_type=jnp.float32)
        acc_scr[:, cols] = jnp.where(step == 0, term, acc_scr[:, cols] + term)

    @pl.when(step == CHUNKS - 1)
    def _():
        write_heads(kv_ref, acc_scr)


def project(hidden, scale, gain, key_weight, value_weight, unit):
    rows, features = hidden.shape
    chunk = features // CHUNKS
    width = key_weight.shape[1] // UNITS
    weight = pl.BlockSpec((chunk, width), lambda i: (i, unit))
    return pl.pallas_call(
        project_kernel,
        grid=(CHUNKS,),
        in_specs=[
            pl.BlockSpec((rows, chunk), lambda i: (0, i)),
            pl.BlockSpec(scale.shape, lambda i: (0, 0)),
            pl.BlockSpec((1, chunk), lambda i: (0, i)),
            weight,
            weight,
        ],
        out_specs=pl.BlockSpec((rows, 2 * width), lambda i: (0, 0)),
        out_shape=jax.ShapeDtypeStruct((rows, 2 * width), jnp.bfloat16),
        scratch_shapes=[pltpu.VMEM((rows, 2 * width), jnp.float32)],
        compiler_params=pltpu.CompilerParams(vmem_limit_bytes=57 * MIB),
        cost_estimate=pl.CostEstimate(
            flops=4 * rows * features * width, bytes_accessed=16 * MIB, transcendentals=0
        ),
        name="project",
    )(hidden, scale, gain.reshape(1, features), key_weight, value_weight)


def attention_kernel(block, near, slot_ref, cut_ref, odd_ref, q_ref, *refs):
    own_hbm, straight, crossed = refs[0], refs[1 : near + 1], refs[near + 1 : 2 * near + 2]
    out_ref, kv_scr, sems = refs[-3:]
    kv_heads, levels = kv_scr.shape[:2]
    depth = levels - 1
    width = kv_scr.shape[3]
    per_group = q_ref.shape[1] // HEAD_DIM
    head, step = pl.program_id(0), pl.program_id(1)
    scale = HEAD_DIM**-0.5 * LOG2E

    def fetch(index):
        def copy(ref, level, number):
            return pltpu.make_async_copy(
                ref.at[:, pl.ds(pl.multiple_of(index * width, width), width)],
                kv_scr.at[index, level],
                sems.at[index, number],
            )

        copies = [copy(own_hbm, depth, 0)]
        for s, ref in enumerate(straight):
            copies.append(copy(ref, 2 * s + 1, s + 1))
        for s, ref in enumerate(crossed):
            level = 2 * lax.rem(s + odd_ref[0] + near, near + 1)
            copies.append(copy(ref, level, near + s + 1))
        return copies

    @pl.when((head == 0) & (step == 0))
    def _():
        for index in range(kv_heads):
            for copy in fetch(index):
                copy.start()

    @pl.when(step == 0)
    def _():
        for copy in fetch(head):
            copy.wait()

    token = lax.broadcasted_iota(jnp.int32, (block, HEAD_DIM), 0)
    lane = lax.broadcasted_iota(jnp.int32, (block, HEAD_DIM), 1)
    hidden_later = jnp.where((lane >= block) & (lane - block > token), MASKED, 0.0)
    query_mask = jnp.where(lane == 0, 1.0, hidden_later).astype(jnp.bfloat16)
    query_mask = jnp.concatenate([query_mask] * per_group, axis=0)
    own_mask = jnp.where(lane - block == token, 1.0, 0.0).astype(jnp.bfloat16)

    def score(local):
        here = step * BLOCKS_PER_STEP + local
        pieces, masks = [], []
        for k in range(depth):
            rows = pl.ds(pl.multiple_of(slot_ref[here, k] * block, block), block)
            pieces.append(kv_scr[head, k, rows, :])
            unseen = (lane == 0) & (token >= cut_ref[here, k])
            masks.append(jnp.where(unseen, MASKED, 0.0).astype(jnp.bfloat16))
        rows = pl.ds(pl.multiple_of(here * block, block), block)
        pieces.append(kv_scr[head, depth, rows, :])
        masks.append(own_mask)
        every = jnp.concatenate(pieces, axis=0)
        keys = jnp.concatenate([every[:, :HEAD_DIM], jnp.concatenate(masks, axis=0)], axis=1)
        rows = slice(local * block, (local + 1) * block)
        queries = jnp.concatenate(
            [q_ref[rows, r * HEAD_DIM : (r + 1) * HEAD_DIM] for r in range(per_group)], axis=0
        )
        queries = jnp.concatenate([queries, query_mask], axis=1)
        scores = lax.dot_general(
            queries, keys, (((1,), (1,)), ((), ())), preferred_element_type=jnp.float32
        )
        return scores, every[:, HEAD_DIM:]

    def finish(local, scores, values):
        peak = jnp.max(scores, axis=-1, keepdims=True)
        weights = jnp.exp2((scores - peak) * scale).astype(jnp.bfloat16)
        padded = jnp.concatenate([values, jnp.ones_like(values)], axis=1)
        both = jnp.dot(weights, padded, preferred_element_type=jnp.float32)
        context = (both[:, :HEAD_DIM] * (1.0 / both[:, HEAD_DIM:])).astype(jnp.bfloat16)
        for r in range(per_group):
            out_ref[local * block : (local + 1) * block, r * HEAD_DIM : (r + 1) * HEAD_DIM] = context[
                r * block : (r + 1) * block
            ]

    waiting = []
    for local in range(BLOCKS_PER_STEP):
        waiting.append((local, *score(local)))
        if len(waiting) > 2:
            finish(*waiting.pop(0))
    for item in waiting:
        finish(*item)


def attention(slots, cuts, odd, queries, own, straight, crossed, unit, previous):
    rows, features = queries.shape
    blocks, depth = slots.shape
    block = rows // blocks
    wide = features // UNITS
    near = len(straight)
    held = pl.BlockSpec(memory_space=pltpu.HBM)
    kv_heads = own.shape[1] // (2 * HEAD_DIM)
    per_head = wide // kv_heads
    part = pl.BlockSpec(
        (BLOCKS_PER_STEP * block, per_head), lambda h, b, *_: (b, unit * kv_heads + h)
    )
    operands = [slots, cuts, odd, queries, own, *straight, *crossed]
    in_specs = [part] + [held] * (1 + near + len(crossed))
    aliases = {}
    if previous is not None:
        aliases = {len(operands): 0}
        operands.append(previous)
        in_specs.append(held)
    return pl.pallas_call(
        functools.partial(attention_kernel, block, near),
        grid_spec=pltpu.PrefetchScalarGridSpec(
            num_scalar_prefetch=3,
            grid=(kv_heads, blocks // BLOCKS_PER_STEP),
            in_specs=in_specs,
            out_specs=part,
            scratch_shapes=[
                pltpu.VMEM((kv_heads, depth + 1, rows, 2 * HEAD_DIM), own.dtype),
                pltpu.SemaphoreType.DMA((kv_heads, depth + 1)),
            ],
        ),
        out_shape=jax.ShapeDtypeStruct((rows, features), jnp.bfloat16),
        input_output_aliases=aliases,
        compiler_params=pltpu.CompilerParams(vmem_limit_bytes=57 * MIB),
        cost_estimate=pl.CostEstimate(
            flops=4 * rows * wide * (depth + 1) * block,
            bytes_accessed=8 * MIB,
            transcendentals=rows * wide // HEAD_DIM * (depth + 1) * block,
        ),
        name="attention",
    )(*operands)


def shards(hidden, queries, norm_gain, key_weight, value_weight, anc_ids, anc_cut):
    blocks, depth = anc_ids.shape
    levels = depth + 1
    size = lax.axis_size("node")
    chains = size // levels
    near = depth // 2
    half = [index // chains // 2 for index in range(size)]
    even = [index // chains % 2 == 0 for index in range(size)]
    other = [index + chains if even[index] else index - chains for index in range(size)]
    odd = (lax.axis_index("node") // chains % 2).astype(jnp.int32).reshape(1)
    slots = jnp.where(anc_ids >= 0, anc_ids % blocks, 0)

    scale, first = norm_project(hidden, norm_gain, key_weight, value_weight)
    own = [first, project(hidden, scale, norm_gain, key_weight, value_weight, 1)]
    def after(array, *earlier):
        return lax.optimization_barrier((array, *earlier))[0]

    column = 2 * chains
    moved = {("own", 0, 0): own[0], ("own", 0, 1): own[1]}

    def step(kind, s, unit, waits):
        if kind == "across":
            source = ("along", s, unit) if s else ("own", 0, unit)
            exchange = s > 0 or unit == UNITS - 1
            pairs = [
                (i, other[i])
                for i in range(size)
                if half[i] >= s and (even[i] or (exchange and half[i] == 0) or s > 0)
            ]
        elif kind == "along":
            source = ("along", s - 1, unit) if s > 1 else ("own", 0, unit)
            pairs = [(i, i + column) for i in range(size - column) if half[i] >= s - 1]
        else:
            source = ("across" if kind == "down" else "own", 0, unit)
            pairs = [(i, i + s * column) for i in range(size - s * column)]
        array = lax.optimization_barrier((moved[source], *[moved[w] for w in waits]))[0]
        key = "along" if kind == "direct" else kind
        moved[key, s, unit] = lax.ppermute(array, "node", pairs)

    for kind, s, unit, waits in PLAN:
        step(kind, s, unit, waits)
    result = None
    for unit in range(UNITS):
        result = attention(
            slots,
            anc_cut,
            odd,
            queries,
            own[unit],
            [moved["along", s, unit] for s in range(1, near + 1)],
            [moved["across", s, unit] for s in range(near)]
            + [moved["across" if unit == 0 else "down", near, unit]],
            unit,
            result,
        )
    return result


def solution(mesh):
    placed = (
        P(("groups", "node"), None),
        P(("groups", "node"), None),
        P(),
        P(),
        P(),
        P(("groups", "node"), None),
        P(("groups", "node"), None),
    )
    return jax.shard_map(
        shards, mesh=mesh, in_specs=placed, out_specs=P(("groups", "node"), None), check_vma=False
    )
```

```python
import functools
import jax
import jax.numpy as jnp
from jax import lax
from jax.experimental import pallas as pl
from jax.experimental.pallas import tpu as pltpu
from jax.sharding import PartitionSpec as P

HEAD_DIM = 128
EPS = 1e-05
LOG2E = 1.4426950408889634
MASKED = -1e30
MIB = 1024 * 1024
CHUNKS = 4
LOADS = 8
UNITS = 2
BLOCKS_PER_STEP = 4


PLAN = (
    ("across", 0, 0, ()),
    ("along", 1, 0, ()),
    ("across", 0, 1, ()),
    ("along", 1, 1, ()),
    ("across", 1, 0, (("across", 0, 0),)),
    ("along", 2, 0, (("along", 1, 0),)),
    ("across", 1, 1, (("across", 0, 1),)),
    ("along", 3, 0, (("along", 1, 1),)),
    ("across", 2, 0, (("across", 1, 0),)),
    ("along", 2, 1, (("along", 2, 0),)),
    ("across", 3, 0, (("across", 1, 1),)),
    ("across", 2, 1, (("across", 2, 0),)),
    ("along", 3, 1, (("along", 2, 1),)),
    ("down", 3, 1, (("along", 3, 0), ("across", 2, 0), ("along", 2, 1))),
)


def norm_project_kernel(
    x_hbm, gain_ref, key_hbm, value_hbm, scale_ref, kv_ref,
    x_scr, weight_scr, even_scr, odd_scr, acc_scr, x_sem, key_sem, value_sem,
):
    loads, rows, chunk = x_scr.shape
    width = weight_scr.shape[2] // 2
    lanes = 128
    band = 128

    def span(c):
        return pl.ds(pl.multiple_of(c * chunk, chunk), chunk)

    def load_x(c):
        return pltpu.make_async_copy(x_hbm.at[:, span(c)], x_scr.at[c], x_sem.at[c])

    def load_weights(c):
        head = pl.ds(0, width)
        return [
            pltpu.make_async_copy(
                key_hbm.at[span(c), head], weight_scr.at[c, :, pl.ds(0, width)], key_sem.at[c]
            ),
            pltpu.make_async_copy(
                value_hbm.at[span(c), head], weight_scr.at[c, :, pl.ds(width, width)], value_sem.at[c]
            ),
        ]

    for c in range(loads):
        load_x(c).start()
    scale_ref[...] = jnp.zeros_like(scale_ref)

    def square(c, carry):
        load_x(c).wait()

        @pl.when(c >= loads // 2)
        def _():
            for part in range(2):
                for copy in load_weights(2 * (c - loads // 2) + part):
                    copy.start()

        for first in range(0, rows, band):
            row = slice(first, first + band)
            total = scale_ref[row, :]
            for lane in range(0, chunk, lanes):
                x = x_scr[c, row, lane : lane + lanes].astype(jnp.float32)
                total += x * x
            scale_ref[row, :] = total
        return carry

    lax.fori_loop(0, loads, square, 0)
    mean_sq = jnp.sum(scale_ref[...], axis=-1, keepdims=True) / (loads * chunk)
    scale_ref[...] = jnp.broadcast_to(lax.rsqrt(mean_sq + EPS), scale_ref.shape)

    def normalise(normed_scr, c, first_lane=0, last_lane=chunk):
        for first in range(0, rows, band):
            row = slice(first, first + band)
            inverse = scale_ref[row, :]
            for lane in range(first_lane, last_lane, lanes):
                cols = slice(lane, lane + lanes)
                x = x_scr[c, row, cols].astype(jnp.float32)
                gain = gain_ref[c, :, cols]
                normed_scr[row, cols] = (x * inverse * gain).astype(jnp.bfloat16)

    def multiply(normed_scr, c, later_scr):
        for copy in load_weights(c):
            copy.wait()
        for part in range(2):
            cols = slice(part * width, (part + 1) * width)
            acc_scr[:, cols] += jnp.dot(
                normed_scr[...], weight_scr[c, :, cols], preferred_element_type=jnp.float32
            )
            if later_scr is not None:
                normalise(later_scr, c + 1, part * chunk // 2, (part + 1) * chunk // 2)

    normalise(even_scr, 0)
    acc_scr[...] = jnp.zeros_like(acc_scr)

    def pair(p, carry):
        multiply(even_scr, 2 * p, odd_scr)
        multiply(odd_scr, 2 * p + 1, even_scr)
        return carry

    lax.fori_loop(0, loads // 2 - 1, pair, 0)
    multiply(even_scr, loads - 2, odd_scr)
    multiply(odd_scr, loads - 1, None)
    write_heads(kv_ref, acc_scr)


def write_heads(kv_ref, acc_scr):
    width = kv_ref.shape[1] // 2
    for head in range(width // HEAD_DIM):
        for part in range(2):
            source = slice(part * width + head * HEAD_DIM, part * width + (head + 1) * HEAD_DIM)
            target = slice((2 * head + part) * HEAD_DIM, (2 * head + part + 1) * HEAD_DIM)
            kv_ref[:, target] = acc_scr[:, source].astype(jnp.bfloat16)


def norm_project(hidden, gain, key_weight, value_weight):
    rows, features = hidden.shape
    width = key_weight.shape[1] // UNITS
    chunk = features // LOADS
    whole = pl.BlockSpec(memory_space=pltpu.VMEM)
    held = pl.BlockSpec(memory_space=pltpu.HBM)
    return pl.pallas_call(
        norm_project_kernel,
        in_specs=[held, whole, held, held],
        out_specs=[whole, whole],
        out_shape=[
            jax.ShapeDtypeStruct((rows, 128), jnp.float32),
            jax.ShapeDtypeStruct((rows, 2 * width), jnp.bfloat16),
        ],
        scratch_shapes=[
            pltpu.VMEM((LOADS, rows, chunk), jnp.bfloat16),
            pltpu.VMEM((LOADS, chunk, 2 * width), jnp.bfloat16),
            pltpu.VMEM((rows, chunk), jnp.bfloat16),
            pltpu.VMEM((rows, chunk), jnp.bfloat16),
            pltpu.VMEM((rows, 2 * width), jnp.float32),
            pltpu.SemaphoreType.DMA((LOADS,)),
            pltpu.SemaphoreType.DMA((LOADS,)),
            pltpu.SemaphoreType.DMA((LOADS,)),
        ],
        compiler_params=pltpu.CompilerParams(vmem_limit_bytes=57 * MIB),
        cost_estimate=pl.CostEstimate(
            flops=4 * rows * features * width, bytes_accessed=16 * MIB, transcendentals=0
        ),
        name="norm_project",
    )(hidden, gain.reshape(LOADS, 1, chunk), key_weight, value_weight)


def project_kernel(x_ref, scale_ref, gain_ref, key_ref, value_ref, kv_ref, acc_scr):
    step = pl.program_id(0)
    rows, chunk = x_ref.shape
    width = key_ref.shape[1]
    lanes = 128
    inverse = scale_ref[...]
    parts = []
    for lane in range(0, chunk, lanes):
        cols = slice(lane, lane + lanes)
        x = x_ref[:, cols].astype(jnp.float32)
        parts.append((x * inverse * gain_ref[:, cols]).astype(jnp.bfloat16))
    normed = jnp.concatenate(parts, axis=1)
    for part, weight in enumerate((key_ref, value_ref)):
        cols = slice(part * width, (part + 1) * width)
        term = jnp.dot(normed, weight[...], preferred_element_type=jnp.float32)
        acc_scr[:, cols] = jnp.where(step == 0, term, acc_scr[:, cols] + term)

    @pl.when(step == CHUNKS - 1)
    def _():
        write_heads(kv_ref, acc_scr)


def project(hidden, scale, gain, key_weight, value_weight, unit):
    rows, features = hidden.shape
    chunk = features // CHUNKS
    width = key_weight.shape[1] // UNITS
    weight = pl.BlockSpec((chunk, width), lambda i: (i, unit))
    return pl.pallas_call(
        project_kernel,
        grid=(CHUNKS,),
        in_specs=[
            pl.BlockSpec((rows, chunk), lambda i: (0, i)),
            pl.BlockSpec(scale.shape, lambda i: (0, 0)),
            pl.BlockSpec((1, chunk), lambda i: (0, i)),
            weight,
            weight,
        ],
        out_specs=pl.BlockSpec((rows, 2 * width), lambda i: (0, 0)),
        out_shape=jax.ShapeDtypeStruct((rows, 2 * width), jnp.bfloat16),
        scratch_shapes=[pltpu.VMEM((rows, 2 * width), jnp.float32)],
        compiler_params=pltpu.CompilerParams(vmem_limit_bytes=57 * MIB),
        cost_estimate=pl.CostEstimate(
            flops=4 * rows * features * width, bytes_accessed=16 * MIB, transcendentals=0
        ),
        name="project",
    )(hidden, scale, gain.reshape(1, features), key_weight, value_weight)


def attention_kernel(block, near, first_head, slot_ref, cut_ref, odd_ref, q_ref, *refs):
    own_hbm, straight, crossed = refs[0], refs[1 : near + 1], refs[near + 1 : 2 * near + 2]
    out_ref, kv_scr, sems = refs[-3:]
    kv_heads, levels = kv_scr.shape[:2]
    depth = levels - 1
    width = kv_scr.shape[3]
    per_group = q_ref.shape[1] // HEAD_DIM
    head, step = pl.program_id(0), pl.program_id(1)
    scale = HEAD_DIM**-0.5 * LOG2E

    def fetch(index):
        def copy(ref, level, number):
            first = 0 if ref.shape[1] == width else (first_head + index) * width
            return pltpu.make_async_copy(
                ref.at[:, first : first + width], kv_scr.at[index, level], sems.at[index, number]
            )

        copies = [copy(own_hbm, depth, 0)]
        for s, ref in enumerate(straight):
            copies.append(copy(ref, 2 * s + 1, s + 1))
        for s, ref in enumerate(crossed):
            level = 2 * lax.rem(s + odd_ref[0] + near, near + 1)
            copies.append(copy(ref, level, near + s + 1))
        return copies

    @pl.when((head == 0) & (step == 0))
    def _():
        for index in range(kv_heads):
            for copy in fetch(index):
                copy.start()

    for index in range(kv_heads):

        @pl.when((head == index) & (step == 0))
        def _(index=index):
            for copy in fetch(index):
                copy.wait()

    token = lax.broadcasted_iota(jnp.int32, (block, HEAD_DIM), 0)
    lane = lax.broadcasted_iota(jnp.int32, (block, HEAD_DIM), 1)
    hidden_later = jnp.where((lane >= block) & (lane - block > token), MASKED, 0.0)
    query_mask = jnp.where(lane == 0, 1.0, hidden_later).astype(jnp.bfloat16)
    query_mask = jnp.concatenate([query_mask] * per_group, axis=0)
    own_mask = jnp.where(lane - block == token, 1.0, 0.0).astype(jnp.bfloat16)

    def score(local):
        here = step * BLOCKS_PER_STEP + local
        pieces, masks = [], []
        for k in range(depth):
            rows = pl.ds(pl.multiple_of(slot_ref[here, k] * block, block), block)
            pieces.append(kv_scr[head, k, rows, :])
            unseen = (lane == 0) & (token >= cut_ref[here, k])
            masks.append(jnp.where(unseen, MASKED, 0.0).astype(jnp.bfloat16))
        rows = pl.ds(pl.multiple_of(here * block, block), block)
        pieces.append(kv_scr[head, depth, rows, :])
        masks.append(own_mask)
        every = jnp.concatenate(pieces, axis=0)
        keys = jnp.concatenate([every[:, :HEAD_DIM], jnp.concatenate(masks, axis=0)], axis=1)
        rows = slice(local * block, (local + 1) * block)
        queries = jnp.concatenate(
            [q_ref[rows, r * HEAD_DIM : (r + 1) * HEAD_DIM] for r in range(per_group)], axis=0
        )
        queries = jnp.concatenate([queries, query_mask], axis=1)
        scores = lax.dot_general(
            queries, keys, (((1,), (1,)), ((), ())), preferred_element_type=jnp.float32
        )
        return scores, every[:, HEAD_DIM:]

    def finish(local, scores, values):
        peak = jnp.max(scores, axis=-1, keepdims=True)
        weights = jnp.exp2(((scores - peak) * scale).astype(jnp.bfloat16))
        padded = jnp.concatenate([values, jnp.ones_like(values)], axis=1)
        both = jnp.dot(weights, padded, preferred_element_type=jnp.float32)
        context = (both[:, :HEAD_DIM] * (1.0 / both[:, HEAD_DIM:])).astype(jnp.bfloat16)
        for r in range(per_group):
            out_ref[local * block : (local + 1) * block, r * HEAD_DIM : (r + 1) * HEAD_DIM] = context[
                r * block : (r + 1) * block
            ]

    waiting = []
    for local in range(BLOCKS_PER_STEP):
        waiting.append((local, *score(local)))
        if len(waiting) > 2:
            finish(*waiting.pop(0))
    for item in waiting:
        finish(*item)


def attention(slots, cuts, odd, queries, own, straight, crossed, unit, first_head, kv_heads, previous):
    rows, features = queries.shape
    blocks, depth = slots.shape
    block = rows // blocks
    near = len(straight)
    per_unit = own.shape[1] // (2 * HEAD_DIM)
    per_head = features // UNITS // per_unit
    first = unit * per_unit + first_head
    part = pl.BlockSpec((BLOCKS_PER_STEP * block, per_head), lambda h, b, *_: (b, first + h))
    held = pl.BlockSpec(memory_space=pltpu.HBM)
    operands = [slots, cuts, odd, queries, own, *straight, *crossed]
    in_specs = [part] + [held] * (len(operands) - 4)
    aliases = {}
    if previous is not None:
        aliases = {len(operands): 0}
        operands.append(previous)
        in_specs.append(held)
    return pl.pallas_call(
        functools.partial(attention_kernel, block, near, first_head),
        grid_spec=pltpu.PrefetchScalarGridSpec(
            num_scalar_prefetch=3,
            grid=(kv_heads, blocks // BLOCKS_PER_STEP),
            in_specs=in_specs,
            out_specs=part,
            scratch_shapes=[
                pltpu.VMEM((kv_heads, depth + 1, rows, 2 * HEAD_DIM), own.dtype),
                pltpu.SemaphoreType.DMA((kv_heads, depth + 1)),
            ],
        ),
        out_shape=jax.ShapeDtypeStruct((rows, features), jnp.bfloat16),
        input_output_aliases=aliases,
        compiler_params=pltpu.CompilerParams(vmem_limit_bytes=57 * MIB),
        cost_estimate=pl.CostEstimate(
            flops=4 * rows * kv_heads * per_head * (depth + 1) * block,
            bytes_accessed=4 * kv_heads * MIB,
            transcendentals=rows * kv_heads * per_head // HEAD_DIM * (depth + 1) * block,
        ),
        name="attention",
    )(*operands)


def shards(hidden, queries, norm_gain, key_weight, value_weight, anc_ids, anc_cut):
    blocks, depth = anc_ids.shape
    levels = depth + 1
    size = lax.axis_size("node")
    chains = size // levels
    near = depth // 2
    half = [index // chains // 2 for index in range(size)]
    even = [index // chains % 2 == 0 for index in range(size)]
    other = [index + chains if even[index] else index - chains for index in range(size)]
    odd = (lax.axis_index("node") // chains % 2).astype(jnp.int32).reshape(1)
    slots = jnp.where(anc_ids >= 0, anc_ids % blocks, 0)

    scale, first = norm_project(hidden, norm_gain, key_weight, value_weight)
    own = [first, project(hidden, scale, norm_gain, key_weight, value_weight, 1)]
    def after(array, *earlier):
        return lax.optimization_barrier((array, *earlier))[0]

    column = 2 * chains
    per_unit = key_weight.shape[1] // HEAD_DIM // UNITS
    width = 2 * HEAD_DIM
    moved = {("own", 0, 0): own[0], ("own", 0, 1): own[1]}

    def step(kind, s, unit, waits):
        if kind == "across":
            source = ("along", s, unit) if s else ("own", 0, unit)
            exchange = unit == UNITS - 1
            pairs = [
                (i, other[i])
                for i in range(size)
                if half[i] >= s and (s > 0 or even[i] or (exchange and half[i] == 0))
            ]
        elif kind == "along":
            source = ("along", s - 1, unit) if s > 1 else ("own", 0, unit)
            pairs = [(i, i + column) for i in range(size - column) if half[i] >= s - 1]
        else:
            source = ("across", 0, unit)
            pairs = [(i, i + s * column) for i in range(size - s * column)]
        array = lax.optimization_barrier((moved[source], *[moved[w] for w in waits]))[0]
        if unit == 1 and s == near:
            parts = [array[:, h * width : (h + 1) * width] for h in range(per_unit)]
        else:
            parts = [array]
        for h, part in enumerate(parts):
            moved[kind, s, unit, h] = lax.ppermute(part, "node", pairs)
        moved[kind, s, unit] = moved[kind, s, unit, 0]

    for kind, s, unit, waits in PLAN:
        step(kind, s, unit, waits)

    result = None
    for unit, first, count in ((0, 0, per_unit), *[(1, h, 1) for h in range(per_unit)]):
        far = "across" if unit == 0 else "down"
        result = attention(
            slots,
            anc_cut,
            odd,
            queries,
            own[unit],
            [moved["along", s, unit] for s in range(1, near)] + [moved["along", near, unit, first]],
            [moved["across", s, unit] for s in range(near)] + [moved[far, near, unit, first]],
            unit,
            first,
            count,
            result,
        )
    return result


def solution(mesh):
    placed = (
        P(("groups", "node"), None),
        P(("groups", "node"), None),
        P(),
        P(),
        P(),
        P(("groups", "node"), None),
        P(("groups", "node"), None),
    )
    return jax.shard_map(
        shards, mesh=mesh, in_specs=placed, out_specs=P(("groups", "node"), None), check_vma=False
    )
```

```python
import functools
import jax
import jax.numpy as jnp
from jax import lax
from jax.experimental import pallas as pl
from jax.experimental.pallas import tpu as pltpu
from jax.sharding import PartitionSpec as P

HEAD_DIM = 128
EPS = 1e-05
LOG2E = 1.4426950408889634
MASKED = -1e30
MIB = 1024 * 1024
CHUNKS = 4
LOADS = 8
UNITS = 2
BLOCKS_PER_STEP = 4


PLAN = (
    ("across", 0, 0, ()),
    ("along", 1, 0, ()),
    ("across", 0, 1, ()),
    ("along", 1, 1, ()),
    ("across", 1, 0, (("across", 0, 0),)),
    ("along", 2, 0, (("along", 1, 0),)),
    ("across", 1, 1, (("across", 0, 1),)),
    ("along", 3, 0, (("along", 1, 1),)),
    ("across", 2, 0, (("across", 1, 0),)),
    ("along", 2, 1, (("along", 2, 0),)),
    ("across", 3, 0, (("across", 1, 1),)),
    ("across", 2, 1, (("across", 2, 0),)),
    ("down", 3, 1, (("along", 3, 0), ("across", 2, 0))),
    ("along", 3, 1, (("along", 2, 1),)),
)


def norm_project_kernel(
    x_hbm, gain_ref, key_hbm, value_hbm, scale_ref, kv_ref,
    x_scr, weight_scr, even_scr, odd_scr, acc_scr, x_sem, key_sem, value_sem,
):
    loads, rows, chunk = x_scr.shape
    width = weight_scr.shape[2] // 2
    lanes = 128
    band = 128

    def span(c):
        return pl.ds(pl.multiple_of(c * chunk, chunk), chunk)

    def load_x(c):
        return pltpu.make_async_copy(x_hbm.at[:, span(c)], x_scr.at[c], x_sem.at[c])

    def load_weights(c):
        head = pl.ds(0, width)
        return [
            pltpu.make_async_copy(
                key_hbm.at[span(c), head], weight_scr.at[c, :, pl.ds(0, width)], key_sem.at[c]
            ),
            pltpu.make_async_copy(
                value_hbm.at[span(c), head], weight_scr.at[c, :, pl.ds(width, width)], value_sem.at[c]
            ),
        ]

    for c in range(loads):
        load_x(c).start()
    scale_ref[...] = jnp.zeros_like(scale_ref)

    def square(c, carry):
        load_x(c).wait()

        @pl.when(c >= loads // 2)
        def _():
            for part in range(2):
                for copy in load_weights(2 * (c - loads // 2) + part):
                    copy.start()

        for first in range(0, rows, band):
            row = slice(first, first + band)
            total = scale_ref[row, :]
            for lane in range(0, chunk, lanes):
                x = x_scr[c, row, lane : lane + lanes].astype(jnp.float32)
                total += x * x
            scale_ref[row, :] = total
        return carry

    lax.fori_loop(0, loads, square, 0)
    mean_sq = jnp.sum(scale_ref[...], axis=-1, keepdims=True) / (loads * chunk)
    scale_ref[...] = jnp.broadcast_to(lax.rsqrt(mean_sq + EPS), scale_ref.shape)

    def normalise(normed_scr, c):
        for first in range(0, rows, band):
            row = slice(first, first + band)
            inverse = scale_ref[row, :]
            for lane in range(0, chunk, lanes):
                cols = slice(lane, lane + lanes)
                x = x_scr[c, row, cols].astype(jnp.float32)
                gain = gain_ref[c, :, cols]
                normed_scr[row, cols] = (x * inverse * gain).astype(jnp.bfloat16)

    def multiply(normed_scr, c):
        for copy in load_weights(c):
            copy.wait()
        acc_scr[...] += jnp.dot(
            normed_scr[...], weight_scr[c], preferred_element_type=jnp.float32
        )

    normalise(even_scr, 0)
    acc_scr[...] = jnp.zeros_like(acc_scr)

    def pair(p, carry):
        multiply(even_scr, 2 * p)
        normalise(odd_scr, 2 * p + 1)
        multiply(odd_scr, 2 * p + 1)
        normalise(even_scr, 2 * p + 2)
        return carry

    lax.fori_loop(0, loads // 2 - 1, pair, 0)
    multiply(even_scr, loads - 2)
    normalise(odd_scr, loads - 1)
    multiply(odd_scr, loads - 1)
    write_heads(kv_ref, acc_scr)


def write_heads(kv_ref, acc_scr):
    width = kv_ref.shape[1] // 2
    for head in range(width // HEAD_DIM):
        for part in range(2):
            source = slice(part * width + head * HEAD_DIM, part * width + (head + 1) * HEAD_DIM)
            target = slice((2 * head + part) * HEAD_DIM, (2 * head + part + 1) * HEAD_DIM)
            kv_ref[:, target] = acc_scr[:, source].astype(jnp.bfloat16)


def norm_project(hidden, gain, key_weight, value_weight):
    rows, features = hidden.shape
    width = key_weight.shape[1] // UNITS
    chunk = features // LOADS
    whole = pl.BlockSpec(memory_space=pltpu.VMEM)
    held = pl.BlockSpec(memory_space=pltpu.HBM)
    return pl.pallas_call(
        norm_project_kernel,
        in_specs=[held, whole, held, held],
        out_specs=[whole, whole],
        out_shape=[
            jax.ShapeDtypeStruct((rows, 128), jnp.float32),
            jax.ShapeDtypeStruct((rows, 2 * width), jnp.bfloat16),
        ],
        scratch_shapes=[
            pltpu.VMEM((LOADS, rows, chunk), jnp.bfloat16),
            pltpu.VMEM((LOADS, chunk, 2 * width), jnp.bfloat16),
            pltpu.VMEM((rows, chunk), jnp.bfloat16),
            pltpu.VMEM((rows, chunk), jnp.bfloat16),
            pltpu.VMEM((rows, 2 * width), jnp.float32),
            pltpu.SemaphoreType.DMA((LOADS,)),
            pltpu.SemaphoreType.DMA((LOADS,)),
            pltpu.SemaphoreType.DMA((LOADS,)),
        ],
        compiler_params=pltpu.CompilerParams(vmem_limit_bytes=57 * MIB),
        cost_estimate=pl.CostEstimate(
            flops=4 * rows * features * width, bytes_accessed=16 * MIB, transcendentals=0
        ),
        name="norm_project",
    )(hidden, gain.reshape(LOADS, 1, chunk), key_weight, value_weight)


def project_kernel(x_ref, scale_ref, gain_ref, key_ref, value_ref, kv_ref, acc_scr):
    step = pl.program_id(0)
    rows, chunk = x_ref.shape
    width = key_ref.shape[1]
    lanes = 128
    inverse = scale_ref[...]
    parts = []
    for lane in range(0, chunk, lanes):
        cols = slice(lane, lane + lanes)
        x = x_ref[:, cols].astype(jnp.float32)
        parts.append((x * inverse * gain_ref[:, cols]).astype(jnp.bfloat16))
    normed = jnp.concatenate(parts, axis=1)
    for part, weight in enumerate((key_ref, value_ref)):
        cols = slice(part * width, (part + 1) * width)
        term = jnp.dot(normed, weight[...], preferred_element_type=jnp.float32)
        acc_scr[:, cols] = jnp.where(step == 0, term, acc_scr[:, cols] + term)

    @pl.when(step == CHUNKS - 1)
    def _():
        write_heads(kv_ref, acc_scr)


def project(hidden, scale, gain, key_weight, value_weight, unit):
    rows, features = hidden.shape
    chunk = features // CHUNKS
    width = key_weight.shape[1] // UNITS
    weight = pl.BlockSpec((chunk, width), lambda i: (i, unit))
    return pl.pallas_call(
        project_kernel,
        grid=(CHUNKS,),
        in_specs=[
            pl.BlockSpec((rows, chunk), lambda i: (0, i)),
            pl.BlockSpec(scale.shape, lambda i: (0, 0)),
            pl.BlockSpec((1, chunk), lambda i: (0, i)),
            weight,
            weight,
        ],
        out_specs=pl.BlockSpec((rows, 2 * width), lambda i: (0, 0)),
        out_shape=jax.ShapeDtypeStruct((rows, 2 * width), jnp.bfloat16),
        scratch_shapes=[pltpu.VMEM((rows, 2 * width), jnp.float32)],
        compiler_params=pltpu.CompilerParams(vmem_limit_bytes=57 * MIB),
        cost_estimate=pl.CostEstimate(
            flops=4 * rows * features * width, bytes_accessed=16 * MIB, transcendentals=0
        ),
        name="project",
    )(hidden, scale, gain.reshape(1, features), key_weight, value_weight)


def attention_kernel(block, unit, near, slot_ref, cut_ref, odd_ref, q_hbm, *refs):
    own_hbm, straight, crossed = refs[0], refs[1 : near + 1], refs[near + 1 : 2 * near + 2]
    out_hbm, kv_scr, q_scr, out_scr, kv_sem, q_sem, out_sem = refs[-7:]
    kv_heads, levels, rows, width = kv_scr.shape
    depth = levels - 1
    steps, tall, wide = q_scr.shape
    per_head = steps // kv_heads
    per_group = wide // HEAD_DIM
    scale = HEAD_DIM**-0.5 * LOG2E

    def load_kv(head):
        def copy(ref, level, number):
            return pltpu.make_async_copy(
                ref.at[:, head * width : (head + 1) * width],
                kv_scr.at[head, level],
                kv_sem.at[head, number],
            )

        copies = [copy(own_hbm, depth, 0)]
        for s, ref in enumerate(straight):
            copies.append(copy(ref, 2 * s + 1, s + 1))
        for s, ref in enumerate(crossed):
            level = 2 * lax.rem(s + odd_ref[0] + near, near + 1)
            copies.append(copy(ref, level, near + s + 1))
        return copies

    def place(ref, step):
        head, part = lax.div(step, per_head), lax.rem(step, per_head)
        span = pl.ds(pl.multiple_of(part * tall, tall), tall)
        cols = pl.ds(pl.multiple_of((unit * kv_heads + head) * wide, wide), wide)
        return ref.at[span, cols]

    def load_q(step):
        return pltpu.make_async_copy(place(q_hbm, step), q_scr.at[step], q_sem.at[step])

    def store(step):
        return pltpu.make_async_copy(out_scr.at[step], place(out_hbm, step), out_sem.at[step])

    for head in range(kv_heads):
        for copy in load_kv(head):
            copy.start()
        for step in range(head * per_head, (head + 1) * per_head):
            load_q(step).start()

    token = lax.broadcasted_iota(jnp.int32, (block, HEAD_DIM), 0)
    lane = lax.broadcasted_iota(jnp.int32, (block, HEAD_DIM), 1)
    hidden_later = jnp.where((lane >= block) & (lane - block > token), MASKED, 0.0)
    query_mask = jnp.where(lane == 0, 1.0, hidden_later).astype(jnp.bfloat16)
    query_mask = jnp.concatenate([query_mask] * per_group, axis=0)
    own_mask = jnp.where(lane - block == token, 1.0, 0.0).astype(jnp.bfloat16)

    def score(step, local):
        head = lax.div(step, per_head)
        here = lax.rem(step, per_head) * BLOCKS_PER_STEP + local
        pieces, masks = [], []
        for k in range(depth):
            span = pl.ds(pl.multiple_of(slot_ref[here, k] * block, block), block)
            pieces.append(kv_scr[head, k, span, :])
            unseen = (lane == 0) & (token >= cut_ref[here, k])
            masks.append(jnp.where(unseen, MASKED, 0.0).astype(jnp.bfloat16))
        span = pl.ds(pl.multiple_of(here * block, block), block)
        pieces.append(kv_scr[head, depth, span, :])
        masks.append(own_mask)
        every = jnp.concatenate(pieces, axis=0)
        keys = jnp.concatenate([every[:, :HEAD_DIM], jnp.concatenate(masks, axis=0)], axis=1)
        span = slice(local * block, (local + 1) * block)
        queries = jnp.concatenate(
            [q_scr[step, span, r * HEAD_DIM : (r + 1) * HEAD_DIM] for r in range(per_group)], axis=0
        )
        queries = jnp.concatenate([queries, query_mask], axis=1)
        scores = lax.dot_general(
            queries, keys, (((1,), (1,)), ((), ())), preferred_element_type=jnp.float32
        )
        return scores, every[:, HEAD_DIM:]

    def finish(step, local, scores, values):
        peak = jnp.max(scores, axis=-1, keepdims=True)
        weights = jnp.exp2((scores - peak) * scale).astype(jnp.bfloat16)
        padded = jnp.concatenate([values, jnp.ones_like(values)], axis=1)
        both = jnp.dot(weights, padded, preferred_element_type=jnp.float32)
        context = (both[:, :HEAD_DIM] * (1.0 / both[:, HEAD_DIM:])).astype(jnp.bfloat16)
        span = slice(local * block, (local + 1) * block)
        for r in range(per_group):
            out_scr[step, span, r * HEAD_DIM : (r + 1) * HEAD_DIM] = context[
                r * block : (r + 1) * block
            ]

    def body(step, carry):
        load_q(step).wait()
        for head in range(kv_heads):

            @pl.when(step == head * per_head)
            def _(head=head):
                for copy in load_kv(head):
                    copy.wait()

        waiting = None
        for local in range(BLOCKS_PER_STEP):
            scores, values = score(step, local)
            if waiting is not None:
                finish(step, *waiting)
            waiting = (local, scores, values)
        finish(step, *waiting)
        store(step).start()
        return carry

    lax.fori_loop(0, steps, body, 0)
    for step in range(steps):
        store(step).wait()


def attention(slots, cuts, odd, queries, own, straight, crossed, unit, previous):
    rows, features = queries.shape
    blocks, depth = slots.shape
    block = rows // blocks
    near = len(straight)
    kv_heads = own.shape[1] // (2 * HEAD_DIM)
    wide = features // UNITS // kv_heads
    steps = kv_heads * blocks // BLOCKS_PER_STEP
    held = pl.BlockSpec(memory_space=pltpu.HBM)
    table = pl.BlockSpec(memory_space=pltpu.SMEM)
    operands = [slots, cuts, odd, queries, own, *straight, *crossed]
    aliases = {}
    if previous is not None:
        aliases = {len(operands): 0}
        operands.append(previous)
    return pl.pallas_call(
        functools.partial(attention_kernel, block, unit, near),
        in_specs=[table] * 3 + [held] * (len(operands) - 3),
        out_specs=held,
        out_shape=jax.ShapeDtypeStruct((rows, features), jnp.bfloat16),
        input_output_aliases=aliases,
        scratch_shapes=[
            pltpu.VMEM((kv_heads, depth + 1, rows, 2 * HEAD_DIM), own.dtype),
            pltpu.VMEM((steps, BLOCKS_PER_STEP * block, wide), jnp.bfloat16),
            pltpu.VMEM((steps, BLOCKS_PER_STEP * block, wide), jnp.bfloat16),
            pltpu.SemaphoreType.DMA((kv_heads, depth + 1)),
            pltpu.SemaphoreType.DMA((steps,)),
            pltpu.SemaphoreType.DMA((steps,)),
        ],
        compiler_params=pltpu.CompilerParams(vmem_limit_bytes=57 * MIB),
        cost_estimate=pl.CostEstimate(
            flops=4 * rows * wide * kv_heads * (depth + 1) * block,
            bytes_accessed=8 * MIB,
            transcendentals=rows * wide // HEAD_DIM * kv_heads * (depth + 1) * block,
        ),
        name="attention",
    )(*operands)


def shards(hidden, queries, norm_gain, key_weight, value_weight, anc_ids, anc_cut):
    blocks, depth = anc_ids.shape
    levels = depth + 1
    size = lax.axis_size("node")
    chains = size // levels
    near = depth // 2
    half = [index // chains // 2 for index in range(size)]
    even = [index // chains % 2 == 0 for index in range(size)]
    other = [index + chains if even[index] else index - chains for index in range(size)]
    odd = (lax.axis_index("node") // chains % 2).astype(jnp.int32).reshape(1)
    slots = jnp.where(anc_ids >= 0, anc_ids % blocks, 0)

    scale, first = norm_project(hidden, norm_gain, key_weight, value_weight)
    own = [first, project(hidden, scale, norm_gain, key_weight, value_weight, 1)]
    def after(array, *earlier):
        return lax.optimization_barrier((array, *earlier))[0]

    column = 2 * chains
    moved = {("own", 0, 0): own[0], ("own", 0, 1): own[1]}

    def step(kind, s, unit, waits):
        if kind == "across":
            source = ("along", s, unit) if s else ("own", 0, unit)
            exchange = s > 0 or unit == UNITS - 1
            pairs = [
                (i, other[i])
                for i in range(size)
                if half[i] >= s and (even[i] or (exchange and half[i] == 0) or s > 0)
            ]
        elif kind == "along":
            source = ("along", s - 1, unit) if s > 1 else ("own", 0, unit)
            pairs = [(i, i + column) for i in range(size - column) if half[i] >= s - 1]
        else:
            source = ("across" if kind == "down" else "own", 0, unit)
            pairs = [(i, i + s * column) for i in range(size - s * column)]
        array = lax.optimization_barrier((moved[source], *[moved[w] for w in waits]))[0]
        key = "along" if kind == "direct" else kind
        moved[key, s, unit] = lax.ppermute(array, "node", pairs)

    for kind, s, unit, waits in PLAN:
        step(kind, s, unit, waits)
    result = None
    for unit in range(UNITS):
        result = attention(
            slots,
            anc_cut,
            odd,
            queries,
            own[unit],
            [moved["along", s, unit] for s in range(1, near + 1)],
            [moved["across", s, unit] for s in range(near)]
            + [moved["across" if unit == 0 else "down", near, unit]],
            unit,
            result,
        )
    return result


def solution(mesh):
    placed = (
        P(("groups", "node"), None),
        P(("groups", "node"), None),
        P(),
        P(),
        P(),
        P(("groups", "node"), None),
        P(("groups", "node"), None),
    )
    return jax.shard_map(
        shards, mesh=mesh, in_specs=placed, out_specs=P(("groups", "node"), None), check_vma=False
    )
```

```python
import functools
import jax
import jax.numpy as jnp
from jax import lax
from jax.experimental import pallas as pl
from jax.experimental.pallas import tpu as pltpu
from jax.sharding import PartitionSpec as P

HEAD_DIM = 128
EPS = 1e-05
LOG2E = 1.4426950408889634
MASKED = -1e30
MIB = 1024 * 1024
CHUNKS = 4
LOADS = 8
UNITS = 2
BLOCKS_PER_STEP = 4


PLAN = (
    ("across", 0, 0, ()),
    ("along", 1, 0, ()),
    ("across", 0, 1, ()),
    ("along", 1, 1, ()),
    ("across", 1, 0, (("across", 0, 0),)),
    ("along", 2, 0, (("along", 1, 0),)),
    ("across", 1, 1, (("across", 0, 1),)),
    ("along", 3, 0, (("along", 1, 1),)),
    ("across", 2, 0, (("across", 1, 0),)),
    ("along", 2, 1, (("along", 2, 0), ("across", 1, 0))),
    ("across", 3, 0, (("across", 1, 1),)),
    ("across", 2, 1, (("across", 2, 0),)),
    ("along", 3, 1, (("along", 2, 1),)),
    ("down", 3, 1, (("along", 3, 0), ("across", 2, 0), ("along", 2, 1))),
)


def norm_project_kernel(
    x_hbm, gain_ref, key_hbm, value_hbm, scale_ref, kv_ref,
    x_scr, weight_scr, even_scr, odd_scr, acc_scr, x_sem, key_sem, value_sem,
):
    loads, rows, piece = x_scr.shape
    chunks, chunk = weight_scr.shape[:2]
    width = weight_scr.shape[2] // 2
    lanes = 128
    band = 128

    def span(c):
        return pl.ds(pl.multiple_of(c * chunk, chunk), chunk)

    def load_x(c):
        cols = pl.ds(pl.multiple_of(c * piece, piece), piece)
        return pltpu.make_async_copy(x_hbm.at[:, cols], x_scr.at[c], x_sem.at[c])

    def load_weights(c):
        head = pl.ds(0, width)
        return [
            pltpu.make_async_copy(
                key_hbm.at[span(c), head], weight_scr.at[c, :, pl.ds(0, width)], key_sem.at[c]
            ),
            pltpu.make_async_copy(
                value_hbm.at[span(c), head], weight_scr.at[c, :, pl.ds(width, width)], value_sem.at[c]
            ),
        ]

    for c in range(loads):
        load_x(c).start()
    scale_ref[...] = jnp.zeros_like(scale_ref)

    def square(c, carry):
        load_x(c).wait()

        @pl.when(c == loads - 2)
        def _():
            for copy in load_weights(0):
                copy.start()

        for first in range(0, rows, band):
            row = slice(first, first + band)
            total = scale_ref[row, :]
            for lane in range(0, piece, lanes):
                x = x_scr[c, row, lane : lane + lanes].astype(jnp.float32)
                total += x * x
            scale_ref[row, :] = total
        return carry

    lax.fori_loop(0, loads, square, 0)
    for c in range(1, chunks):
        for copy in load_weights(c):
            copy.start()
    mean_sq = jnp.sum(scale_ref[...], axis=-1, keepdims=True) / (loads * piece)
    scale_ref[...] = jnp.broadcast_to(lax.rsqrt(mean_sq + EPS), scale_ref.shape)

    def normalise(normed_scr, c):
        for first in range(0, rows, band):
            row = slice(first, first + band)
            inverse = scale_ref[row, :]
            for lane in range(0, chunk, lanes):
                index, inner = c * (chunk // piece) + lane // piece, lane % piece
                x = x_scr[index, row, inner : inner + lanes].astype(jnp.float32)
                gain = gain_ref[index, :, inner : inner + lanes]
                normed_scr[row, lane : lane + lanes] = (x * inverse * gain).astype(jnp.bfloat16)

    def multiply(normed_scr, c):
        for copy in load_weights(c):
            copy.wait()
        return jnp.dot(normed_scr[...], weight_scr[c], preferred_element_type=jnp.float32)

    normalise(even_scr, 0)
    acc_scr[...] = multiply(even_scr, 0)
    normalise(odd_scr, 1)

    def pair(p, carry):
        acc_scr[...] += multiply(odd_scr, 2 * p + 1)
        normalise(even_scr, 2 * p + 2)
        acc_scr[...] += multiply(even_scr, 2 * p + 2)
        normalise(odd_scr, 2 * p + 3)
        return carry

    lax.fori_loop(0, chunks // 2 - 1, pair, 0)
    acc_scr[...] += multiply(odd_scr, chunks - 1)
    write_heads(kv_ref, acc_scr)


def write_heads(kv_ref, acc_scr):
    width = kv_ref.shape[1] // 2
    for head in range(width // HEAD_DIM):
        for part in range(2):
            source = slice(part * width + head * HEAD_DIM, part * width + (head + 1) * HEAD_DIM)
            target = slice((2 * head + part) * HEAD_DIM, (2 * head + part + 1) * HEAD_DIM)
            kv_ref[:, target] = acc_scr[:, source].astype(jnp.bfloat16)


def norm_project(hidden, gain, key_weight, value_weight):
    rows, features = hidden.shape
    width = key_weight.shape[1] // UNITS
    piece = features // LOADS
    chunk = features // CHUNKS
    whole = pl.BlockSpec(memory_space=pltpu.VMEM)
    held = pl.BlockSpec(memory_space=pltpu.HBM)
    return pl.pallas_call(
        norm_project_kernel,
        in_specs=[held, whole, held, held],
        out_specs=[whole, whole],
        out_shape=[
            jax.ShapeDtypeStruct((rows, 128), jnp.float32),
            jax.ShapeDtypeStruct((rows, 2 * width), jnp.bfloat16),
        ],
        scratch_shapes=[
            pltpu.VMEM((LOADS, rows, piece), jnp.bfloat16),
            pltpu.VMEM((CHUNKS, chunk, 2 * width), jnp.bfloat16),
            pltpu.VMEM((rows, chunk), jnp.bfloat16),
            pltpu.VMEM((rows, chunk), jnp.bfloat16),
            pltpu.VMEM((rows, 2 * width), jnp.float32),
            pltpu.SemaphoreType.DMA((LOADS,)),
            pltpu.SemaphoreType.DMA((CHUNKS,)),
            pltpu.SemaphoreType.DMA((CHUNKS,)),
        ],
        compiler_params=pltpu.CompilerParams(vmem_limit_bytes=57 * MIB),
        cost_estimate=pl.CostEstimate(
            flops=4 * rows * features * width, bytes_accessed=16 * MIB, transcendentals=0
        ),
        name="norm_project",
    )(hidden, gain.reshape(LOADS, 1, piece), key_weight, value_weight)


def project_kernel(x_ref, scale_ref, gain_ref, key_ref, value_ref, kv_ref, acc_scr):
    step = pl.program_id(0)
    rows, chunk = x_ref.shape
    width = key_ref.shape[1]
    lanes = 128
    inverse = scale_ref[...]
    parts = []
    for lane in range(0, chunk, lanes):
        cols = slice(lane, lane + lanes)
        x = x_ref[:, cols].astype(jnp.float32)
        parts.append((x * inverse * gain_ref[:, cols]).astype(jnp.bfloat16))
    normed = jnp.concatenate(parts, axis=1)
    for part, weight in enumerate((key_ref, value_ref)):
        cols = slice(part * width, (part + 1) * width)
        term = jnp.dot(normed, weight[...], preferred_element_type=jnp.float32)
        acc_scr[:, cols] = jnp.where(step == 0, term, acc_scr[:, cols] + term)

    @pl.when(step == CHUNKS - 1)
    def _():
        write_heads(kv_ref, acc_scr)


def project(hidden, scale, gain, key_weight, value_weight, unit):
    rows, features = hidden.shape
    chunk = features // CHUNKS
    width = key_weight.shape[1] // UNITS
    weight = pl.BlockSpec((chunk, width), lambda i: (i, unit))
    return pl.pallas_call(
        project_kernel,
        grid=(CHUNKS,),
        in_specs=[
            pl.BlockSpec((rows, chunk), lambda i: (0, i)),
            pl.BlockSpec(scale.shape, lambda i: (0, 0)),
            pl.BlockSpec((1, chunk), lambda i: (0, i)),
            weight,
            weight,
        ],
        out_specs=pl.BlockSpec((rows, 2 * width), lambda i: (0, 0)),
        out_shape=jax.ShapeDtypeStruct((rows, 2 * width), jnp.bfloat16),
        scratch_shapes=[pltpu.VMEM((rows, 2 * width), jnp.float32)],
        compiler_params=pltpu.CompilerParams(vmem_limit_bytes=57 * MIB),
        cost_estimate=pl.CostEstimate(
            flops=4 * rows * features * width, bytes_accessed=16 * MIB, transcendentals=0
        ),
        name="project",
    )(hidden, scale, gain.reshape(1, features), key_weight, value_weight)


def attention_kernel(block, head_from, near, skip, slot_ref, cut_ref, odd_ref, q_hbm, *refs):
    own_hbm, straight, crossed = refs[0], refs[1 : near + 1], refs[near + 1 : 2 * near + 2]
    out_hbm, kv_scr, q_scr, out_scr, kv_sem, q_sem, out_sem = refs[-7:]
    kv_heads, levels, rows, width = kv_scr.shape
    depth = levels - 1
    steps, tall, wide = q_scr.shape
    per_head = steps // kv_heads
    per_group = wide // HEAD_DIM
    scale = HEAD_DIM**-0.5 * LOG2E

    def load_kv(head):
        def copy(ref, level, number):
            first = 0 if ref.shape[1] == width else (skip + head) * width
            return pltpu.make_async_copy(
                ref.at[:, first : first + width], kv_scr.at[head, level], kv_sem.at[head, number]
            )

        copies = [copy(own_hbm, depth, 0)]
        for s, ref in enumerate(straight):
            copies.append(copy(ref, 2 * s + 1, s + 1))
        for s, ref in enumerate(crossed):
            level = 2 * lax.rem(s + odd_ref[0] + near, near + 1)
            copies.append(copy(ref, level, near + s + 1))
        return copies

    def place(ref, step):
        head, part = lax.div(step, per_head), lax.rem(step, per_head)
        span = pl.ds(pl.multiple_of(part * tall, tall), tall)
        cols = pl.ds(pl.multiple_of((head_from + head) * wide, wide), wide)
        return ref.at[span, cols]

    def load_q(step):
        return pltpu.make_async_copy(place(q_hbm, step), q_scr.at[step], q_sem.at[step])

    def store(step):
        return pltpu.make_async_copy(out_scr.at[step], place(out_hbm, step), out_sem.at[step])

    for head in range(kv_heads):
        for copy in load_kv(head):
            copy.start()
        for step in range(head * per_head, (head + 1) * per_head):
            load_q(step).start()

    token = lax.broadcasted_iota(jnp.int32, (block, HEAD_DIM), 0)
    lane = lax.broadcasted_iota(jnp.int32, (block, HEAD_DIM), 1)
    hidden_later = jnp.where((lane >= block) & (lane - block > token), MASKED, 0.0)
    query_mask = jnp.where(lane == 0, 1.0, hidden_later).astype(jnp.bfloat16)
    query_mask = jnp.concatenate([query_mask] * per_group, axis=0)
    own_mask = jnp.where(lane - block == token, 1.0, 0.0).astype(jnp.bfloat16)

    def score(step, local):
        head = lax.div(step, per_head)
        here = lax.rem(step, per_head) * BLOCKS_PER_STEP + local
        pieces, masks = [], []
        for k in range(depth):
            span = pl.ds(pl.multiple_of(slot_ref[here, k] * block, block), block)
            pieces.append(kv_scr[head, k, span, :])
            unseen = (lane == 0) & (token >= cut_ref[here, k])
            masks.append(jnp.where(unseen, MASKED, 0.0).astype(jnp.bfloat16))
        span = pl.ds(pl.multiple_of(here * block, block), block)
        pieces.append(kv_scr[head, depth, span, :])
        masks.append(own_mask)
        every = jnp.concatenate(pieces, axis=0)
        keys = jnp.concatenate([every[:, :HEAD_DIM], jnp.concatenate(masks, axis=0)], axis=1)
        span = slice(local * block, (local + 1) * block)
        queries = jnp.concatenate(
            [q_scr[step, span, r * HEAD_DIM : (r + 1) * HEAD_DIM] for r in range(per_group)], axis=0
        )
        queries = jnp.concatenate([queries, query_mask], axis=1)
        scores = lax.dot_general(
            queries, keys, (((1,), (1,)), ((), ())), preferred_element_type=jnp.float32
        )
        return scores, every[:, HEAD_DIM:]

    def finish(step, local, scores, values):
        peak = jnp.max(scores, axis=-1, keepdims=True)
        weights = jnp.exp2((scores - peak) * scale).astype(jnp.bfloat16)
        padded = jnp.concatenate([values, jnp.ones_like(values)], axis=1)
        both = jnp.dot(weights, padded, preferred_element_type=jnp.float32)
        context = (both[:, :HEAD_DIM] * (1.0 / both[:, HEAD_DIM:])).astype(jnp.bfloat16)
        span = slice(local * block, (local + 1) * block)
        for r in range(per_group):
            out_scr[step, span, r * HEAD_DIM : (r + 1) * HEAD_DIM] = context[
                r * block : (r + 1) * block
            ]

    def body(step, carry):
        load_q(step).wait()
        for head in range(kv_heads):

            @pl.when(step == head * per_head)
            def _(head=head):
                for copy in load_kv(head):
                    copy.wait()

        waiting = None
        for local in range(BLOCKS_PER_STEP):
            scores, values = score(step, local)
            if waiting is not None:
                finish(step, *waiting)
            waiting = (local, scores, values)
        finish(step, *waiting)
        store(step).start()
        return carry

    lax.fori_loop(0, steps, body, 0)
    for step in range(steps):
        store(step).wait()


def attention(slots, cuts, odd, queries, own, straight, crossed, unit, skip, kv_heads, previous):
    rows, features = queries.shape
    blocks, depth = slots.shape
    block = rows // blocks
    near = len(straight)
    per_unit = own.shape[1] // (2 * HEAD_DIM)
    wide = features // UNITS // per_unit
    steps = kv_heads * blocks // BLOCKS_PER_STEP
    held = pl.BlockSpec(memory_space=pltpu.HBM)
    table = pl.BlockSpec(memory_space=pltpu.SMEM)
    operands = [slots, cuts, odd, queries, own, *straight, *crossed]
    aliases = {}
    if previous is not None:
        aliases = {len(operands): 0}
        operands.append(previous)
    return pl.pallas_call(
        functools.partial(attention_kernel, block, unit * per_unit + skip, near, skip),
        in_specs=[table] * 3 + [held] * (len(operands) - 3),
        out_specs=held,
        out_shape=jax.ShapeDtypeStruct((rows, features), jnp.bfloat16),
        input_output_aliases=aliases,
        scratch_shapes=[
            pltpu.VMEM((kv_heads, depth + 1, rows, 2 * HEAD_DIM), own.dtype),
            pltpu.VMEM((steps, BLOCKS_PER_STEP * block, wide), jnp.bfloat16),
            pltpu.VMEM((steps, BLOCKS_PER_STEP * block, wide), jnp.bfloat16),
            pltpu.SemaphoreType.DMA((kv_heads, depth + 1)),
            pltpu.SemaphoreType.DMA((steps,)),
            pltpu.SemaphoreType.DMA((steps,)),
        ],
        compiler_params=pltpu.CompilerParams(vmem_limit_bytes=57 * MIB),
        cost_estimate=pl.CostEstimate(
            flops=4 * rows * wide * kv_heads * (depth + 1) * block,
            bytes_accessed=4 * kv_heads * MIB,
            transcendentals=rows * wide // HEAD_DIM * kv_heads * (depth + 1) * block,
        ),
        name="attention",
    )(*operands)


def shards(hidden, queries, norm_gain, key_weight, value_weight, anc_ids, anc_cut):
    blocks, depth = anc_ids.shape
    levels = depth + 1
    size = lax.axis_size("node")
    chains = size // levels
    near = depth // 2
    half = [index // chains // 2 for index in range(size)]
    even = [index // chains % 2 == 0 for index in range(size)]
    other = [index + chains if even[index] else index - chains for index in range(size)]
    odd = (lax.axis_index("node") // chains % 2).astype(jnp.int32).reshape(1)
    slots = jnp.where(anc_ids >= 0, anc_ids % blocks, 0)

    scale, first = norm_project(hidden, norm_gain, key_weight, value_weight)
    own = [first, project(hidden, scale, norm_gain, key_weight, value_weight, 1)]
    def after(array, *earlier):
        return lax.optimization_barrier((array, *earlier))[0]

    column = 2 * chains
    per_unit = key_weight.shape[1] // HEAD_DIM // UNITS
    width = 2 * HEAD_DIM
    moved = {("own", 0, 0): own[0], ("own", 0, 1): own[1]}

    def step(kind, s, unit, waits):
        if kind == "across":
            source = ("along", s, unit) if s else ("own", 0, unit)
            exchange = unit == UNITS - 1
            pairs = [
                (i, other[i])
                for i in range(size)
                if half[i] >= s and (s > 0 or even[i] or (exchange and half[i] == 0))
            ]
        elif kind == "along":
            source = ("along", s - 1, unit) if s > 1 else ("own", 0, unit)
            pairs = [(i, i + column) for i in range(size - column) if half[i] >= s - 1]
        else:
            source = ("across", 0, unit)
            pairs = [(i, i + s * column) for i in range(size - s * column)]
        array = lax.optimization_barrier((moved[source], *[moved[w] for w in waits]))[0]
        if unit == 1 and s == near:
            parts = [array[:, h * width : (h + 1) * width] for h in range(per_unit)]
        else:
            parts = [array]
        for h, part in enumerate(parts):
            moved[kind, s, unit, h] = lax.ppermute(part, "node", pairs)
        moved[kind, s, unit] = moved[kind, s, unit, 0]

    for kind, s, unit, waits in PLAN:
        step(kind, s, unit, waits)

    result = None
    for unit, first, count in ((0, 0, per_unit), *[(1, h, 1) for h in range(per_unit)]):
        far = "across" if unit == 0 else "down"
        result = attention(
            slots,
            anc_cut,
            odd,
            queries,
            own[unit],
            [moved["along", s, unit] for s in range(1, near)] + [moved["along", near, unit, first]],
            [moved["across", s, unit] for s in range(near)] + [moved[far, near, unit, first]],
            unit,
            first,
            count,
            result,
        )
    return result


def solution(mesh):
    placed = (
        P(("groups", "node"), None),
        P(("groups", "node"), None),
        P(),
        P(),
        P(),
        P(("groups", "node"), None),
        P(("groups", "node"), None),
    )
    return jax.shard_map(
        shards, mesh=mesh, in_specs=placed, out_specs=P(("groups", "node"), None), check_vma=False
    )
```

```python
import functools
import jax
import jax.numpy as jnp
from jax import lax
from jax.experimental import pallas as pl
from jax.experimental.pallas import tpu as pltpu
from jax.sharding import PartitionSpec as P

HEAD_DIM = 128
EPS = 1e-05
LOG2E = 1.4426950408889634
MASKED = -1e30
MIB = 1024 * 1024
CHUNKS = 4
LOADS = 8
UNITS = 2
BLOCKS_PER_STEP = 4


PLAN = (
    ("across", 0, 0, ()),
    ("along", 1, 0, ()),
    ("across", 0, 1, ()),
    ("along", 1, 1, ()),
    ("across", 1, 0, (("across", 0, 0),)),
    ("along", 2, 0, (("along", 1, 0),)),
    ("across", 1, 1, (("across", 0, 1),)),
    ("along", 3, 0, (("along", 1, 1),)),
    ("across", 2, 0, (("across", 1, 0),)),
    ("along", 2, 1, (("along", 2, 0),)),
    ("across", 3, 0, (("across", 1, 1),)),
    ("across", 2, 1, (("across", 2, 0),)),
    ("down", 3, 1, (("along", 3, 0), ("across", 2, 0))),
    ("along", 3, 1, (("along", 2, 1),)),
)


def norm_project_kernel(
    x_hbm, gain_ref, key_hbm, value_hbm, scale_ref, kv_ref,
    x_scr, weight_scr, even_scr, odd_scr, acc_scr, x_sem, key_sem, value_sem,
):
    rows, features = x_scr.shape
    loads = LOADS
    tall = rows // loads
    chunks, chunk = weight_scr.shape[:2]
    width = weight_scr.shape[2] // 2
    lanes = 128
    band = 128

    def span(c):
        return pl.ds(pl.multiple_of(c * chunk, chunk), chunk)

    def load_x(c):
        row = pl.ds(pl.multiple_of(c * tall, tall), tall)
        return pltpu.make_async_copy(x_hbm.at[row], x_scr.at[row], x_sem.at[c])

    def load_weights(c):
        head = pl.ds(0, width)
        return [
            pltpu.make_async_copy(
                key_hbm.at[span(c), head], weight_scr.at[c, :, pl.ds(0, width)], key_sem.at[c]
            ),
            pltpu.make_async_copy(
                value_hbm.at[span(c), head], weight_scr.at[c, :, pl.ds(width, width)], value_sem.at[c]
            ),
        ]

    for c in range(loads):
        load_x(c).start()

    def square(c, carry):
        load_x(c).wait()

        @pl.when(c == loads - 2)
        def _():
            for copy in load_weights(0):
                copy.start()

        row = pl.ds(pl.multiple_of(c * tall, tall), tall)
        total = jnp.zeros((tall, lanes), jnp.float32)
        for lane in range(0, features, lanes):
            x = x_scr[row, lane : lane + lanes].astype(jnp.float32)
            total += x * x
        scale_ref[row, :] = total
        return carry

    lax.fori_loop(0, loads, square, 0)
    for c in range(1, chunks):
        for copy in load_weights(c):
            copy.start()
    mean_sq = jnp.sum(scale_ref[...], axis=-1, keepdims=True) / features
    scale_ref[...] = jnp.broadcast_to(lax.rsqrt(mean_sq + EPS), scale_ref.shape)

    def normalise(normed_scr, c):
        for first in range(0, rows, band):
            row = slice(first, first + band)
            inverse = scale_ref[row, :]
            for lane in range(0, chunk, lanes):
                cols = pl.ds(pl.multiple_of(c * chunk + lane, lanes), lanes)
                x = x_scr[row, cols].astype(jnp.float32)
                normed_scr[row, lane : lane + lanes] = (
                    x * inverse * gain_ref[:, cols]
                ).astype(jnp.bfloat16)

    def multiply(normed_scr, c):
        for copy in load_weights(c):
            copy.wait()
        return jnp.dot(normed_scr[...], weight_scr[c], preferred_element_type=jnp.float32)

    normalise(even_scr, 0)
    acc_scr[...] = multiply(even_scr, 0)
    normalise(odd_scr, 1)

    def pair(p, carry):
        acc_scr[...] += multiply(odd_scr, 2 * p + 1)
        normalise(even_scr, 2 * p + 2)
        acc_scr[...] += multiply(even_scr, 2 * p + 2)
        normalise(odd_scr, 2 * p + 3)
        return carry

    lax.fori_loop(0, chunks // 2 - 1, pair, 0)
    acc_scr[...] += multiply(odd_scr, chunks - 1)
    write_heads(kv_ref, acc_scr)


def write_heads(kv_ref, acc_scr):
    width = kv_ref.shape[1] // 2
    for head in range(width // HEAD_DIM):
        for part in range(2):
            source = slice(part * width + head * HEAD_DIM, part * width + (head + 1) * HEAD_DIM)
            target = slice((2 * head + part) * HEAD_DIM, (2 * head + part + 1) * HEAD_DIM)
            kv_ref[:, target] = acc_scr[:, source].astype(jnp.bfloat16)


def norm_project(hidden, gain, key_weight, value_weight):
    rows, features = hidden.shape
    width = key_weight.shape[1] // UNITS
    chunk = features // CHUNKS
    whole = pl.BlockSpec(memory_space=pltpu.VMEM)
    held = pl.BlockSpec(memory_space=pltpu.HBM)
    return pl.pallas_call(
        norm_project_kernel,
        in_specs=[held, whole, held, held],
        out_specs=[whole, whole],
        out_shape=[
            jax.ShapeDtypeStruct((rows, 128), jnp.float32),
            jax.ShapeDtypeStruct((rows, 2 * width), jnp.bfloat16),
        ],
        scratch_shapes=[
            pltpu.VMEM((rows, features), jnp.bfloat16),
            pltpu.VMEM((CHUNKS, chunk, 2 * width), jnp.bfloat16),
            pltpu.VMEM((rows, chunk), jnp.bfloat16),
            pltpu.VMEM((rows, chunk), jnp.bfloat16),
            pltpu.VMEM((rows, 2 * width), jnp.float32),
            pltpu.SemaphoreType.DMA((LOADS,)),
            pltpu.SemaphoreType.DMA((CHUNKS,)),
            pltpu.SemaphoreType.DMA((CHUNKS,)),
        ],
        compiler_params=pltpu.CompilerParams(vmem_limit_bytes=57 * MIB),
        cost_estimate=pl.CostEstimate(
            flops=4 * rows * features * width, bytes_accessed=16 * MIB, transcendentals=0
        ),
        name="norm_project",
    )(hidden, gain.reshape(1, features), key_weight, value_weight)


def project_kernel(x_ref, scale_ref, gain_ref, key_ref, value_ref, kv_ref, acc_scr):
    step = pl.program_id(0)
    rows, chunk = x_ref.shape
    width = key_ref.shape[1]
    lanes = 128
    inverse = scale_ref[...]
    parts = []
    for lane in range(0, chunk, lanes):
        cols = slice(lane, lane + lanes)
        x = x_ref[:, cols].astype(jnp.float32)
        parts.append((x * inverse * gain_ref[:, cols]).astype(jnp.bfloat16))
    normed = jnp.concatenate(parts, axis=1)
    for part, weight in enumerate((key_ref, value_ref)):
        cols = slice(part * width, (part + 1) * width)
        term = jnp.dot(normed, weight[...], preferred_element_type=jnp.float32)
        acc_scr[:, cols] = jnp.where(step == 0, term, acc_scr[:, cols] + term)

    @pl.when(step == CHUNKS - 1)
    def _():
        write_heads(kv_ref, acc_scr)


def project(hidden, scale, gain, key_weight, value_weight, unit):
    rows, features = hidden.shape
    chunk = features // CHUNKS
    width = key_weight.shape[1] // UNITS
    weight = pl.BlockSpec((chunk, width), lambda i: (i, unit))
    return pl.pallas_call(
        project_kernel,
        grid=(CHUNKS,),
        in_specs=[
            pl.BlockSpec((rows, chunk), lambda i: (0, i)),
            pl.BlockSpec(scale.shape, lambda i: (0, 0)),
            pl.BlockSpec((1, chunk), lambda i: (0, i)),
            weight,
            weight,
        ],
        out_specs=pl.BlockSpec((rows, 2 * width), lambda i: (0, 0)),
        out_shape=jax.ShapeDtypeStruct((rows, 2 * width), jnp.bfloat16),
        scratch_shapes=[pltpu.VMEM((rows, 2 * width), jnp.float32)],
        compiler_params=pltpu.CompilerParams(vmem_limit_bytes=57 * MIB),
        cost_estimate=pl.CostEstimate(
            flops=4 * rows * features * width, bytes_accessed=16 * MIB, transcendentals=0
        ),
        name="project",
    )(hidden, scale, gain.reshape(1, features), key_weight, value_weight)


def attention_kernel(block, unit, near, slot_ref, cut_ref, odd_ref, q_hbm, *refs):
    own_hbm, straight, crossed = refs[0], refs[1 : near + 1], refs[near + 1 : 2 * near + 2]
    out_hbm, kv_scr, q_scr, out_scr, kv_sem, q_sem, out_sem = refs[-7:]
    kv_heads, levels, rows, width = kv_scr.shape
    depth = levels - 1
    steps, tall, wide = q_scr.shape
    per_head = steps // kv_heads
    per_group = wide // HEAD_DIM
    scale = HEAD_DIM**-0.5 * LOG2E

    def load_kv(head):
        def copy(ref, level, number):
            return pltpu.make_async_copy(
                ref.at[:, head * width : (head + 1) * width],
                kv_scr.at[head, level],
                kv_sem.at[head, number],
            )

        copies = [copy(own_hbm, depth, 0)]
        for s, ref in enumerate(straight):
            copies.append(copy(ref, 2 * s + 1, s + 1))
        for s, ref in enumerate(crossed):
            level = 2 * lax.rem(s + odd_ref[0] + near, near + 1)
            copies.append(copy(ref, level, near + s + 1))
        return copies

    def place(ref, step):
        head, part = lax.div(step, per_head), lax.rem(step, per_head)
        span = pl.ds(pl.multiple_of(part * tall, tall), tall)
        cols = pl.ds(pl.multiple_of((unit * kv_heads + head) * wide, wide), wide)
        return ref.at[span, cols]

    def load_q(step):
        return pltpu.make_async_copy(place(q_hbm, step), q_scr.at[step], q_sem.at[step])

    def store(step):
        return pltpu.make_async_copy(out_scr.at[step], place(out_hbm, step), out_sem.at[step])

    for head in range(kv_heads):
        for copy in load_kv(head):
            copy.start()
        for step in range(head * per_head, (head + 1) * per_head):
            load_q(step).start()

    token = lax.broadcasted_iota(jnp.int32, (block, HEAD_DIM), 0)
    lane = lax.broadcasted_iota(jnp.int32, (block, HEAD_DIM), 1)
    hidden_later = jnp.where((lane >= block) & (lane - block > token), MASKED, 0.0)
    query_mask = jnp.where(lane == 0, 1.0, hidden_later).astype(jnp.bfloat16)
    query_mask = jnp.concatenate([query_mask] * per_group, axis=0)
    own_mask = jnp.where(lane - block == token, 1.0, 0.0).astype(jnp.bfloat16)

    def score(step, local):
        head = lax.div(step, per_head)
        here = lax.rem(step, per_head) * BLOCKS_PER_STEP + local
        pieces, masks = [], []
        for k in range(depth):
            span = pl.ds(pl.multiple_of(slot_ref[here, k] * block, block), block)
            pieces.append(kv_scr[head, k, span, :])
            unseen = (lane == 0) & (token >= cut_ref[here, k])
            masks.append(jnp.where(unseen, MASKED, 0.0).astype(jnp.bfloat16))
        span = pl.ds(pl.multiple_of(here * block, block), block)
        pieces.append(kv_scr[head, depth, span, :])
        masks.append(own_mask)
        every = jnp.concatenate(pieces, axis=0)
        keys = jnp.concatenate([every[:, :HEAD_DIM], jnp.concatenate(masks, axis=0)], axis=1)
        span = slice(local * block, (local + 1) * block)
        queries = jnp.concatenate(
            [q_scr[step, span, r * HEAD_DIM : (r + 1) * HEAD_DIM] for r in range(per_group)], axis=0
        )
        queries = jnp.concatenate([queries, query_mask], axis=1)
        scores = lax.dot_general(
            queries, keys, (((1,), (1,)), ((), ())), preferred_element_type=jnp.float32
        )
        return scores, every[:, HEAD_DIM:]

    def finish(step, local, scores, values):
        peak = jnp.max(scores, axis=-1, keepdims=True)
        weights = jnp.exp2((scores - peak) * scale).astype(jnp.bfloat16)
        padded = jnp.concatenate([values, jnp.ones_like(values)], axis=1)
        both = jnp.dot(weights, padded, preferred_element_type=jnp.float32)
        context = (both[:, :HEAD_DIM] * (1.0 / both[:, HEAD_DIM:])).astype(jnp.bfloat16)
        span = slice(local * block, (local + 1) * block)
        for r in range(per_group):
            out_scr[step, span, r * HEAD_DIM : (r + 1) * HEAD_DIM] = context[
                r * block : (r + 1) * block
            ]

    def body(step, carry):
        load_q(step).wait()
        for head in range(kv_heads):

            @pl.when(step == head * per_head)
            def _(head=head):
                for copy in load_kv(head):
                    copy.wait()

        waiting = None
        for local in range(BLOCKS_PER_STEP):
            scores, values = score(step, local)
            if waiting is not None:
                finish(step, *waiting)
            waiting = (local, scores, values)
        finish(step, *waiting)
        store(step).start()
        return carry

    lax.fori_loop(0, steps, body, 0)
    for step in range(steps):
        store(step).wait()


def attention(slots, cuts, odd, queries, own, straight, crossed, unit, previous):
    rows, features = queries.shape
    blocks, depth = slots.shape
    block = rows // blocks
    near = len(straight)
    kv_heads = own.shape[1] // (2 * HEAD_DIM)
    wide = features // UNITS // kv_heads
    steps = kv_heads * blocks // BLOCKS_PER_STEP
    held = pl.BlockSpec(memory_space=pltpu.HBM)
    table = pl.BlockSpec(memory_space=pltpu.SMEM)
    operands = [slots, cuts, odd, queries, own, *straight, *crossed]
    aliases = {}
    if previous is not None:
        aliases = {len(operands): 0}
        operands.append(previous)
    return pl.pallas_call(
        functools.partial(attention_kernel, block, unit, near),
        in_specs=[table] * 3 + [held] * (len(operands) - 3),
        out_specs=held,
        out_shape=jax.ShapeDtypeStruct((rows, features), jnp.bfloat16),
        input_output_aliases=aliases,
        scratch_shapes=[
            pltpu.VMEM((kv_heads, depth + 1, rows, 2 * HEAD_DIM), own.dtype),
            pltpu.VMEM((steps, BLOCKS_PER_STEP * block, wide), jnp.bfloat16),
            pltpu.VMEM((steps, BLOCKS_PER_STEP * block, wide), jnp.bfloat16),
            pltpu.SemaphoreType.DMA((kv_heads, depth + 1)),
            pltpu.SemaphoreType.DMA((steps,)),
            pltpu.SemaphoreType.DMA((steps,)),
        ],
        compiler_params=pltpu.CompilerParams(vmem_limit_bytes=57 * MIB),
        cost_estimate=pl.CostEstimate(
            flops=4 * rows * wide * kv_heads * (depth + 1) * block,
            bytes_accessed=8 * MIB,
            transcendentals=rows * wide // HEAD_DIM * kv_heads * (depth + 1) * block,
        ),
        name="attention",
    )(*operands)


def shards(hidden, queries, norm_gain, key_weight, value_weight, anc_ids, anc_cut):
    blocks, depth = anc_ids.shape
    levels = depth + 1
    size = lax.axis_size("node")
    chains = size // levels
    near = depth // 2
    half = [index // chains // 2 for index in range(size)]
    even = [index // chains % 2 == 0 for index in range(size)]
    other = [index + chains if even[index] else index - chains for index in range(size)]
    odd = (lax.axis_index("node") // chains % 2).astype(jnp.int32).reshape(1)
    slots = jnp.where(anc_ids >= 0, anc_ids % blocks, 0)

    scale, first = norm_project(hidden, norm_gain, key_weight, value_weight)
    own = [first, project(hidden, scale, norm_gain, key_weight, value_weight, 1)]
    def after(array, *earlier):
        return lax.optimization_barrier((array, *earlier))[0]

    column = 2 * chains
    moved = {("own", 0, 0): own[0], ("own", 0, 1): own[1]}

    def step(kind, s, unit, waits):
        if kind == "across":
            source = ("along", s, unit) if s else ("own", 0, unit)
            exchange = s > 0 or unit == UNITS - 1
            pairs = [
                (i, other[i])
                for i in range(size)
                if half[i] >= s and (even[i] or (exchange and half[i] == 0) or s > 0)
            ]
        elif kind == "along":
            source = ("along", s - 1, unit) if s > 1 else ("own", 0, unit)
            pairs = [(i, i + column) for i in range(size - column) if half[i] >= s - 1]
        else:
            source = ("across" if kind == "down" else "own", 0, unit)
            pairs = [(i, i + s * column) for i in range(size - s * column)]
        array = lax.optimization_barrier((moved[source], *[moved[w] for w in waits]))[0]
        key = "along" if kind == "direct" else kind
        moved[key, s, unit] = lax.ppermute(array, "node", pairs)

    for kind, s, unit, waits in PLAN:
        step(kind, s, unit, waits)
    result = None
    for unit in range(UNITS):
        result = attention(
            slots,
            anc_cut,
            odd,
            queries,
            own[unit],
            [moved["along", s, unit] for s in range(1, near + 1)],
            [moved["across", s, unit] for s in range(near)]
            + [moved["across" if unit == 0 else "down", near, unit]],
            unit,
            result,
        )
    return result


def solution(mesh):
    placed = (
        P(("groups", "node"), None),
        P(("groups", "node"), None),
        P(),
        P(),
        P(),
        P(("groups", "node"), None),
        P(("groups", "node"), None),
    )
    return jax.shard_map(
        shards, mesh=mesh, in_specs=placed, out_specs=P(("groups", "node"), None), check_vma=False
    )
```

```python
import functools
import jax
import jax.numpy as jnp
from jax import lax
from jax.experimental import pallas as pl
from jax.experimental.pallas import tpu as pltpu
from jax.sharding import PartitionSpec as P

HEAD_DIM = 128
EPS = 1e-05
LOG2E = 1.4426950408889634
MASKED = -1e30
MIB = 1024 * 1024
CHUNKS = 4
LOADS = 8
UNITS = 2
BLOCKS_PER_STEP = 4


PLAN = (
    ("across", 0, 0, ()),
    ("along", 1, 0, ()),
    ("across", 0, 1, ()),
    ("along", 1, 1, ()),
    ("across", 1, 0, (("across", 0, 0),)),
    ("along", 2, 0, (("along", 1, 0),)),
    ("across", 1, 1, (("across", 0, 1),)),
    ("along", 3, 0, (("along", 1, 1),)),
    ("across", 2, 0, (("across", 1, 0),)),
    ("along", 2, 1, (("along", 2, 0),)),
    ("across", 3, 0, (("across", 1, 1),)),
    ("across", 2, 1, (("across", 2, 0),)),
    ("down", 3, 1, (("along", 3, 0), ("across", 2, 0))),
    ("along", 3, 1, (("along", 2, 1),)),
)


def norm_project_kernel(
    x_hbm, gain_ref, key_hbm, value_hbm, scale_ref, kv_ref,
    x_scr, key_scr, value_scr, even_scr, odd_scr, acc_scr, x_sem, key_sem, value_sem,
):
    rows, features = x_scr.shape
    loads = LOADS
    tall = rows // loads
    chunks, chunk = key_scr.shape[:2]
    width = key_scr.shape[2] // UNITS
    lanes = 128
    band = 128

    def span(c):
        return pl.ds(pl.multiple_of(c * chunk, chunk), chunk)

    def load_x(c):
        row = pl.ds(pl.multiple_of(c * tall, tall), tall)
        return pltpu.make_async_copy(x_hbm.at[row], x_scr.at[row], x_sem.at[c])

    def load_weights(c):
        return [
            pltpu.make_async_copy(hbm.at[span(c)], scr.at[c], sem.at[c])
            for hbm, scr, sem in ((key_hbm, key_scr, key_sem), (value_hbm, value_scr, value_sem))
        ]

    for c in range(loads):
        load_x(c).start()

    def square(c, carry):
        load_x(c).wait()

        @pl.when(c == loads - 2)
        def _():
            for copy in load_weights(0):
                copy.start()

        row = pl.ds(pl.multiple_of(c * tall, tall), tall)
        total = jnp.zeros((tall, lanes), jnp.float32)
        for lane in range(0, features, lanes):
            x = x_scr[row, lane : lane + lanes].astype(jnp.float32)
            total += x * x
        scale_ref[row, :] = total
        return carry

    lax.fori_loop(0, loads, square, 0)
    for c in range(1, chunks):
        for copy in load_weights(c):
            copy.start()
    mean_sq = jnp.sum(scale_ref[...], axis=-1, keepdims=True) / features
    scale_ref[...] = jnp.broadcast_to(lax.rsqrt(mean_sq + EPS), scale_ref.shape)

    def normalise(normed_scr, c):
        for first in range(0, rows, band):
            row = slice(first, first + band)
            inverse = scale_ref[row, :]
            for lane in range(0, chunk, lanes):
                cols = pl.ds(pl.multiple_of(c * chunk + lane, lanes), lanes)
                x = x_scr[row, cols].astype(jnp.float32)
                normed_scr[row, lane : lane + lanes] = (
                    x * inverse * gain_ref[:, cols]
                ).astype(jnp.bfloat16)

    def multiply(normed_scr, c):
        for copy in load_weights(c):
            copy.wait()
        normed = normed_scr[...]
        for part, weight in enumerate((key_scr, value_scr)):
            acc_scr[:, part * width : (part + 1) * width] += jnp.dot(
                normed, weight[c, :, :width], preferred_element_type=jnp.float32
            )

    normalise(even_scr, 0)
    acc_scr[...] = jnp.zeros_like(acc_scr)

    def pair(p, carry):
        multiply(even_scr, 2 * p)
        normalise(odd_scr, 2 * p + 1)
        multiply(odd_scr, 2 * p + 1)
        normalise(even_scr, 2 * p + 2)
        return carry

    lax.fori_loop(0, chunks // 2 - 1, pair, 0)
    multiply(even_scr, chunks - 2)
    normalise(odd_scr, chunks - 1)
    multiply(odd_scr, chunks - 1)
    write_heads(kv_ref, acc_scr)


def write_heads(kv_ref, acc_scr):
    width = kv_ref.shape[1] // 2
    for head in range(width // HEAD_DIM):
        for part in range(2):
            source = slice(part * width + head * HEAD_DIM, part * width + (head + 1) * HEAD_DIM)
            target = slice((2 * head + part) * HEAD_DIM, (2 * head + part + 1) * HEAD_DIM)
            kv_ref[:, target] = acc_scr[:, source].astype(jnp.bfloat16)


def norm_project(hidden, gain, key_weight, value_weight):
    rows, features = hidden.shape
    width = key_weight.shape[1] // UNITS
    chunk = features // LOADS
    whole = pl.BlockSpec(memory_space=pltpu.VMEM)
    held = pl.BlockSpec(memory_space=pltpu.HBM)
    return pl.pallas_call(
        norm_project_kernel,
        in_specs=[held, whole, held, held],
        out_specs=[whole, whole],
        out_shape=[
            jax.ShapeDtypeStruct((rows, 128), jnp.float32),
            jax.ShapeDtypeStruct((rows, 2 * width), jnp.bfloat16),
        ],
        scratch_shapes=[
            pltpu.VMEM((rows, features), jnp.bfloat16),
            pltpu.VMEM((LOADS, chunk, key_weight.shape[1]), jnp.bfloat16),
            pltpu.VMEM((LOADS, chunk, key_weight.shape[1]), jnp.bfloat16),
            pltpu.VMEM((rows, chunk), jnp.bfloat16),
            pltpu.VMEM((rows, chunk), jnp.bfloat16),
            pltpu.VMEM((rows, 2 * width), jnp.float32),
            pltpu.SemaphoreType.DMA((LOADS,)),
            pltpu.SemaphoreType.DMA((LOADS,)),
            pltpu.SemaphoreType.DMA((LOADS,)),
        ],
        compiler_params=pltpu.CompilerParams(vmem_limit_bytes=57 * MIB),
        cost_estimate=pl.CostEstimate(
            flops=4 * rows * features * width, bytes_accessed=16 * MIB, transcendentals=0
        ),
        name="norm_project",
    )(hidden, gain.reshape(1, features), key_weight, value_weight)


def project_kernel(x_ref, scale_ref, gain_ref, key_ref, value_ref, kv_ref, acc_scr):
    step = pl.program_id(0)
    rows, chunk = x_ref.shape
    width = key_ref.shape[1]
    lanes = 128
    inverse = scale_ref[...]
    parts = []
    for lane in range(0, chunk, lanes):
        cols = slice(lane, lane + lanes)
        x = x_ref[:, cols].astype(jnp.float32)
        parts.append((x * inverse * gain_ref[:, cols]).astype(jnp.bfloat16))
    normed = jnp.concatenate(parts, axis=1)
    for part, weight in enumerate((key_ref, value_ref)):
        cols = slice(part * width, (part + 1) * width)
        term = jnp.dot(normed, weight[...], preferred_element_type=jnp.float32)
        acc_scr[:, cols] = jnp.where(step == 0, term, acc_scr[:, cols] + term)

    @pl.when(step == CHUNKS - 1)
    def _():
        write_heads(kv_ref, acc_scr)


def project(hidden, scale, gain, key_weight, value_weight, unit):
    rows, features = hidden.shape
    chunk = features // CHUNKS
    width = key_weight.shape[1] // UNITS
    weight = pl.BlockSpec((chunk, width), lambda i: (i, unit))
    return pl.pallas_call(
        project_kernel,
        grid=(CHUNKS,),
        in_specs=[
            pl.BlockSpec((rows, chunk), lambda i: (0, i)),
            pl.BlockSpec(scale.shape, lambda i: (0, 0)),
            pl.BlockSpec((1, chunk), lambda i: (0, i)),
            weight,
            weight,
        ],
        out_specs=pl.BlockSpec((rows, 2 * width), lambda i: (0, 0)),
        out_shape=jax.ShapeDtypeStruct((rows, 2 * width), jnp.bfloat16),
        scratch_shapes=[pltpu.VMEM((rows, 2 * width), jnp.float32)],
        compiler_params=pltpu.CompilerParams(vmem_limit_bytes=57 * MIB),
        cost_estimate=pl.CostEstimate(
            flops=4 * rows * features * width, bytes_accessed=16 * MIB, transcendentals=0
        ),
        name="project",
    )(hidden, scale, gain.reshape(1, features), key_weight, value_weight)


def attention_kernel(block, unit, near, slot_ref, cut_ref, odd_ref, q_hbm, *refs):
    own_hbm, straight, crossed = refs[0], refs[1 : near + 1], refs[near + 1 : 2 * near + 2]
    out_hbm, kv_scr, q_scr, out_scr, kv_sem, q_sem, out_sem = refs[-7:]
    kv_heads, levels, rows, width = kv_scr.shape
    depth = levels - 1
    steps, tall, wide = q_scr.shape
    per_head = steps // kv_heads
    per_group = wide // HEAD_DIM
    scale = HEAD_DIM**-0.5 * LOG2E

    def load_kv(head):
        def copy(ref, level, number):
            return pltpu.make_async_copy(
                ref.at[:, head * width : (head + 1) * width],
                kv_scr.at[head, level],
                kv_sem.at[head, number],
            )

        copies = [copy(own_hbm, depth, 0)]
        for s, ref in enumerate(straight):
            copies.append(copy(ref, 2 * s + 1, s + 1))
        for s, ref in enumerate(crossed):
            level = 2 * lax.rem(s + odd_ref[0] + near, near + 1)
            copies.append(copy(ref, level, near + s + 1))
        return copies

    def place(ref, step):
        head, part = lax.div(step, per_head), lax.rem(step, per_head)
        span = pl.ds(pl.multiple_of(part * tall, tall), tall)
        cols = pl.ds(pl.multiple_of((unit * kv_heads + head) * wide, wide), wide)
        return ref.at[span, cols]

    def load_q(step):
        return pltpu.make_async_copy(place(q_hbm, step), q_scr.at[step], q_sem.at[step])

    def store(step):
        return pltpu.make_async_copy(out_scr.at[step], place(out_hbm, step), out_sem.at[step])

    for head in range(kv_heads):
        for copy in load_kv(head):
            copy.start()
        for step in range(head * per_head, (head + 1) * per_head):
            load_q(step).start()

    token = lax.broadcasted_iota(jnp.int32, (block, HEAD_DIM), 0)
    lane = lax.broadcasted_iota(jnp.int32, (block, HEAD_DIM), 1)
    hidden_later = jnp.where((lane >= block) & (lane - block > token), MASKED, 0.0)
    query_mask = jnp.where(lane == 0, 1.0, hidden_later).astype(jnp.bfloat16)
    query_mask = jnp.concatenate([query_mask] * per_group, axis=0)
    own_mask = jnp.where(lane - block == token, 1.0, 0.0).astype(jnp.bfloat16)

    def score(step, local):
        head = lax.div(step, per_head)
        here = lax.rem(step, per_head) * BLOCKS_PER_STEP + local
        pieces, masks = [], []
        for k in range(depth):
            span = pl.ds(pl.multiple_of(slot_ref[here, k] * block, block), block)
            pieces.append(kv_scr[head, k, span, :])
            unseen = (lane == 0) & (token >= cut_ref[here, k])
            masks.append(jnp.where(unseen, MASKED, 0.0).astype(jnp.bfloat16))
        span = pl.ds(pl.multiple_of(here * block, block), block)
        pieces.append(kv_scr[head, depth, span, :])
        masks.append(own_mask)
        every = jnp.concatenate(pieces, axis=0)
        keys = jnp.concatenate([every[:, :HEAD_DIM], jnp.concatenate(masks, axis=0)], axis=1)
        span = slice(local * block, (local + 1) * block)
        queries = jnp.concatenate(
            [q_scr[step, span, r * HEAD_DIM : (r + 1) * HEAD_DIM] for r in range(per_group)], axis=0
        )
        queries = jnp.concatenate([queries, query_mask], axis=1)
        scores = lax.dot_general(
            queries, keys, (((1,), (1,)), ((), ())), preferred_element_type=jnp.float32
        )
        return scores, every[:, HEAD_DIM:]

    def finish(step, local, scores, values):
        peak = jnp.max(scores, axis=-1, keepdims=True)
        weights = jnp.exp2((scores - peak) * scale).astype(jnp.bfloat16)
        padded = jnp.concatenate([values, jnp.ones_like(values)], axis=1)
        both = jnp.dot(weights, padded, preferred_element_type=jnp.float32)
        context = (both[:, :HEAD_DIM] * (1.0 / both[:, HEAD_DIM:])).astype(jnp.bfloat16)
        span = slice(local * block, (local + 1) * block)
        for r in range(per_group):
            out_scr[step, span, r * HEAD_DIM : (r + 1) * HEAD_DIM] = context[
                r * block : (r + 1) * block
            ]

    def body(step, carry):
        load_q(step).wait()
        for head in range(kv_heads):

            @pl.when(step == head * per_head)
            def _(head=head):
                for copy in load_kv(head):
                    copy.wait()

        waiting = None
        for local in range(BLOCKS_PER_STEP):
            scores, values = score(step, local)
            if waiting is not None:
                finish(step, *waiting)
            waiting = (local, scores, values)
        finish(step, *waiting)
        store(step).start()
        return carry

    lax.fori_loop(0, steps, body, 0)
    for step in range(steps):
        store(step).wait()


def attention(slots, cuts, odd, queries, own, straight, crossed, unit, previous):
    rows, features = queries.shape
    blocks, depth = slots.shape
    block = rows // blocks
    near = len(straight)
    kv_heads = own.shape[1] // (2 * HEAD_DIM)
    wide = features // UNITS // kv_heads
    steps = kv_heads * blocks // BLOCKS_PER_STEP
    held = pl.BlockSpec(memory_space=pltpu.HBM)
    table = pl.BlockSpec(memory_space=pltpu.SMEM)
    operands = [slots, cuts, odd, queries, own, *straight, *crossed]
    aliases = {}
    if previous is not None:
        aliases = {len(operands): 0}
        operands.append(previous)
    return pl.pallas_call(
        functools.partial(attention_kernel, block, unit, near),
        in_specs=[table] * 3 + [held] * (len(operands) - 3),
        out_specs=held,
        out_shape=jax.ShapeDtypeStruct((rows, features), jnp.bfloat16),
        input_output_aliases=aliases,
        scratch_shapes=[
            pltpu.VMEM((kv_heads, depth + 1, rows, 2 * HEAD_DIM), own.dtype),
            pltpu.VMEM((steps, BLOCKS_PER_STEP * block, wide), jnp.bfloat16),
            pltpu.VMEM((steps, BLOCKS_PER_STEP * block, wide), jnp.bfloat16),
            pltpu.SemaphoreType.DMA((kv_heads, depth + 1)),
            pltpu.SemaphoreType.DMA((steps,)),
            pltpu.SemaphoreType.DMA((steps,)),
        ],
        compiler_params=pltpu.CompilerParams(vmem_limit_bytes=57 * MIB),
        cost_estimate=pl.CostEstimate(
            flops=4 * rows * wide * kv_heads * (depth + 1) * block,
            bytes_accessed=8 * MIB,
            transcendentals=rows * wide // HEAD_DIM * kv_heads * (depth + 1) * block,
        ),
        name="attention",
    )(*operands)


def shards(hidden, queries, norm_gain, key_weight, value_weight, anc_ids, anc_cut):
    blocks, depth = anc_ids.shape
    levels = depth + 1
    size = lax.axis_size("node")
    chains = size // levels
    near = depth // 2
    half = [index // chains // 2 for index in range(size)]
    even = [index // chains % 2 == 0 for index in range(size)]
    other = [index + chains if even[index] else index - chains for index in range(size)]
    odd = (lax.axis_index("node") // chains % 2).astype(jnp.int32).reshape(1)
    slots = jnp.where(anc_ids >= 0, anc_ids % blocks, 0)

    scale, first = norm_project(hidden, norm_gain, key_weight, value_weight)
    own = [first, project(hidden, scale, norm_gain, key_weight, value_weight, 1)]
    def after(array, *earlier):
        return lax.optimization_barrier((array, *earlier))[0]

    column = 2 * chains
    moved = {("own", 0, 0): own[0], ("own", 0, 1): own[1]}

    def step(kind, s, unit, waits):
        if kind == "across":
            source = ("along", s, unit) if s else ("own", 0, unit)
            exchange = s > 0 or unit == UNITS - 1
            pairs = [
                (i, other[i])
                for i in range(size)
                if half[i] >= s and (even[i] or (exchange and half[i] == 0) or s > 0)
            ]
        elif kind == "along":
            source = ("along", s - 1, unit) if s > 1 else ("own", 0, unit)
            pairs = [(i, i + column) for i in range(size - column) if half[i] >= s - 1]
        else:
            source = ("across" if kind == "down" else "own", 0, unit)
            pairs = [(i, i + s * column) for i in range(size - s * column)]
        array = lax.optimization_barrier((moved[source], *[moved[w] for w in waits]))[0]
        key = "along" if kind == "direct" else kind
        moved[key, s, unit] = lax.ppermute(array, "node", pairs)

    for kind, s, unit, waits in PLAN:
        step(kind, s, unit, waits)
    result = None
    for unit in range(UNITS):
        result = attention(
            slots,
            anc_cut,
            odd,
            queries,
            own[unit],
            [moved["along", s, unit] for s in range(1, near + 1)],
            [moved["across", s, unit] for s in range(near)]
            + [moved["across" if unit == 0 else "down", near, unit]],
            unit,
            result,
        )
    return result


def solution(mesh):
    placed = (
        P(("groups", "node"), None),
        P(("groups", "node"), None),
        P(),
        P(),
        P(),
        P(("groups", "node"), None),
        P(("groups", "node"), None),
    )
    return jax.shard_map(
        shards, mesh=mesh, in_specs=placed, out_specs=P(("groups", "node"), None), check_vma=False
    )
```

```python
import functools
import jax
import jax.numpy as jnp
from jax import lax
from jax.experimental import pallas as pl
from jax.experimental.pallas import tpu as pltpu
from jax.sharding import PartitionSpec as P

HEAD_DIM = 128
EPS = 1e-05
LOG2E = 1.4426950408889634
MASKED = -1e30
MIB = 1024 * 1024
CHUNKS = 4
LOADS = 8
UNITS = 2
BLOCKS_PER_STEP = 8


PLAN = (
    ("across", 0, 0, ()),
    ("along", 1, 0, ()),
    ("across", 0, 1, ()),
    ("along", 1, 1, ()),
    ("across", 1, 0, (("across", 0, 0),)),
    ("along", 2, 0, (("along", 1, 0),)),
    ("across", 1, 1, (("across", 0, 1),)),
    ("along", 3, 0, (("along", 1, 1),)),
    ("across", 2, 0, (("across", 1, 0),)),
    ("along", 2, 1, (("along", 2, 0),)),
    ("across", 3, 0, (("across", 1, 1),)),
    ("across", 2, 1, (("across", 2, 0),)),
    ("down", 3, 1, (("along", 3, 0),)),
    ("along", 3, 1, (("along", 2, 1), ("down", 3, 1))),
)


def norm_project_kernel(
    x_hbm, gain_ref, key_hbm, value_hbm, scale_ref, kv_ref,
    x_scr, weight_scr, even_scr, odd_scr, acc_scr, x_sem, key_sem, value_sem,
):
    loads, rows, chunk = x_scr.shape
    width = weight_scr.shape[2] // 2
    lanes = 128
    band = 128

    def span(c):
        return pl.ds(pl.multiple_of(c * chunk, chunk), chunk)

    def load_x(c):
        return pltpu.make_async_copy(x_hbm.at[:, span(c)], x_scr.at[c], x_sem.at[c])

    def load_weights(c):
        head = pl.ds(0, width)
        return [
            pltpu.make_async_copy(
                key_hbm.at[span(c), head], weight_scr.at[c, :, pl.ds(0, width)], key_sem.at[c]
            ),
            pltpu.make_async_copy(
                value_hbm.at[span(c), head], weight_scr.at[c, :, pl.ds(width, width)], value_sem.at[c]
            ),
        ]

    for c in range(loads):
        load_x(c).start()
    scale_ref[...] = jnp.zeros_like(scale_ref)

    def square(c, carry):
        load_x(c).wait()

        @pl.when(c >= loads // 2)
        def _():
            for part in range(2):
                for copy in load_weights(2 * (c - loads // 2) + part):
                    copy.start()

        for first in range(0, rows, band):
            row = slice(first, first + band)
            total = scale_ref[row, :]
            for lane in range(0, chunk, lanes):
                x = x_scr[c, row, lane : lane + lanes].astype(jnp.float32)
                total += x * x
            scale_ref[row, :] = total
        return carry

    lax.fori_loop(0, loads, square, 0)
    mean_sq = jnp.sum(scale_ref[...], axis=-1, keepdims=True) / (loads * chunk)
    scale_ref[...] = jnp.broadcast_to(lax.rsqrt(mean_sq + EPS), scale_ref.shape)

    def normalise(normed_scr, c):
        for first in range(0, rows, band):
            row = slice(first, first + band)
            inverse = scale_ref[row, :]
            for lane in range(0, chunk, lanes):
                cols = slice(lane, lane + lanes)
                x = x_scr[c, row, cols].astype(jnp.float32)
                gain = gain_ref[c, :, cols]
                normed_scr[row, cols] = (x * inverse * gain).astype(jnp.bfloat16)

    def multiply(normed_scr, c):
        for copy in load_weights(c):
            copy.wait()
        acc_scr[...] += jnp.dot(
            normed_scr[...], weight_scr[c], preferred_element_type=jnp.float32
        )

    normalise(even_scr, 0)
    acc_scr[...] = jnp.zeros_like(acc_scr)

    def pair(p, carry):
        multiply(even_scr, 2 * p)
        normalise(odd_scr, 2 * p + 1)
        multiply(odd_scr, 2 * p + 1)
        normalise(even_scr, 2 * p + 2)
        return carry

    lax.fori_loop(0, loads // 2 - 1, pair, 0)
    multiply(even_scr, loads - 2)
    normalise(odd_scr, loads - 1)
    multiply(odd_scr, loads - 1)
    write_heads(kv_ref, acc_scr)


def write_heads(kv_ref, acc_scr):
    width = kv_ref.shape[1] // 2
    for head in range(width // HEAD_DIM):
        for part in range(2):
            source = slice(part * width + head * HEAD_DIM, part * width + (head + 1) * HEAD_DIM)
            target = slice((2 * head + part) * HEAD_DIM, (2 * head + part + 1) * HEAD_DIM)
            kv_ref[:, target] = acc_scr[:, source].astype(jnp.bfloat16)


def norm_project(hidden, gain, key_weight, value_weight):
    rows, features = hidden.shape
    width = key_weight.shape[1] // UNITS
    chunk = features // LOADS
    whole = pl.BlockSpec(memory_space=pltpu.VMEM)
    held = pl.BlockSpec(memory_space=pltpu.HBM)
    return pl.pallas_call(
        norm_project_kernel,
        in_specs=[held, whole, held, held],
        out_specs=[whole, whole],
        out_shape=[
            jax.ShapeDtypeStruct((rows, 128), jnp.float32),
            jax.ShapeDtypeStruct((rows, 2 * width), jnp.bfloat16),
        ],
        scratch_shapes=[
            pltpu.VMEM((LOADS, rows, chunk), jnp.bfloat16),
            pltpu.VMEM((LOADS, chunk, 2 * width), jnp.bfloat16),
            pltpu.VMEM((rows, chunk), jnp.bfloat16),
            pltpu.VMEM((rows, chunk), jnp.bfloat16),
            pltpu.VMEM((rows, 2 * width), jnp.float32),
            pltpu.SemaphoreType.DMA((LOADS,)),
            pltpu.SemaphoreType.DMA((LOADS,)),
            pltpu.SemaphoreType.DMA((LOADS,)),
        ],
        compiler_params=pltpu.CompilerParams(vmem_limit_bytes=57 * MIB),
        cost_estimate=pl.CostEstimate(
            flops=4 * rows * features * width, bytes_accessed=16 * MIB, transcendentals=0
        ),
        name="norm_project",
    )(hidden, gain.reshape(LOADS, 1, chunk), key_weight, value_weight)


def project_kernel(x_ref, scale_ref, gain_ref, key_ref, value_ref, kv_ref, acc_scr):
    step = pl.program_id(0)
    rows, chunk = x_ref.shape
    width = key_ref.shape[1]
    lanes = 128
    inverse = scale_ref[...]
    parts = []
    for lane in range(0, chunk, lanes):
        cols = slice(lane, lane + lanes)
        x = x_ref[:, cols].astype(jnp.float32)
        parts.append((x * inverse * gain_ref[:, cols]).astype(jnp.bfloat16))
    normed = jnp.concatenate(parts, axis=1)
    for part, weight in enumerate((key_ref, value_ref)):
        cols = slice(part * width, (part + 1) * width)
        term = jnp.dot(normed, weight[...], preferred_element_type=jnp.float32)
        acc_scr[:, cols] = jnp.where(step == 0, term, acc_scr[:, cols] + term)

    @pl.when(step == CHUNKS - 1)
    def _():
        write_heads(kv_ref, acc_scr)


def project(hidden, scale, gain, key_weight, value_weight, unit):
    rows, features = hidden.shape
    chunk = features // CHUNKS
    width = key_weight.shape[1] // UNITS
    weight = pl.BlockSpec((chunk, width), lambda i: (i, unit))
    return pl.pallas_call(
        project_kernel,
        grid=(CHUNKS,),
        in_specs=[
            pl.BlockSpec((rows, chunk), lambda i: (0, i)),
            pl.BlockSpec(scale.shape, lambda i: (0, 0)),
            pl.BlockSpec((1, chunk), lambda i: (0, i)),
            weight,
            weight,
        ],
        out_specs=pl.BlockSpec((rows, 2 * width), lambda i: (0, 0)),
        out_shape=jax.ShapeDtypeStruct((rows, 2 * width), jnp.bfloat16),
        scratch_shapes=[pltpu.VMEM((rows, 2 * width), jnp.float32)],
        compiler_params=pltpu.CompilerParams(vmem_limit_bytes=57 * MIB),
        cost_estimate=pl.CostEstimate(
            flops=4 * rows * features * width, bytes_accessed=16 * MIB, transcendentals=0
        ),
        name="project",
    )(hidden, scale, gain.reshape(1, features), key_weight, value_weight)


def attention_kernel(block, unit, near, slot_ref, cut_ref, odd_ref, q_hbm, *refs):
    own_hbm, straight, crossed = refs[0], refs[1 : near + 1], refs[near + 1 : 2 * near + 2]
    out_hbm, kv_scr, q_scr, out_scr, kv_sem, q_sem, out_sem = refs[-7:]
    kv_heads, levels, rows, width = kv_scr.shape
    depth = levels - 1
    steps, tall, wide = q_scr.shape
    per_head = steps // kv_heads
    per_group = wide // HEAD_DIM
    scale = HEAD_DIM**-0.5 * LOG2E

    def load_kv(head):
        def copy(ref, level, number):
            return pltpu.make_async_copy(
                ref.at[:, head * width : (head + 1) * width],
                kv_scr.at[head, level],
                kv_sem.at[head, number],
            )

        copies = [copy(own_hbm, depth, 0)]
        for s, ref in enumerate(straight):
            copies.append(copy(ref, 2 * s + 1, s + 1))
        for s, ref in enumerate(crossed):
            level = 2 * lax.rem(s + odd_ref[0] + near, near + 1)
            copies.append(copy(ref, level, near + s + 1))
        return copies

    def place(ref, step):
        head, part = lax.div(step, per_head), lax.rem(step, per_head)
        span = pl.ds(pl.multiple_of(part * tall, tall), tall)
        cols = pl.ds(pl.multiple_of((unit * kv_heads + head) * wide, wide), wide)
        return ref.at[span, cols]

    def load_q(step):
        return pltpu.make_async_copy(place(q_hbm, step), q_scr.at[step], q_sem.at[step])

    def store(step):
        return pltpu.make_async_copy(out_scr.at[step], place(out_hbm, step), out_sem.at[step])

    for head in range(kv_heads):
        for copy in load_kv(head):
            copy.start()
        for step in range(head * per_head, (head + 1) * per_head):
            load_q(step).start()

    token = lax.broadcasted_iota(jnp.int32, (block, HEAD_DIM), 0)
    lane = lax.broadcasted_iota(jnp.int32, (block, HEAD_DIM), 1)
    hidden_later = jnp.where((lane >= block) & (lane - block > token), MASKED, 0.0)
    query_mask = jnp.where(lane == 0, 1.0, hidden_later).astype(jnp.bfloat16)
    query_mask = jnp.concatenate([query_mask] * per_group, axis=0)
    own_mask = jnp.where(lane - block == token, 1.0, 0.0).astype(jnp.bfloat16)

    def score(step, local):
        head = lax.div(step, per_head)
        here = lax.rem(step, per_head) * BLOCKS_PER_STEP + local
        pieces, masks = [], []
        for k in range(depth):
            span = pl.ds(pl.multiple_of(slot_ref[here, k] * block, block), block)
            pieces.append(kv_scr[head, k, span, :])
            unseen = (lane == 0) & (token >= cut_ref[here, k])
            masks.append(jnp.where(unseen, MASKED, 0.0).astype(jnp.bfloat16))
        span = pl.ds(pl.multiple_of(here * block, block), block)
        pieces.append(kv_scr[head, depth, span, :])
        masks.append(own_mask)
        every = jnp.concatenate(pieces, axis=0)
        keys = jnp.concatenate([every[:, :HEAD_DIM], jnp.concatenate(masks, axis=0)], axis=1)
        span = slice(local * block, (local + 1) * block)
        queries = jnp.concatenate(
            [q_scr[step, span, r * HEAD_DIM : (r + 1) * HEAD_DIM] for r in range(per_group)], axis=0
        )
        queries = jnp.concatenate([queries, query_mask], axis=1)
        scores = lax.dot_general(
            queries, keys, (((1,), (1,)), ((), ())), preferred_element_type=jnp.float32
        )
        return scores, every[:, HEAD_DIM:]

    def finish(step, local, scores, values):
        peak = jnp.max(scores, axis=-1, keepdims=True)
        weights = jnp.exp2((scores - peak) * scale).astype(jnp.bfloat16)
        padded = jnp.concatenate([values, jnp.ones_like(values)], axis=1)
        both = jnp.dot(weights, padded, preferred_element_type=jnp.float32)
        context = (both[:, :HEAD_DIM] * (1.0 / both[:, HEAD_DIM:])).astype(jnp.bfloat16)
        span = slice(local * block, (local + 1) * block)
        for r in range(per_group):
            out_scr[step, span, r * HEAD_DIM : (r + 1) * HEAD_DIM] = context[
                r * block : (r + 1) * block
            ]

    def body(step, carry):
        load_q(step).wait()
        for head in range(kv_heads):

            @pl.when(step == head * per_head)
            def _(head=head):
                for copy in load_kv(head):
                    copy.wait()

        waiting = None
        for local in range(BLOCKS_PER_STEP):
            scores, values = score(step, local)
            if waiting is not None:
                finish(step, *waiting)
            waiting = (local, scores, values)
        finish(step, *waiting)
        store(step).start()
        return carry

    lax.fori_loop(0, steps, body, 0)
    for step in range(steps):
        store(step).wait()


def attention(slots, cuts, odd, queries, own, straight, crossed, unit, previous):
    rows, features = queries.shape
    blocks, depth = slots.shape
    block = rows // blocks
    near = len(straight)
    kv_heads = own.shape[1] // (2 * HEAD_DIM)
    wide = features // UNITS // kv_heads
    steps = kv_heads * blocks // BLOCKS_PER_STEP
    held = pl.BlockSpec(memory_space=pltpu.HBM)
    table = pl.BlockSpec(memory_space=pltpu.SMEM)
    operands = [slots, cuts, odd, queries, own, *straight, *crossed]
    aliases = {}
    if previous is not None:
        aliases = {len(operands): 0}
        operands.append(previous)
    return pl.pallas_call(
        functools.partial(attention_kernel, block, unit, near),
        in_specs=[table] * 3 + [held] * (len(operands) - 3),
        out_specs=held,
        out_shape=jax.ShapeDtypeStruct((rows, features), jnp.bfloat16),
        input_output_aliases=aliases,
        scratch_shapes=[
            pltpu.VMEM((kv_heads, depth + 1, rows, 2 * HEAD_DIM), own.dtype),
            pltpu.VMEM((steps, BLOCKS_PER_STEP * block, wide), jnp.bfloat16),
            pltpu.VMEM((steps, BLOCKS_PER_STEP * block, wide), jnp.bfloat16),
            pltpu.SemaphoreType.DMA((kv_heads, depth + 1)),
            pltpu.SemaphoreType.DMA((steps,)),
            pltpu.SemaphoreType.DMA((steps,)),
        ],
        compiler_params=pltpu.CompilerParams(vmem_limit_bytes=57 * MIB),
        cost_estimate=pl.CostEstimate(
            flops=4 * rows * wide * kv_heads * (depth + 1) * block,
            bytes_accessed=8 * MIB,
            transcendentals=rows * wide // HEAD_DIM * kv_heads * (depth + 1) * block,
        ),
        name="attention",
    )(*operands)


def shards(hidden, queries, norm_gain, key_weight, value_weight, anc_ids, anc_cut):
    blocks, depth = anc_ids.shape
    levels = depth + 1
    size = lax.axis_size("node")
    chains = size // levels
    near = depth // 2
    half = [index // chains // 2 for index in range(size)]
    even = [index // chains % 2 == 0 for index in range(size)]
    other = [index + chains if even[index] else index - chains for index in range(size)]
    odd = (lax.axis_index("node") // chains % 2).astype(jnp.int32).reshape(1)
    slots = jnp.where(anc_ids >= 0, anc_ids % blocks, 0)

    scale, first = norm_project(hidden, norm_gain, key_weight, value_weight)
    own = [first, project(hidden, scale, norm_gain, key_weight, value_weight, 1)]
    def after(array, *earlier):
        return lax.optimization_barrier((array, *earlier))[0]

    column = 2 * chains
    moved = {("own", 0, 0): own[0], ("own", 0, 1): own[1]}

    def step(kind, s, unit, waits):
        if kind == "across":
            source = ("along", s, unit) if s else ("own", 0, unit)
            exchange = s > 0 or unit == UNITS - 1
            pairs = [
                (i, other[i])
                for i in range(size)
                if half[i] >= s and (even[i] or (exchange and half[i] == 0) or s > 0)
            ]
        elif kind == "along":
            source = ("along", s - 1, unit) if s > 1 else ("own", 0, unit)
            pairs = [(i, i + column) for i in range(size - column) if half[i] >= s - 1]
        else:
            source = ("across" if kind == "down" else "own", 0, unit)
            pairs = [(i, i + s * column) for i in range(size - s * column)]
        array = lax.optimization_barrier((moved[source], *[moved[w] for w in waits]))[0]
        key = "along" if kind == "direct" else kind
        moved[key, s, unit] = lax.ppermute(array, "node", pairs)

    for kind, s, unit, waits in PLAN:
        step(kind, s, unit, waits)
    result = None
    for unit in range(UNITS):
        result = attention(
            slots,
            anc_cut,
            odd,
            queries,
            own[unit],
            [moved["along", s, unit] for s in range(1, near + 1)],
            [moved["across", s, unit] for s in range(near)]
            + [moved["across" if unit == 0 else "down", near, unit]],
            unit,
            result,
        )
    return result


def solution(mesh):
    placed = (
        P(("groups", "node"), None),
        P(("groups", "node"), None),
        P(),
        P(),
        P(),
        P(("groups", "node"), None),
        P(("groups", "node"), None),
    )
    return jax.shard_map(
        shards, mesh=mesh, in_specs=placed, out_specs=P(("groups", "node"), None), check_vma=False
    )
```

```python
import functools
import jax
import jax.numpy as jnp
from jax import lax
from jax.experimental import pallas as pl
from jax.experimental.pallas import tpu as pltpu
from jax.sharding import PartitionSpec as P

HEAD_DIM = 128
EPS = 1e-05
LOG2E = 1.4426950408889634
MASKED = -1e30
MIB = 1024 * 1024
CHUNKS = 4
LOADS = 8
UNITS = 2
BLOCKS_PER_STEP = 8


PLAN = (
    ("across", 0, 0, ()),
    ("along", 1, 0, ()),
    ("across", 0, 1, ()),
    ("along", 1, 1, ()),
    ("across", 1, 0, (("across", 0, 0),)),
    ("along", 2, 0, (("along", 1, 0),)),
    ("across", 1, 1, (("across", 0, 1),)),
    ("along", 3, 0, (("along", 1, 1),)),
    ("across", 2, 0, (("across", 1, 0),)),
    ("along", 2, 1, (("along", 2, 0),)),
    ("across", 3, 0, (("across", 1, 1),)),
    ("across", 2, 1, (("across", 2, 0), ("across", 1, 1))),
    ("down", 3, 1, (("along", 3, 0),)),
    ("along", 3, 1, (("along", 2, 1),)),
)


def norm_project_kernel(
    x_hbm, gain_ref, key_hbm, value_hbm, scale_ref, kv_ref,
    x_scr, weight_scr, even_scr, odd_scr, acc_scr, x_sem, key_sem, value_sem,
):
    loads, rows, chunk = x_scr.shape
    width = weight_scr.shape[2] // 2
    lanes = 128
    band = 128

    def span(c):
        return pl.ds(pl.multiple_of(c * chunk, chunk), chunk)

    def load_x(c):
        return pltpu.make_async_copy(x_hbm.at[:, span(c)], x_scr.at[c], x_sem.at[c])

    def load_weights(c):
        head = pl.ds(0, width)
        return [
            pltpu.make_async_copy(
                key_hbm.at[span(c), head], weight_scr.at[c, :, pl.ds(0, width)], key_sem.at[c]
            ),
            pltpu.make_async_copy(
                value_hbm.at[span(c), head], weight_scr.at[c, :, pl.ds(width, width)], value_sem.at[c]
            ),
        ]

    for c in range(loads):
        load_x(c).start()
    scale_ref[...] = jnp.zeros_like(scale_ref)

    def square(c, carry):
        load_x(c).wait()

        @pl.when(c >= loads // 2)
        def _():
            for part in range(2):
                for copy in load_weights(2 * (c - loads // 2) + part):
                    copy.start()

        for first in range(0, rows, band):
            row = slice(first, first + band)
            total = scale_ref[row, :]
            for lane in range(0, chunk, lanes):
                x = x_scr[c, row, lane : lane + lanes].astype(jnp.float32)
                total += x * x
            scale_ref[row, :] = total
        return carry

    lax.fori_loop(0, loads, square, 0)
    mean_sq = jnp.sum(scale_ref[...], axis=-1, keepdims=True) / (loads * chunk)
    scale_ref[...] = jnp.broadcast_to(lax.rsqrt(mean_sq + EPS), scale_ref.shape)

    def normalise(normed_scr, c):
        for first in range(0, rows, band):
            row = slice(first, first + band)
            inverse = scale_ref[row, :]
            for lane in range(0, chunk, lanes):
                cols = slice(lane, lane + lanes)
                x = x_scr[c, row, cols].astype(jnp.float32)
                gain = gain_ref[c, :, cols]
                normed_scr[row, cols] = (x * inverse * gain).astype(jnp.bfloat16)

    def multiply(normed_scr, c):
        for copy in load_weights(c):
            copy.wait()
        acc_scr[...] += jnp.dot(
            normed_scr[...], weight_scr[c], preferred_element_type=jnp.float32
        )

    normalise(even_scr, 0)
    acc_scr[...] = jnp.zeros_like(acc_scr)

    def pair(p, carry):
        multiply(even_scr, 2 * p)
        normalise(odd_scr, 2 * p + 1)
        multiply(odd_scr, 2 * p + 1)
        normalise(even_scr, 2 * p + 2)
        return carry

    lax.fori_loop(0, loads // 2 - 1, pair, 0)
    multiply(even_scr, loads - 2)
    normalise(odd_scr, loads - 1)
    multiply(odd_scr, loads - 1)
    write_heads(kv_ref, acc_scr)


def write_heads(kv_ref, acc_scr):
    heads = kv_ref.shape[0]
    for head in range(heads):
        for part in range(2):
            first = (part * heads + head) * HEAD_DIM
            source = acc_scr[:, first : first + HEAD_DIM]
            kv_ref[head, :, part * HEAD_DIM : (part + 1) * HEAD_DIM] = source.astype(jnp.bfloat16)


def norm_project(hidden, gain, key_weight, value_weight):
    rows, features = hidden.shape
    width = key_weight.shape[1] // UNITS
    chunk = features // LOADS
    whole = pl.BlockSpec(memory_space=pltpu.VMEM)
    held = pl.BlockSpec(memory_space=pltpu.HBM)
    return pl.pallas_call(
        norm_project_kernel,
        in_specs=[held, whole, held, held],
        out_specs=[whole, whole],
        out_shape=[
            jax.ShapeDtypeStruct((rows, 128), jnp.float32),
            jax.ShapeDtypeStruct((width // HEAD_DIM, rows, 2 * HEAD_DIM), jnp.bfloat16),
        ],
        scratch_shapes=[
            pltpu.VMEM((LOADS, rows, chunk), jnp.bfloat16),
            pltpu.VMEM((LOADS, chunk, 2 * width), jnp.bfloat16),
            pltpu.VMEM((rows, chunk), jnp.bfloat16),
            pltpu.VMEM((rows, chunk), jnp.bfloat16),
            pltpu.VMEM((rows, 2 * width), jnp.float32),
            pltpu.SemaphoreType.DMA((LOADS,)),
            pltpu.SemaphoreType.DMA((LOADS,)),
            pltpu.SemaphoreType.DMA((LOADS,)),
        ],
        compiler_params=pltpu.CompilerParams(vmem_limit_bytes=57 * MIB),
        cost_estimate=pl.CostEstimate(
            flops=4 * rows * features * width, bytes_accessed=16 * MIB, transcendentals=0
        ),
        name="norm_project",
    )(hidden, gain.reshape(LOADS, 1, chunk), key_weight, value_weight)


def project_kernel(x_ref, scale_ref, gain_ref, key_ref, value_ref, kv_ref, acc_scr):
    step = pl.program_id(0)
    rows, chunk = x_ref.shape
    width = key_ref.shape[1]
    lanes = 128
    inverse = scale_ref[...]
    parts = []
    for lane in range(0, chunk, lanes):
        cols = slice(lane, lane + lanes)
        x = x_ref[:, cols].astype(jnp.float32)
        parts.append((x * inverse * gain_ref[:, cols]).astype(jnp.bfloat16))
    normed = jnp.concatenate(parts, axis=1)
    for part, weight in enumerate((key_ref, value_ref)):
        cols = slice(part * width, (part + 1) * width)
        term = jnp.dot(normed, weight[...], preferred_element_type=jnp.float32)
        acc_scr[:, cols] = jnp.where(step == 0, term, acc_scr[:, cols] + term)

    @pl.when(step == CHUNKS - 1)
    def _():
        write_heads(kv_ref, acc_scr)


def project(hidden, scale, gain, key_weight, value_weight, unit):
    rows, features = hidden.shape
    chunk = features // CHUNKS
    width = key_weight.shape[1] // UNITS
    weight = pl.BlockSpec((chunk, width), lambda i: (i, unit))
    return pl.pallas_call(
        project_kernel,
        grid=(CHUNKS,),
        in_specs=[
            pl.BlockSpec((rows, chunk), lambda i: (0, i)),
            pl.BlockSpec(scale.shape, lambda i: (0, 0)),
            pl.BlockSpec((1, chunk), lambda i: (0, i)),
            weight,
            weight,
        ],
        out_specs=pl.BlockSpec((width // HEAD_DIM, rows, 2 * HEAD_DIM), lambda i: (0, 0, 0)),
        out_shape=jax.ShapeDtypeStruct((width // HEAD_DIM, rows, 2 * HEAD_DIM), jnp.bfloat16),
        scratch_shapes=[pltpu.VMEM((rows, 2 * width), jnp.float32)],
        compiler_params=pltpu.CompilerParams(vmem_limit_bytes=57 * MIB),
        cost_estimate=pl.CostEstimate(
            flops=4 * rows * features * width, bytes_accessed=16 * MIB, transcendentals=0
        ),
        name="project",
    )(hidden, scale, gain.reshape(1, features), key_weight, value_weight)


def attention_kernel(block, unit, near, slot_ref, cut_ref, odd_ref, q_hbm, *refs):
    own_hbm, straight, crossed = refs[0], refs[1 : near + 1], refs[near + 1 : 2 * near + 2]
    out_hbm, kv_scr, q_scr, out_scr, kv_sem, q_sem, out_sem = refs[-7:]
    kv_heads, levels, rows, width = kv_scr.shape
    depth = levels - 1
    steps, tall, wide = q_scr.shape
    per_head = steps // kv_heads
    per_group = wide // HEAD_DIM
    scale = HEAD_DIM**-0.5 * LOG2E

    def load_kv(head):
        def copy(ref, level, number):
            return pltpu.make_async_copy(
                ref.at[head],
                kv_scr.at[head, level],
                kv_sem.at[head, number],
            )

        copies = [copy(own_hbm, depth, 0)]
        for s, ref in enumerate(straight):
            copies.append(copy(ref, 2 * s + 1, s + 1))
        for s, ref in enumerate(crossed):
            level = 2 * lax.rem(s + odd_ref[0] + near, near + 1)
            copies.append(copy(ref, level, near + s + 1))
        return copies

    def place(ref, step):
        head, part = lax.div(step, per_head), lax.rem(step, per_head)
        span = pl.ds(pl.multiple_of(part * tall, tall), tall)
        cols = pl.ds(pl.multiple_of((unit * kv_heads + head) * wide, wide), wide)
        return ref.at[span, cols]

    def load_q(step):
        return pltpu.make_async_copy(place(q_hbm, step), q_scr.at[step], q_sem.at[step])

    def store(step):
        return pltpu.make_async_copy(out_scr.at[step], place(out_hbm, step), out_sem.at[step])

    for head in range(kv_heads):
        for copy in load_kv(head):
            copy.start()
        for step in range(head * per_head, (head + 1) * per_head):
            load_q(step).start()

    token = lax.broadcasted_iota(jnp.int32, (block, HEAD_DIM), 0)
    lane = lax.broadcasted_iota(jnp.int32, (block, HEAD_DIM), 1)
    hidden_later = jnp.where((lane >= block) & (lane - block > token), MASKED, 0.0)
    query_mask = jnp.where(lane == 0, 1.0, hidden_later).astype(jnp.bfloat16)
    query_mask = jnp.concatenate([query_mask] * per_group, axis=0)
    own_mask = jnp.where(lane - block == token, 1.0, 0.0).astype(jnp.bfloat16)

    def score(step, local):
        head = lax.div(step, per_head)
        here = lax.rem(step, per_head) * BLOCKS_PER_STEP + local
        pieces, masks = [], []
        for k in range(depth):
            span = pl.ds(pl.multiple_of(slot_ref[here, k] * block, block), block)
            pieces.append(kv_scr[head, k, span, :])
            unseen = (lane == 0) & (token >= cut_ref[here, k])
            masks.append(jnp.where(unseen, MASKED, 0.0).astype(jnp.bfloat16))
        span = pl.ds(pl.multiple_of(here * block, block), block)
        pieces.append(kv_scr[head, depth, span, :])
        masks.append(own_mask)
        every = jnp.concatenate(pieces, axis=0)
        keys = jnp.concatenate([every[:, :HEAD_DIM], jnp.concatenate(masks, axis=0)], axis=1)
        span = slice(local * block, (local + 1) * block)
        queries = jnp.concatenate(
            [q_scr[step, span, r * HEAD_DIM : (r + 1) * HEAD_DIM] for r in range(per_group)], axis=0
        )
        queries = jnp.concatenate([queries, query_mask], axis=1)
        scores = lax.dot_general(
            queries, keys, (((1,), (1,)), ((), ())), preferred_element_type=jnp.float32
        )
        return scores, every[:, HEAD_DIM:]

    def finish(step, local, scores, values):
        peak = jnp.max(scores, axis=-1, keepdims=True)
        weights = jnp.exp2((scores - peak) * scale).astype(jnp.bfloat16)
        padded = jnp.concatenate([values, jnp.ones_like(values)], axis=1)
        both = jnp.dot(weights, padded, preferred_element_type=jnp.float32)
        context = (both[:, :HEAD_DIM] * (1.0 / both[:, HEAD_DIM:])).astype(jnp.bfloat16)
        span = slice(local * block, (local + 1) * block)
        for r in range(per_group):
            out_scr[step, span, r * HEAD_DIM : (r + 1) * HEAD_DIM] = context[
                r * block : (r + 1) * block
            ]

    def body(step, carry):
        load_q(step).wait()
        for head in range(kv_heads):

            @pl.when(step == head * per_head)
            def _(head=head):
                for copy in load_kv(head):
                    copy.wait()

        waiting = None
        for local in range(BLOCKS_PER_STEP):
            scores, values = score(step, local)
            if waiting is not None:
                finish(step, *waiting)
            waiting = (local, scores, values)
        finish(step, *waiting)
        store(step).start()
        return carry

    lax.fori_loop(0, steps, body, 0)
    for step in range(steps):
        store(step).wait()


def attention(slots, cuts, odd, queries, own, straight, crossed, unit, previous):
    rows, features = queries.shape
    blocks, depth = slots.shape
    block = rows // blocks
    near = len(straight)
    kv_heads = own.shape[0]
    wide = features // UNITS // kv_heads
    steps = kv_heads * blocks // BLOCKS_PER_STEP
    held = pl.BlockSpec(memory_space=pltpu.HBM)
    table = pl.BlockSpec(memory_space=pltpu.SMEM)
    operands = [slots, cuts, odd, queries, own, *straight, *crossed]
    aliases = {}
    if previous is not None:
        aliases = {len(operands): 0}
        operands.append(previous)
    return pl.pallas_call(
        functools.partial(attention_kernel, block, unit, near),
        in_specs=[table] * 3 + [held] * (len(operands) - 3),
        out_specs=held,
        out_shape=jax.ShapeDtypeStruct((rows, features), jnp.bfloat16),
        input_output_aliases=aliases,
        scratch_shapes=[
            pltpu.VMEM((kv_heads, depth + 1, rows, 2 * HEAD_DIM), own.dtype),
            pltpu.VMEM((steps, BLOCKS_PER_STEP * block, wide), jnp.bfloat16),
            pltpu.VMEM((steps, BLOCKS_PER_STEP * block, wide), jnp.bfloat16),
            pltpu.SemaphoreType.DMA((kv_heads, depth + 1)),
            pltpu.SemaphoreType.DMA((steps,)),
            pltpu.SemaphoreType.DMA((steps,)),
        ],
        compiler_params=pltpu.CompilerParams(vmem_limit_bytes=57 * MIB),
        cost_estimate=pl.CostEstimate(
            flops=4 * rows * wide * kv_heads * (depth + 1) * block,
            bytes_accessed=8 * MIB,
            transcendentals=rows * wide // HEAD_DIM * kv_heads * (depth + 1) * block,
        ),
        name="attention",
    )(*operands)


def shards(hidden, queries, norm_gain, key_weight, value_weight, anc_ids, anc_cut):
    blocks, depth = anc_ids.shape
    levels = depth + 1
    size = lax.axis_size("node")
    chains = size // levels
    near = depth // 2
    half = [index // chains // 2 for index in range(size)]
    even = [index // chains % 2 == 0 for index in range(size)]
    other = [index + chains if even[index] else index - chains for index in range(size)]
    odd = (lax.axis_index("node") // chains % 2).astype(jnp.int32).reshape(1)
    slots = jnp.where(anc_ids >= 0, anc_ids % blocks, 0)

    scale, first = norm_project(hidden, norm_gain, key_weight, value_weight)
    own = [first, project(hidden, scale, norm_gain, key_weight, value_weight, 1)]
    def after(array, *earlier):
        return lax.optimization_barrier((array, *earlier))[0]

    column = 2 * chains
    moved = {("own", 0, 0): own[0], ("own", 0, 1): own[1]}

    def step(kind, s, unit, waits):
        if kind == "across":
            source = ("along", s, unit) if s else ("own", 0, unit)
            exchange = s > 0 or unit == UNITS - 1
            pairs = [
                (i, other[i])
                for i in range(size)
                if half[i] >= s and (even[i] or (exchange and half[i] == 0) or s > 0)
            ]
        elif kind == "along":
            source = ("along", s - 1, unit) if s > 1 else ("own", 0, unit)
            pairs = [(i, i + column) for i in range(size - column) if half[i] >= s - 1]
        else:
            source = ("across" if kind == "down" else "own", 0, unit)
            pairs = [(i, i + s * column) for i in range(size - s * column)]
        array = lax.optimization_barrier((moved[source], *[moved[w] for w in waits]))[0]
        key = "along" if kind == "direct" else kind
        moved[key, s, unit] = lax.ppermute(array, "node", pairs)

    for kind, s, unit, waits in PLAN:
        step(kind, s, unit, waits)
    result = None
    for unit in range(UNITS):
        result = attention(
            slots,
            anc_cut,
            odd,
            queries,
            own[unit],
            [moved["along", s, unit] for s in range(1, near + 1)],
            [moved["across", s, unit] for s in range(near)]
            + [moved["across" if unit == 0 else "down", near, unit]],
            unit,
            result,
        )
    return result


def solution(mesh):
    placed = (
        P(("groups", "node"), None),
        P(("groups", "node"), None),
        P(),
        P(),
        P(),
        P(("groups", "node"), None),
        P(("groups", "node"), None),
    )
    return jax.shard_map(
        shards, mesh=mesh, in_specs=placed, out_specs=P(("groups", "node"), None), check_vma=False
    )
```

```python
import functools
import jax
import jax.numpy as jnp
from jax import lax
from jax.experimental import pallas as pl
from jax.experimental.pallas import tpu as pltpu
from jax.sharding import PartitionSpec as P

HEAD_DIM = 128
EPS = 1e-05
LOG2E = 1.4426950408889634
MASKED = -1e30
MIB = 1024 * 1024
CHUNKS = 4
LOADS = 8
UNITS = 2
BLOCKS_PER_STEP = 8


PLAN = (
    ("across", 0, 0, ()),
    ("along", 1, 0, ()),
    ("across", 0, 1, ()),
    ("along", 1, 1, ()),
    ("across", 1, 0, (("across", 0, 0),)),
    ("along", 2, 0, (("along", 1, 0),)),
    ("across", 1, 1, (("across", 0, 1),)),
    ("along", 3, 0, (("along", 1, 1),)),
    ("across", 2, 0, (("across", 1, 0),)),
    ("along", 2, 1, (("along", 2, 0),)),
    ("across", 3, 0, (("across", 1, 1),)),
    ("across", 2, 1, (("across", 2, 0), ("across", 1, 1))),
    ("down", 3, 1, (("along", 3, 0),)),
    ("along", 3, 1, (("along", 2, 1),)),
)


def norm_project_kernel(
    x_hbm, gain_ref, key_hbm, value_hbm, scale_ref, kv_ref,
    x_scr, weight_scr, even_scr, odd_scr, acc_scr, x_sem, key_sem, value_sem,
):
    rows, features = x_scr.shape
    loads = LOADS
    tall = rows // loads
    chunks, chunk = weight_scr.shape[:2]
    width = weight_scr.shape[2] // 2
    lanes = 128
    band = 128

    def span(c):
        return pl.ds(pl.multiple_of(c * chunk, chunk), chunk)

    def load_x(c):
        row = pl.ds(pl.multiple_of(c * tall, tall), tall)
        return pltpu.make_async_copy(x_hbm.at[row], x_scr.at[row], x_sem.at[c])

    def load_weights(c):
        head = pl.ds(0, width)
        return [
            pltpu.make_async_copy(
                key_hbm.at[span(c), head], weight_scr.at[c, :, pl.ds(0, width)], key_sem.at[c]
            ),
            pltpu.make_async_copy(
                value_hbm.at[span(c), head], weight_scr.at[c, :, pl.ds(width, width)], value_sem.at[c]
            ),
        ]

    for c in range(loads):
        load_x(c).start()
    for c in range(chunks):
        for copy in load_weights(c):
            copy.start()

    def square(c, carry):
        load_x(c).wait()

        row = pl.ds(pl.multiple_of(c * tall, tall), tall)
        total = jnp.zeros((tall, lanes), jnp.float32)
        for lane in range(0, features, lanes):
            x = x_scr[row, lane : lane + lanes].astype(jnp.float32)
            total += x * x
        scale_ref[row, :] = total
        return carry

    lax.fori_loop(0, loads, square, 0)
    mean_sq = jnp.sum(scale_ref[...], axis=-1, keepdims=True) / features
    scale_ref[...] = jnp.broadcast_to(lax.rsqrt(mean_sq + EPS), scale_ref.shape)

    def normalise(normed_scr, c):
        for first in range(0, rows, band):
            row = slice(first, first + band)
            inverse = scale_ref[row, :]
            for lane in range(0, chunk, lanes):
                cols = pl.ds(pl.multiple_of(c * chunk + lane, lanes), lanes)
                x = x_scr[row, cols].astype(jnp.float32)
                normed_scr[row, lane : lane + lanes] = (
                    x * inverse * gain_ref[:, cols]
                ).astype(jnp.bfloat16)

    def multiply(normed_scr, c):
        for copy in load_weights(c):
            copy.wait()
        return jnp.dot(normed_scr[...], weight_scr[c], preferred_element_type=jnp.float32)

    normalise(even_scr, 0)
    acc_scr[...] = multiply(even_scr, 0)
    normalise(odd_scr, 1)

    def pair(p, carry):
        acc_scr[...] += multiply(odd_scr, 2 * p + 1)
        normalise(even_scr, 2 * p + 2)
        acc_scr[...] += multiply(even_scr, 2 * p + 2)
        normalise(odd_scr, 2 * p + 3)
        return carry

    lax.fori_loop(0, chunks // 2 - 1, pair, 0)
    acc_scr[...] += multiply(odd_scr, chunks - 1)
    write_heads(kv_ref, acc_scr)


def write_heads(kv_ref, acc_scr):
    heads = kv_ref.shape[0]
    for head in range(heads):
        for part in range(2):
            first = (part * heads + head) * HEAD_DIM
            source = acc_scr[:, first : first + HEAD_DIM]
            kv_ref[head, :, part * HEAD_DIM : (part + 1) * HEAD_DIM] = source.astype(jnp.bfloat16)


def norm_project(hidden, gain, key_weight, value_weight):
    rows, features = hidden.shape
    width = key_weight.shape[1] // UNITS
    chunk = features // CHUNKS
    whole = pl.BlockSpec(memory_space=pltpu.VMEM)
    held = pl.BlockSpec(memory_space=pltpu.HBM)
    return pl.pallas_call(
        norm_project_kernel,
        in_specs=[held, whole, held, held],
        out_specs=[whole, whole],
        out_shape=[
            jax.ShapeDtypeStruct((rows, 128), jnp.float32),
            jax.ShapeDtypeStruct((width // HEAD_DIM, rows, 2 * HEAD_DIM), jnp.bfloat16),
        ],
        scratch_shapes=[
            pltpu.VMEM((rows, features), jnp.bfloat16),
            pltpu.VMEM((CHUNKS, chunk, 2 * width), jnp.bfloat16),
            pltpu.VMEM((rows, chunk), jnp.bfloat16),
            pltpu.VMEM((rows, chunk), jnp.bfloat16),
            pltpu.VMEM((rows, 2 * width), jnp.float32),
            pltpu.SemaphoreType.DMA((LOADS,)),
            pltpu.SemaphoreType.DMA((CHUNKS,)),
            pltpu.SemaphoreType.DMA((CHUNKS,)),
        ],
        compiler_params=pltpu.CompilerParams(vmem_limit_bytes=57 * MIB),
        cost_estimate=pl.CostEstimate(
            flops=4 * rows * features * width, bytes_accessed=16 * MIB, transcendentals=0
        ),
        name="norm_project",
    )(hidden, gain.reshape(1, features), key_weight, value_weight)


def project_kernel(x_ref, scale_ref, gain_ref, key_ref, value_ref, kv_ref, acc_scr):
    step = pl.program_id(0)
    rows, chunk = x_ref.shape
    width = key_ref.shape[1]
    lanes = 128
    inverse = scale_ref[...]
    parts = []
    for lane in range(0, chunk, lanes):
        cols = slice(lane, lane + lanes)
        x = x_ref[:, cols].astype(jnp.float32)
        parts.append((x * inverse * gain_ref[:, cols]).astype(jnp.bfloat16))
    normed = jnp.concatenate(parts, axis=1)
    for part, weight in enumerate((key_ref, value_ref)):
        cols = slice(part * width, (part + 1) * width)
        term = jnp.dot(normed, weight[...], preferred_element_type=jnp.float32)
        acc_scr[:, cols] = jnp.where(step == 0, term, acc_scr[:, cols] + term)

    @pl.when(step == CHUNKS - 1)
    def _():
        write_heads(kv_ref, acc_scr)


def project(hidden, scale, gain, key_weight, value_weight, unit):
    rows, features = hidden.shape
    chunk = features // CHUNKS
    width = key_weight.shape[1] // UNITS
    weight = pl.BlockSpec((chunk, width), lambda i: (i, unit))
    return pl.pallas_call(
        project_kernel,
        grid=(CHUNKS,),
        in_specs=[
            pl.BlockSpec((rows, chunk), lambda i: (0, i)),
            pl.BlockSpec(scale.shape, lambda i: (0, 0)),
            pl.BlockSpec((1, chunk), lambda i: (0, i)),
            weight,
            weight,
        ],
        out_specs=pl.BlockSpec((width // HEAD_DIM, rows, 2 * HEAD_DIM), lambda i: (0, 0, 0)),
        out_shape=jax.ShapeDtypeStruct((width // HEAD_DIM, rows, 2 * HEAD_DIM), jnp.bfloat16),
        scratch_shapes=[pltpu.VMEM((rows, 2 * width), jnp.float32)],
        compiler_params=pltpu.CompilerParams(vmem_limit_bytes=57 * MIB),
        cost_estimate=pl.CostEstimate(
            flops=4 * rows * features * width, bytes_accessed=16 * MIB, transcendentals=0
        ),
        name="project",
    )(hidden, scale, gain.reshape(1, features), key_weight, value_weight)


def attention_kernel(block, unit, near, slot_ref, cut_ref, odd_ref, q_hbm, *refs):
    own_hbm, straight, crossed = refs[0], refs[1 : near + 1], refs[near + 1 : 2 * near + 2]
    out_hbm, kv_scr, q_scr, out_scr, kv_sem, q_sem, out_sem = refs[-7:]
    kv_heads, levels, rows, width = kv_scr.shape
    depth = levels - 1
    steps, tall, wide = q_scr.shape
    per_head = steps // kv_heads
    per_group = wide // HEAD_DIM
    scale = HEAD_DIM**-0.5 * LOG2E

    def load_kv(head):
        def copy(ref, level, number):
            return pltpu.make_async_copy(
                ref.at[head],
                kv_scr.at[head, level],
                kv_sem.at[head, number],
            )

        copies = [copy(own_hbm, depth, 0)]
        for s, ref in enumerate(straight):
            copies.append(copy(ref, 2 * s + 1, s + 1))
        for s, ref in enumerate(crossed):
            level = 2 * lax.rem(s + odd_ref[0] + near, near + 1)
            copies.append(copy(ref, level, near + s + 1))
        return copies

    def place(ref, step):
        head, part = lax.div(step, per_head), lax.rem(step, per_head)
        span = pl.ds(pl.multiple_of(part * tall, tall), tall)
        cols = pl.ds(pl.multiple_of((unit * kv_heads + head) * wide, wide), wide)
        return ref.at[span, cols]

    def load_q(step):
        return pltpu.make_async_copy(place(q_hbm, step), q_scr.at[step], q_sem.at[step])

    def store(step):
        return pltpu.make_async_copy(out_scr.at[step], place(out_hbm, step), out_sem.at[step])

    for head in range(kv_heads):
        for copy in load_kv(head):
            copy.start()
        for step in range(head * per_head, (head + 1) * per_head):
            load_q(step).start()

    token = lax.broadcasted_iota(jnp.int32, (block, HEAD_DIM), 0)
    lane = lax.broadcasted_iota(jnp.int32, (block, HEAD_DIM), 1)
    hidden_later = jnp.where((lane >= block) & (lane - block > token), MASKED, 0.0)
    query_mask = jnp.where(lane == 0, 1.0, hidden_later).astype(jnp.bfloat16)
    query_mask = jnp.concatenate([query_mask] * per_group, axis=0)
    own_mask = jnp.where(lane - block == token, 1.0, 0.0).astype(jnp.bfloat16)

    def score(step, local):
        head = lax.div(step, per_head)
        here = lax.rem(step, per_head) * BLOCKS_PER_STEP + local
        pieces, masks = [], []
        for k in range(depth):
            span = pl.ds(pl.multiple_of(slot_ref[here, k] * block, block), block)
            pieces.append(kv_scr[head, k, span, :])
            unseen = (lane == 0) & (token >= cut_ref[here, k])
            masks.append(jnp.where(unseen, MASKED, 0.0).astype(jnp.bfloat16))
        span = pl.ds(pl.multiple_of(here * block, block), block)
        pieces.append(kv_scr[head, depth, span, :])
        masks.append(own_mask)
        every = jnp.concatenate(pieces, axis=0)
        keys = jnp.concatenate([every[:, :HEAD_DIM], jnp.concatenate(masks, axis=0)], axis=1)
        span = slice(local * block, (local + 1) * block)
        queries = jnp.concatenate(
            [q_scr[step, span, r * HEAD_DIM : (r + 1) * HEAD_DIM] for r in range(per_group)], axis=0
        )
        queries = jnp.concatenate([queries, query_mask], axis=1)
        scores = lax.dot_general(
            queries, keys, (((1,), (1,)), ((), ())), preferred_element_type=jnp.float32
        )
        return scores, every[:, HEAD_DIM:]

    def finish(step, local, scores, values):
        peak = jnp.max(scores, axis=-1, keepdims=True)
        weights = jnp.exp2((scores - peak) * scale).astype(jnp.bfloat16)
        padded = jnp.concatenate([values, jnp.ones_like(values)], axis=1)
        both = jnp.dot(weights, padded, preferred_element_type=jnp.float32)
        context = (both[:, :HEAD_DIM] * (1.0 / both[:, HEAD_DIM:])).astype(jnp.bfloat16)
        span = slice(local * block, (local + 1) * block)
        for r in range(per_group):
            out_scr[step, span, r * HEAD_DIM : (r + 1) * HEAD_DIM] = context[
                r * block : (r + 1) * block
            ]

    def body(step, carry):
        load_q(step).wait()
        for head in range(kv_heads):

            @pl.when(step == head * per_head)
            def _(head=head):
                for copy in load_kv(head):
                    copy.wait()

        waiting = None
        for local in range(BLOCKS_PER_STEP):
            scores, values = score(step, local)
            if waiting is not None:
                finish(step, *waiting)
            waiting = (local, scores, values)
        finish(step, *waiting)
        store(step).start()
        return carry

    lax.fori_loop(0, steps, body, 0)
    for step in range(steps):
        store(step).wait()


def attention(slots, cuts, odd, queries, own, straight, crossed, unit, previous):
    rows, features = queries.shape
    blocks, depth = slots.shape
    block = rows // blocks
    near = len(straight)
    kv_heads = own.shape[0]
    wide = features // UNITS // kv_heads
    steps = kv_heads * blocks // BLOCKS_PER_STEP
    held = pl.BlockSpec(memory_space=pltpu.HBM)
    table = pl.BlockSpec(memory_space=pltpu.SMEM)
    operands = [slots, cuts, odd, queries, own, *straight, *crossed]
    aliases = {}
    if previous is not None:
        aliases = {len(operands): 0}
        operands.append(previous)
    return pl.pallas_call(
        functools.partial(attention_kernel, block, unit, near),
        in_specs=[table] * 3 + [held] * (len(operands) - 3),
        out_specs=held,
        out_shape=jax.ShapeDtypeStruct((rows, features), jnp.bfloat16),
        input_output_aliases=aliases,
        scratch_shapes=[
            pltpu.VMEM((kv_heads, depth + 1, rows, 2 * HEAD_DIM), own.dtype),
            pltpu.VMEM((steps, BLOCKS_PER_STEP * block, wide), jnp.bfloat16),
            pltpu.VMEM((steps, BLOCKS_PER_STEP * block, wide), jnp.bfloat16),
            pltpu.SemaphoreType.DMA((kv_heads, depth + 1)),
            pltpu.SemaphoreType.DMA((steps,)),
            pltpu.SemaphoreType.DMA((steps,)),
        ],
        compiler_params=pltpu.CompilerParams(vmem_limit_bytes=57 * MIB),
        cost_estimate=pl.CostEstimate(
            flops=4 * rows * wide * kv_heads * (depth + 1) * block,
            bytes_accessed=8 * MIB,
            transcendentals=rows * wide // HEAD_DIM * kv_heads * (depth + 1) * block,
        ),
        name="attention",
    )(*operands)


def shards(hidden, queries, norm_gain, key_weight, value_weight, anc_ids, anc_cut):
    blocks, depth = anc_ids.shape
    levels = depth + 1
    size = lax.axis_size("node")
    chains = size // levels
    near = depth // 2
    half = [index // chains // 2 for index in range(size)]
    even = [index // chains % 2 == 0 for index in range(size)]
    other = [index + chains if even[index] else index - chains for index in range(size)]
    odd = (lax.axis_index("node") // chains % 2).astype(jnp.int32).reshape(1)
    slots = jnp.where(anc_ids >= 0, anc_ids % blocks, 0)

    scale, first = norm_project(hidden, norm_gain, key_weight, value_weight)
    own = [first, project(hidden, scale, norm_gain, key_weight, value_weight, 1)]
    def after(array, *earlier):
        return lax.optimization_barrier((array, *earlier))[0]

    column = 2 * chains
    moved = {("own", 0, 0): own[0], ("own", 0, 1): own[1]}

    def step(kind, s, unit, waits):
        if kind == "across":
            source = ("along", s, unit) if s else ("own", 0, unit)
            exchange = s > 0 or unit == UNITS - 1
            pairs = [
                (i, other[i])
                for i in range(size)
                if half[i] >= s and (even[i] or (exchange and half[i] == 0) or s > 0)
            ]
        elif kind == "along":
            source = ("along", s - 1, unit) if s > 1 else ("own", 0, unit)
            pairs = [(i, i + column) for i in range(size - column) if half[i] >= s - 1]
        else:
            source = ("across" if kind == "down" else "own", 0, unit)
            pairs = [(i, i + s * column) for i in range(size - s * column)]
        array = lax.optimization_barrier((moved[source], *[moved[w] for w in waits]))[0]
        key = "along" if kind == "direct" else kind
        moved[key, s, unit] = lax.ppermute(array, "node", pairs)

    for kind, s, unit, waits in PLAN:
        step(kind, s, unit, waits)
    result = None
    for unit in range(UNITS):
        result = attention(
            slots,
            anc_cut,
            odd,
            queries,
            own[unit],
            [moved["along", s, unit] for s in range(1, near + 1)],
            [moved["across", s, unit] for s in range(near)]
            + [moved["across" if unit == 0 else "down", near, unit]],
            unit,
            result,
        )
    return result


def solution(mesh):
    placed = (
        P(("groups", "node"), None),
        P(("groups", "node"), None),
        P(),
        P(),
        P(),
        P(("groups", "node"), None),
        P(("groups", "node"), None),
    )
    return jax.shard_map(
        shards, mesh=mesh, in_specs=placed, out_specs=P(("groups", "node"), None), check_vma=False
    )
```

```python
import functools
import jax
import jax.numpy as jnp
from jax import lax
from jax.experimental import pallas as pl
from jax.experimental.pallas import tpu as pltpu
from jax.sharding import PartitionSpec as P

HEAD_DIM = 128
EPS = 1e-05
LOG2E = 1.4426950408889634
MASKED = -1e30
MIB = 1024 * 1024
CHUNKS = 4
LOADS = 8
UNITS = 2
BLOCKS_PER_STEP = 8


PLAN = (
    ("across", 0, 0, ()),
    ("along", 1, 0, ()),
    ("across", 0, 1, ()),
    ("along", 1, 1, ()),
    ("across", 1, 0, (("across", 0, 0),)),
    ("along", 2, 0, (("along", 1, 0),)),
    ("across", 1, 1, (("across", 0, 1),)),
    ("along", 3, 0, (("along", 1, 1),)),
    ("across", 2, 0, (("across", 1, 0),)),
    ("along", 2, 1, (("along", 2, 0),)),
    ("across", 3, 0, (("across", 1, 1),)),
    ("across", 2, 1, (("across", 2, 0), ("across", 1, 1))),
    ("down", 3, 1, (("along", 3, 0),)),
    ("along", 3, 1, (("along", 2, 1),)),
)


def norm_project_kernel(
    x_hbm, gain_ref, key_hbm, value_hbm, scale_ref, kv_ref,
    x_scr, weight_scr, acc_scr, x_sem, key_sem, value_sem,
):
    rows, features = x_scr.shape
    loads = LOADS
    tall = rows // loads
    chunks, chunk = weight_scr.shape[:2]
    width = weight_scr.shape[2] // 2
    lanes = 128

    def span(c):
        return pl.ds(pl.multiple_of(c * chunk, chunk), chunk)

    def load_x(c):
        row = pl.ds(pl.multiple_of(c * tall, tall), tall)
        return pltpu.make_async_copy(x_hbm.at[row], x_scr.at[row], x_sem.at[c])

    def load_weights(c):
        head = pl.ds(0, width)
        return [
            pltpu.make_async_copy(
                key_hbm.at[span(c), head], weight_scr.at[c, :, pl.ds(0, width)], key_sem.at[c]
            ),
            pltpu.make_async_copy(
                value_hbm.at[span(c), head], weight_scr.at[c, :, pl.ds(width, width)], value_sem.at[c]
            ),
        ]

    for c in range(loads):
        load_x(c).start()

    def square(c, carry):
        load_x(c).wait()

        @pl.when(c == loads - 2)
        def _():
            for copy in load_weights(0):
                copy.start()

        row = pl.ds(pl.multiple_of(c * tall, tall), tall)
        total = jnp.zeros((tall, lanes), jnp.float32)
        for lane in range(0, features, lanes):
            x = x_scr[row, lane : lane + lanes].astype(jnp.float32)
            total += x * x
        scale_ref[row, :] = total
        return carry

    lax.fori_loop(0, loads, square, 0)
    for c in range(1, chunks):
        for copy in load_weights(c):
            copy.start()
    mean_sq = jnp.sum(scale_ref[...], axis=-1, keepdims=True) / features
    scale_ref[...] = jnp.broadcast_to(lax.rsqrt(mean_sq + EPS), scale_ref.shape)

    acc_scr[...] = jnp.zeros_like(acc_scr)

    def multiply(c, carry):
        for copy in load_weights(c):
            copy.wait()
        inverse = scale_ref[...]
        parts = []
        for lane in range(0, chunk, lanes):
            cols = pl.ds(pl.multiple_of(c * chunk + lane, lanes), lanes)
            x = x_scr[:, cols].astype(jnp.float32)
            parts.append((x * inverse * gain_ref[:, cols]).astype(jnp.bfloat16))
        normed = jnp.concatenate(parts, axis=1)
        for part in range(2):
            cols = slice(part * width, (part + 1) * width)
            acc_scr[:, cols] += jnp.dot(
                normed, weight_scr[c, :, cols], preferred_element_type=jnp.float32
            )
        return carry

    lax.fori_loop(0, chunks, multiply, 0)
    write_heads(kv_ref, acc_scr)


def write_heads(kv_ref, acc_scr):
    heads = kv_ref.shape[0]
    for head in range(heads):
        for part in range(2):
            first = (part * heads + head) * HEAD_DIM
            source = acc_scr[:, first : first + HEAD_DIM]
            kv_ref[head, :, part * HEAD_DIM : (part + 1) * HEAD_DIM] = source.astype(jnp.bfloat16)


def norm_project(hidden, gain, key_weight, value_weight):
    rows, features = hidden.shape
    width = key_weight.shape[1] // UNITS
    chunk = features // CHUNKS
    whole = pl.BlockSpec(memory_space=pltpu.VMEM)
    held = pl.BlockSpec(memory_space=pltpu.HBM)
    return pl.pallas_call(
        norm_project_kernel,
        in_specs=[held, whole, held, held],
        out_specs=[whole, whole],
        out_shape=[
            jax.ShapeDtypeStruct((rows, 128), jnp.float32),
            jax.ShapeDtypeStruct((width // HEAD_DIM, rows, 2 * HEAD_DIM), jnp.bfloat16),
        ],
        scratch_shapes=[
            pltpu.VMEM((rows, features), jnp.bfloat16),
            pltpu.VMEM((CHUNKS, chunk, 2 * width), jnp.bfloat16),
            pltpu.VMEM((rows, 2 * width), jnp.float32),
            pltpu.SemaphoreType.DMA((LOADS,)),
            pltpu.SemaphoreType.DMA((CHUNKS,)),
            pltpu.SemaphoreType.DMA((CHUNKS,)),
        ],
        compiler_params=pltpu.CompilerParams(vmem_limit_bytes=57 * MIB),
        cost_estimate=pl.CostEstimate(
            flops=4 * rows * features * width, bytes_accessed=16 * MIB, transcendentals=0
        ),
        name="norm_project",
    )(hidden, gain.reshape(1, features), key_weight, value_weight)


def project_kernel(x_ref, scale_ref, gain_ref, key_ref, value_ref, kv_ref, acc_scr):
    step = pl.program_id(0)
    rows, chunk = x_ref.shape
    width = key_ref.shape[1]
    lanes = 128
    inverse = scale_ref[...]
    parts = []
    for lane in range(0, chunk, lanes):
        cols = slice(lane, lane + lanes)
        x = x_ref[:, cols].astype(jnp.float32)
        parts.append((x * inverse * gain_ref[:, cols]).astype(jnp.bfloat16))
    normed = jnp.concatenate(parts, axis=1)
    for part, weight in enumerate((key_ref, value_ref)):
        cols = slice(part * width, (part + 1) * width)
        term = jnp.dot(normed, weight[...], preferred_element_type=jnp.float32)
        acc_scr[:, cols] = jnp.where(step == 0, term, acc_scr[:, cols] + term)

    @pl.when(step == CHUNKS - 1)
    def _():
        write_heads(kv_ref, acc_scr)


def project(hidden, scale, gain, key_weight, value_weight, unit):
    rows, features = hidden.shape
    chunk = features // CHUNKS
    width = key_weight.shape[1] // UNITS
    weight = pl.BlockSpec((chunk, width), lambda i: (i, unit))
    return pl.pallas_call(
        project_kernel,
        grid=(CHUNKS,),
        in_specs=[
            pl.BlockSpec((rows, chunk), lambda i: (0, i)),
            pl.BlockSpec(scale.shape, lambda i: (0, 0)),
            pl.BlockSpec((1, chunk), lambda i: (0, i)),
            weight,
            weight,
        ],
        out_specs=pl.BlockSpec((width // HEAD_DIM, rows, 2 * HEAD_DIM), lambda i: (0, 0, 0)),
        out_shape=jax.ShapeDtypeStruct((width // HEAD_DIM, rows, 2 * HEAD_DIM), jnp.bfloat16),
        scratch_shapes=[pltpu.VMEM((rows, 2 * width), jnp.float32)],
        compiler_params=pltpu.CompilerParams(vmem_limit_bytes=57 * MIB),
        cost_estimate=pl.CostEstimate(
            flops=4 * rows * features * width, bytes_accessed=16 * MIB, transcendentals=0
        ),
        name="project",
    )(hidden, scale, gain.reshape(1, features), key_weight, value_weight)


def attention_kernel(block, unit, near, slot_ref, cut_ref, odd_ref, q_hbm, *refs):
    own_hbm, straight, crossed = refs[0], refs[1 : near + 1], refs[near + 1 : 2 * near + 2]
    out_hbm, kv_scr, q_scr, out_scr, kv_sem, q_sem, out_sem = refs[-7:]
    kv_heads, levels, rows, width = kv_scr.shape
    depth = levels - 1
    steps, tall, wide = q_scr.shape
    per_head = steps // kv_heads
    per_group = wide // HEAD_DIM
    scale = HEAD_DIM**-0.5 * LOG2E

    def load_kv(head):
        def copy(ref, level, number):
            return pltpu.make_async_copy(
                ref.at[head],
                kv_scr.at[head, level],
                kv_sem.at[head, number],
            )

        copies = [copy(own_hbm, depth, 0)]
        for s, ref in enumerate(straight):
            copies.append(copy(ref, 2 * s + 1, s + 1))
        for s, ref in enumerate(crossed):
            level = 2 * lax.rem(s + odd_ref[0] + near, near + 1)
            copies.append(copy(ref, level, near + s + 1))
        return copies

    def place(ref, step):
        head, part = lax.div(step, per_head), lax.rem(step, per_head)
        span = pl.ds(pl.multiple_of(part * tall, tall), tall)
        cols = pl.ds(pl.multiple_of((unit * kv_heads + head) * wide, wide), wide)
        return ref.at[span, cols]

    def load_q(step):
        return pltpu.make_async_copy(place(q_hbm, step), q_scr.at[step], q_sem.at[step])

    def store(step):
        return pltpu.make_async_copy(out_scr.at[step], place(out_hbm, step), out_sem.at[step])

    for head in range(kv_heads):
        for copy in load_kv(head):
            copy.start()
        for step in range(head * per_head, (head + 1) * per_head):
            load_q(step).start()

    token = lax.broadcasted_iota(jnp.int32, (block, HEAD_DIM), 0)
    lane = lax.broadcasted_iota(jnp.int32, (block, HEAD_DIM), 1)
    hidden_later = jnp.where((lane >= block) & (lane - block > token), MASKED, 0.0)
    query_mask = jnp.where(lane == 0, 1.0, hidden_later).astype(jnp.bfloat16)
    query_mask = jnp.concatenate([query_mask] * per_group, axis=0)
    own_mask = jnp.where(lane - block == token, 1.0, 0.0).astype(jnp.bfloat16)

    def score(step, local):
        head = lax.div(step, per_head)
        here = lax.rem(step, per_head) * BLOCKS_PER_STEP + local
        pieces, masks = [], []
        for k in range(depth):
            span = pl.ds(pl.multiple_of(slot_ref[here, k] * block, block), block)
            pieces.append(kv_scr[head, k, span, :])
            unseen = (lane == 0) & (token >= cut_ref[here, k])
            masks.append(jnp.where(unseen, MASKED, 0.0).astype(jnp.bfloat16))
        span = pl.ds(pl.multiple_of(here * block, block), block)
        pieces.append(kv_scr[head, depth, span, :])
        masks.append(own_mask)
        every = jnp.concatenate(pieces, axis=0)
        keys = jnp.concatenate([every[:, :HEAD_DIM], jnp.concatenate(masks, axis=0)], axis=1)
        span = slice(local * block, (local + 1) * block)
        queries = jnp.concatenate(
            [q_scr[step, span, r * HEAD_DIM : (r + 1) * HEAD_DIM] for r in range(per_group)], axis=0
        )
        queries = jnp.concatenate([queries, query_mask], axis=1)
        scores = lax.dot_general(
            queries, keys, (((1,), (1,)), ((), ())), preferred_element_type=jnp.float32
        )
        return scores, every[:, HEAD_DIM:]

    def finish(step, local, scores, values):
        peak = jnp.max(scores, axis=-1, keepdims=True)
        weights = jnp.exp2((scores - peak) * scale).astype(jnp.bfloat16)
        padded = jnp.concatenate([values, jnp.ones_like(values)], axis=1)
        both = jnp.dot(weights, padded, preferred_element_type=jnp.float32)
        context = (both[:, :HEAD_DIM] * (1.0 / both[:, HEAD_DIM:])).astype(jnp.bfloat16)
        span = slice(local * block, (local + 1) * block)
        for r in range(per_group):
            out_scr[step, span, r * HEAD_DIM : (r + 1) * HEAD_DIM] = context[
                r * block : (r + 1) * block
            ]

    def body(step, carry):
        load_q(step).wait()
        for head in range(kv_heads):

            @pl.when(step == head * per_head)
            def _(head=head):
                for copy in load_kv(head):
                    copy.wait()

        waiting = None
        for local in range(BLOCKS_PER_STEP):
            scores, values = score(step, local)
            if waiting is not None:
                finish(step, *waiting)
            waiting = (local, scores, values)
        finish(step, *waiting)
        store(step).start()
        return carry

    lax.fori_loop(0, steps, body, 0)
    for step in range(steps):
        store(step).wait()


def attention(slots, cuts, odd, queries, own, straight, crossed, unit, previous):
    rows, features = queries.shape
    blocks, depth = slots.shape
    block = rows // blocks
    near = len(straight)
    kv_heads = own.shape[0]
    wide = features // UNITS // kv_heads
    steps = kv_heads * blocks // BLOCKS_PER_STEP
    held = pl.BlockSpec(memory_space=pltpu.HBM)
    table = pl.BlockSpec(memory_space=pltpu.SMEM)
    operands = [slots, cuts, odd, queries, own, *straight, *crossed]
    aliases = {}
    if previous is not None:
        aliases = {len(operands): 0}
        operands.append(previous)
    return pl.pallas_call(
        functools.partial(attention_kernel, block, unit, near),
        in_specs=[table] * 3 + [held] * (len(operands) - 3),
        out_specs=held,
        out_shape=jax.ShapeDtypeStruct((rows, features), jnp.bfloat16),
        input_output_aliases=aliases,
        scratch_shapes=[
            pltpu.VMEM((kv_heads, depth + 1, rows, 2 * HEAD_DIM), own.dtype),
            pltpu.VMEM((steps, BLOCKS_PER_STEP * block, wide), jnp.bfloat16),
            pltpu.VMEM((steps, BLOCKS_PER_STEP * block, wide), jnp.bfloat16),
            pltpu.SemaphoreType.DMA((kv_heads, depth + 1)),
            pltpu.SemaphoreType.DMA((steps,)),
            pltpu.SemaphoreType.DMA((steps,)),
        ],
        compiler_params=pltpu.CompilerParams(vmem_limit_bytes=57 * MIB),
        cost_estimate=pl.CostEstimate(
            flops=4 * rows * wide * kv_heads * (depth + 1) * block,
            bytes_accessed=8 * MIB,
            transcendentals=rows * wide // HEAD_DIM * kv_heads * (depth + 1) * block,
        ),
        name="attention",
    )(*operands)


def shards(hidden, queries, norm_gain, key_weight, value_weight, anc_ids, anc_cut):
    blocks, depth = anc_ids.shape
    levels = depth + 1
    size = lax.axis_size("node")
    chains = size // levels
    near = depth // 2
    half = [index // chains // 2 for index in range(size)]
    even = [index // chains % 2 == 0 for index in range(size)]
    other = [index + chains if even[index] else index - chains for index in range(size)]
    odd = (lax.axis_index("node") // chains % 2).astype(jnp.int32).reshape(1)
    slots = jnp.where(anc_ids >= 0, anc_ids % blocks, 0)

    scale, first = norm_project(hidden, norm_gain, key_weight, value_weight)
    own = [first, project(hidden, scale, norm_gain, key_weight, value_weight, 1)]
    def after(array, *earlier):
        return lax.optimization_barrier((array, *earlier))[0]

    column = 2 * chains
    moved = {("own", 0, 0): own[0], ("own", 0, 1): own[1]}

    def step(kind, s, unit, waits):
        if kind == "across":
            source = ("along", s, unit) if s else ("own", 0, unit)
            exchange = s > 0 or unit == UNITS - 1
            pairs = [
                (i, other[i])
                for i in range(size)
                if half[i] >= s and (even[i] or (exchange and half[i] == 0) or s > 0)
            ]
        elif kind == "along":
            source = ("along", s - 1, unit) if s > 1 else ("own", 0, unit)
            pairs = [(i, i + column) for i in range(size - column) if half[i] >= s - 1]
        else:
            source = ("across" if kind == "down" else "own", 0, unit)
            pairs = [(i, i + s * column) for i in range(size - s * column)]
        array = lax.optimization_barrier((moved[source], *[moved[w] for w in waits]))[0]
        key = "along" if kind == "direct" else kind
        moved[key, s, unit] = lax.ppermute(array, "node", pairs)

    for kind, s, unit, waits in PLAN:
        step(kind, s, unit, waits)
    result = None
    for unit in range(UNITS):
        result = attention(
            slots,
            anc_cut,
            odd,
            queries,
            own[unit],
            [moved["along", s, unit] for s in range(1, near + 1)],
            [moved["across", s, unit] for s in range(near)]
            + [moved["across" if unit == 0 else "down", near, unit]],
            unit,
            result,
        )
    return result


def solution(mesh):
    placed = (
        P(("groups", "node"), None),
        P(("groups", "node"), None),
        P(),
        P(),
        P(),
        P(("groups", "node"), None),
        P(("groups", "node"), None),
    )
    return jax.shard_map(
        shards, mesh=mesh, in_specs=placed, out_specs=P(("groups", "node"), None), check_vma=False
    )
```

```python
import functools
import jax
import jax.numpy as jnp
from jax import lax
from jax.experimental import pallas as pl
from jax.experimental.pallas import tpu as pltpu
from jax.sharding import PartitionSpec as P

HEAD_DIM = 128
EPS = 1e-05
LOG2E = 1.4426950408889634
MASKED = -1e30
MIB = 1024 * 1024
CHUNKS = 4
LOADS = 16
UNITS = 2
BLOCKS_PER_STEP = 8


PLAN = (
    ("across", 0, 0, ()),
    ("along", 1, 0, ()),
    ("across", 0, 1, ()),
    ("along", 1, 1, ()),
    ("across", 1, 0, (("across", 0, 0),)),
    ("along", 2, 0, (("along", 1, 0),)),
    ("across", 1, 1, (("across", 0, 1),)),
    ("along", 3, 0, (("along", 1, 1),)),
    ("across", 2, 0, (("across", 1, 0),)),
    ("along", 2, 1, (("along", 2, 0),)),
    ("across", 3, 0, (("across", 1, 1),)),
    ("across", 2, 1, (("across", 2, 0), ("across", 1, 1))),
    ("down", 3, 1, (("along", 3, 0),)),
    ("along", 3, 1, (("along", 2, 1),)),
)


def norm_project_kernel(
    x_hbm, gain_ref, key_hbm, value_hbm, scale_ref, kv_ref,
    x_scr, weight_scr, acc_scr, x_sem, key_sem, value_sem,
):
    rows, features = x_scr.shape
    loads = LOADS
    tall = rows // loads
    chunks, chunk = weight_scr.shape[:2]
    width = weight_scr.shape[2] // 2
    lanes = 128

    def span(c):
        return pl.ds(pl.multiple_of(c * chunk, chunk), chunk)

    def load_x(c):
        row = pl.ds(pl.multiple_of(c * tall, tall), tall)
        return pltpu.make_async_copy(x_hbm.at[row], x_scr.at[row], x_sem.at[c])

    def load_weights(c):
        head = pl.ds(0, width)
        return [
            pltpu.make_async_copy(
                key_hbm.at[span(c), head], weight_scr.at[c, :, pl.ds(0, width)], key_sem.at[c]
            ),
            pltpu.make_async_copy(
                value_hbm.at[span(c), head], weight_scr.at[c, :, pl.ds(width, width)], value_sem.at[c]
            ),
        ]

    for c in range(loads):
        load_x(c).start()

    def square(c, carry):
        load_x(c).wait()

        @pl.when(c == loads - 4)
        def _():
            for copy in load_weights(0):
                copy.start()

        row = pl.ds(pl.multiple_of(c * tall, tall), tall)
        total = jnp.zeros((tall, lanes), jnp.float32)
        for lane in range(0, features, lanes):
            x = x_scr[row, lane : lane + lanes].astype(jnp.float32)
            total += x * x
        scale_ref[row, :] = total
        return carry

    lax.fori_loop(0, loads, square, 0)
    for c in range(1, chunks):
        for copy in load_weights(c):
            copy.start()
    mean_sq = jnp.sum(scale_ref[...], axis=-1, keepdims=True) / features
    scale_ref[...] = jnp.broadcast_to(lax.rsqrt(mean_sq + EPS), scale_ref.shape)

    acc_scr[...] = jnp.zeros_like(acc_scr)

    def multiply(c, carry):
        for copy in load_weights(c):
            copy.wait()
        inverse = scale_ref[...]
        parts = []
        for lane in range(0, chunk, lanes):
            cols = pl.ds(pl.multiple_of(c * chunk + lane, lanes), lanes)
            x = x_scr[:, cols].astype(jnp.float32)
            parts.append((x * inverse * gain_ref[:, cols]).astype(jnp.bfloat16))
        normed = jnp.concatenate(parts, axis=1)
        acc_scr[...] += jnp.dot(normed, weight_scr[c], preferred_element_type=jnp.float32)
        return carry

    lax.fori_loop(0, chunks, multiply, 0)
    write_heads(kv_ref, acc_scr)


def write_heads(kv_ref, acc_scr):
    heads = kv_ref.shape[0]
    for head in range(heads):
        for part in range(2):
            first = (part * heads + head) * HEAD_DIM
            source = acc_scr[:, first : first + HEAD_DIM]
            kv_ref[head, :, part * HEAD_DIM : (part + 1) * HEAD_DIM] = source.astype(jnp.bfloat16)


def norm_project(hidden, gain, key_weight, value_weight):
    rows, features = hidden.shape
    width = key_weight.shape[1] // UNITS
    chunk = features // CHUNKS
    whole = pl.BlockSpec(memory_space=pltpu.VMEM)
    held = pl.BlockSpec(memory_space=pltpu.HBM)
    return pl.pallas_call(
        norm_project_kernel,
        in_specs=[held, whole, held, held],
        out_specs=[whole, whole],
        out_shape=[
            jax.ShapeDtypeStruct((rows, 128), jnp.float32),
            jax.ShapeDtypeStruct((width // HEAD_DIM, rows, 2 * HEAD_DIM), jnp.bfloat16),
        ],
        scratch_shapes=[
            pltpu.VMEM((rows, features), jnp.bfloat16),
            pltpu.VMEM((CHUNKS, chunk, 2 * width), jnp.bfloat16),
            pltpu.VMEM((rows, 2 * width), jnp.float32),
            pltpu.SemaphoreType.DMA((LOADS,)),
            pltpu.SemaphoreType.DMA((CHUNKS,)),
            pltpu.SemaphoreType.DMA((CHUNKS,)),
        ],
        compiler_params=pltpu.CompilerParams(vmem_limit_bytes=57 * MIB),
        cost_estimate=pl.CostEstimate(
            flops=4 * rows * features * width, bytes_accessed=16 * MIB, transcendentals=0
        ),
        name="norm_project",
    )(hidden, gain.reshape(1, features), key_weight, value_weight)


def project_kernel(x_ref, scale_ref, gain_ref, key_ref, value_ref, kv_ref, acc_scr):
    step = pl.program_id(0)
    rows, chunk = x_ref.shape
    width = key_ref.shape[1]
    lanes = 128
    inverse = scale_ref[...]
    parts = []
    for lane in range(0, chunk, lanes):
        cols = slice(lane, lane + lanes)
        x = x_ref[:, cols].astype(jnp.float32)
        parts.append((x * inverse * gain_ref[:, cols]).astype(jnp.bfloat16))
    normed = jnp.concatenate(parts, axis=1)
    for part, weight in enumerate((key_ref, value_ref)):
        cols = slice(part * width, (part + 1) * width)
        term = jnp.dot(normed, weight[...], preferred_element_type=jnp.float32)
        acc_scr[:, cols] = jnp.where(step == 0, term, acc_scr[:, cols] + term)

    @pl.when(step == CHUNKS - 1)
    def _():
        write_heads(kv_ref, acc_scr)


def project(hidden, scale, gain, key_weight, value_weight, unit):
    rows, features = hidden.shape
    chunk = features // CHUNKS
    width = key_weight.shape[1] // UNITS
    weight = pl.BlockSpec((chunk, width), lambda i: (i, unit))
    return pl.pallas_call(
        project_kernel,
        grid=(CHUNKS,),
        in_specs=[
            pl.BlockSpec((rows, chunk), lambda i: (0, i)),
            pl.BlockSpec(scale.shape, lambda i: (0, 0)),
            pl.BlockSpec((1, chunk), lambda i: (0, i)),
            weight,
            weight,
        ],
        out_specs=pl.BlockSpec((width // HEAD_DIM, rows, 2 * HEAD_DIM), lambda i: (0, 0, 0)),
        out_shape=jax.ShapeDtypeStruct((width // HEAD_DIM, rows, 2 * HEAD_DIM), jnp.bfloat16),
        scratch_shapes=[pltpu.VMEM((rows, 2 * width), jnp.float32)],
        compiler_params=pltpu.CompilerParams(vmem_limit_bytes=57 * MIB),
        cost_estimate=pl.CostEstimate(
            flops=4 * rows * features * width, bytes_accessed=16 * MIB, transcendentals=0
        ),
        name="project",
    )(hidden, scale, gain.reshape(1, features), key_weight, value_weight)


def attention_kernel(block, unit, near, slot_ref, cut_ref, odd_ref, q_hbm, *refs):
    own_hbm, straight, crossed = refs[0], refs[1 : near + 1], refs[near + 1 : 2 * near + 2]
    out_hbm, kv_scr, q_scr, out_scr, kv_sem, q_sem, out_sem = refs[-7:]
    kv_heads, levels, rows, width = kv_scr.shape
    depth = levels - 1
    steps, tall, wide = q_scr.shape
    per_head = steps // kv_heads
    per_group = wide // HEAD_DIM
    scale = HEAD_DIM**-0.5 * LOG2E

    def load_kv(head):
        def copy(ref, level, number):
            return pltpu.make_async_copy(
                ref.at[head],
                kv_scr.at[head, level],
                kv_sem.at[head, number],
            )

        copies = [copy(own_hbm, depth, 0)]
        for s, ref in enumerate(straight):
            copies.append(copy(ref, 2 * s + 1, s + 1))
        for s, ref in enumerate(crossed):
            level = 2 * lax.rem(s + odd_ref[0] + near, near + 1)
            copies.append(copy(ref, level, near + s + 1))
        return copies

    def place(ref, step):
        head, part = lax.div(step, per_head), lax.rem(step, per_head)
        span = pl.ds(pl.multiple_of(part * tall, tall), tall)
        cols = pl.ds(pl.multiple_of((unit * kv_heads + head) * wide, wide), wide)
        return ref.at[span, cols]

    def load_q(step):
        return pltpu.make_async_copy(place(q_hbm, step), q_scr.at[step], q_sem.at[step])

    def store(step):
        return pltpu.make_async_copy(out_scr.at[step], place(out_hbm, step), out_sem.at[step])

    for head in range(kv_heads):
        for copy in load_kv(head):
            copy.start()
        for step in range(head * per_head, (head + 1) * per_head):
            load_q(step).start()

    token = lax.broadcasted_iota(jnp.int32, (block, HEAD_DIM), 0)
    lane = lax.broadcasted_iota(jnp.int32, (block, HEAD_DIM), 1)
    hidden_later = jnp.where((lane >= block) & (lane - block > token), MASKED, 0.0)
    query_mask = jnp.where(lane == 0, 1.0, hidden_later).astype(jnp.bfloat16)
    query_mask = jnp.concatenate([query_mask] * per_group, axis=0)
    own_mask = jnp.where(lane - block == token, 1.0, 0.0).astype(jnp.bfloat16)

    def score(step, local):
        head = lax.div(step, per_head)
        here = lax.rem(step, per_head) * BLOCKS_PER_STEP + local
        pieces, masks = [], []
        for k in range(depth):
            span = pl.ds(pl.multiple_of(slot_ref[here, k] * block, block), block)
            pieces.append(kv_scr[head, k, span, :])
            unseen = (lane == 0) & (token >= cut_ref[here, k])
            masks.append(jnp.where(unseen, MASKED, 0.0).astype(jnp.bfloat16))
        span = pl.ds(pl.multiple_of(here * block, block), block)
        pieces.append(kv_scr[head, depth, span, :])
        masks.append(own_mask)
        every = jnp.concatenate(pieces, axis=0)
        keys = jnp.concatenate([every[:, :HEAD_DIM], jnp.concatenate(masks, axis=0)], axis=1)
        span = slice(local * block, (local + 1) * block)
        queries = jnp.concatenate(
            [q_scr[step, span, r * HEAD_DIM : (r + 1) * HEAD_DIM] for r in range(per_group)], axis=0
        )
        queries = jnp.concatenate([queries, query_mask], axis=1)
        scores = lax.dot_general(
            queries, keys, (((1,), (1,)), ((), ())), preferred_element_type=jnp.float32
        )
        return scores, every[:, HEAD_DIM:]

    def finish(step, local, scores, values):
        peak = jnp.max(scores, axis=-1, keepdims=True)
        weights = jnp.exp2((scores - peak) * scale).astype(jnp.bfloat16)
        padded = jnp.concatenate([values, jnp.ones_like(values)], axis=1)
        both = jnp.dot(weights, padded, preferred_element_type=jnp.float32)
        context = (both[:, :HEAD_DIM] * (1.0 / both[:, HEAD_DIM:])).astype(jnp.bfloat16)
        span = slice(local * block, (local + 1) * block)
        for r in range(per_group):
            out_scr[step, span, r * HEAD_DIM : (r + 1) * HEAD_DIM] = context[
                r * block : (r + 1) * block
            ]

    def body(step, carry):
        load_q(step).wait()
        for head in range(kv_heads):

            @pl.when(step == head * per_head)
            def _(head=head):
                for copy in load_kv(head):
                    copy.wait()

        waiting = None
        for local in range(BLOCKS_PER_STEP):
            scores, values = score(step, local)
            if waiting is not None:
                finish(step, *waiting)
            waiting = (local, scores, values)
        finish(step, *waiting)
        store(step).start()
        return carry

    lax.fori_loop(0, steps, body, 0)
    for step in range(steps):
        store(step).wait()


def attention(slots, cuts, odd, queries, own, straight, crossed, unit, previous):
    rows, features = queries.shape
    blocks, depth = slots.shape
    block = rows // blocks
    near = len(straight)
    kv_heads = own.shape[0]
    wide = features // UNITS // kv_heads
    steps = kv_heads * blocks // BLOCKS_PER_STEP
    held = pl.BlockSpec(memory_space=pltpu.HBM)
    table = pl.BlockSpec(memory_space=pltpu.SMEM)
    operands = [slots, cuts, odd, queries, own, *straight, *crossed]
    aliases = {}
    if previous is not None:
        aliases = {len(operands): 0}
        operands.append(previous)
    return pl.pallas_call(
        functools.partial(attention_kernel, block, unit, near),
        in_specs=[table] * 3 + [held] * (len(operands) - 3),
        out_specs=held,
        out_shape=jax.ShapeDtypeStruct((rows, features), jnp.bfloat16),
        input_output_aliases=aliases,
        scratch_shapes=[
            pltpu.VMEM((kv_heads, depth + 1, rows, 2 * HEAD_DIM), own.dtype),
            pltpu.VMEM((steps, BLOCKS_PER_STEP * block, wide), jnp.bfloat16),
            pltpu.VMEM((steps, BLOCKS_PER_STEP * block, wide), jnp.bfloat16),
            pltpu.SemaphoreType.DMA((kv_heads, depth + 1)),
            pltpu.SemaphoreType.DMA((steps,)),
            pltpu.SemaphoreType.DMA((steps,)),
        ],
        compiler_params=pltpu.CompilerParams(vmem_limit_bytes=57 * MIB),
        cost_estimate=pl.CostEstimate(
            flops=4 * rows * wide * kv_heads * (depth + 1) * block,
            bytes_accessed=8 * MIB,
            transcendentals=rows * wide // HEAD_DIM * kv_heads * (depth + 1) * block,
        ),
        name="attention",
    )(*operands)


def shards(hidden, queries, norm_gain, key_weight, value_weight, anc_ids, anc_cut):
    blocks, depth = anc_ids.shape
    levels = depth + 1
    size = lax.axis_size("node")
    chains = size // levels
    near = depth // 2
    half = [index // chains // 2 for index in range(size)]
    even = [index // chains % 2 == 0 for index in range(size)]
    other = [index + chains if even[index] else index - chains for index in range(size)]
    odd = (lax.axis_index("node") // chains % 2).astype(jnp.int32).reshape(1)
    slots = jnp.where(anc_ids >= 0, anc_ids % blocks, 0)

    scale, first = norm_project(hidden, norm_gain, key_weight, value_weight)
    own = [first, project(hidden, scale, norm_gain, key_weight, value_weight, 1)]
    def after(array, *earlier):
        return lax.optimization_barrier((array, *earlier))[0]

    column = 2 * chains
    moved = {("own", 0, 0): own[0], ("own", 0, 1): own[1]}

    def step(kind, s, unit, waits):
        if kind == "across":
            source = ("along", s, unit) if s else ("own", 0, unit)
            exchange = s > 0 or unit == UNITS - 1
            pairs = [
                (i, other[i])
                for i in range(size)
                if half[i] >= s and (even[i] or (exchange and half[i] == 0) or s > 0)
            ]
        elif kind == "along":
            source = ("along", s - 1, unit) if s > 1 else ("own", 0, unit)
            pairs = [(i, i + column) for i in range(size - column) if half[i] >= s - 1]
        else:
            source = ("across" if kind == "down" else "own", 0, unit)
            pairs = [(i, i + s * column) for i in range(size - s * column)]
        array = lax.optimization_barrier((moved[source], *[moved[w] for w in waits]))[0]
        key = "along" if kind == "direct" else kind
        moved[key, s, unit] = lax.ppermute(array, "node", pairs)

    for kind, s, unit, waits in PLAN:
        step(kind, s, unit, waits)
    result = None
    for unit in range(UNITS):
        result = attention(
            slots,
            anc_cut,
            odd,
            queries,
            own[unit],
            [moved["along", s, unit] for s in range(1, near + 1)],
            [moved["across", s, unit] for s in range(near)]
            + [moved["across" if unit == 0 else "down", near, unit]],
            unit,
            result,
        )
    return result


def solution(mesh):
    placed = (
        P(("groups", "node"), None),
        P(("groups", "node"), None),
        P(),
        P(),
        P(),
        P(("groups", "node"), None),
        P(("groups", "node"), None),
    )
    return jax.shard_map(
        shards, mesh=mesh, in_specs=placed, out_specs=P(("groups", "node"), None), check_vma=False
    )
```

```python
import functools
import jax
import jax.numpy as jnp
from jax import lax
from jax.experimental import pallas as pl
from jax.experimental.pallas import tpu as pltpu
from jax.sharding import PartitionSpec as P

HEAD_DIM = 128
EPS = 1e-05
LOG2E = 1.4426950408889634
MASKED = -1e30
MIB = 1024 * 1024
CHUNKS = 4
LOADS = 16
UNITS = 2
BLOCKS_PER_STEP = 8
STORED = 2


PLAN = (
    ("across", 0, 0, ()),
    ("along", 1, 0, ()),
    ("across", 0, 1, ()),
    ("along", 1, 1, ()),
    ("across", 1, 0, (("across", 0, 0),)),
    ("along", 2, 0, (("along", 1, 0),)),
    ("across", 1, 1, (("across", 0, 1),)),
    ("along", 3, 0, (("along", 1, 1),)),
    ("across", 2, 0, (("across", 1, 0),)),
    ("along", 2, 1, (("along", 2, 0),)),
    ("across", 3, 0, (("across", 1, 1),)),
    ("across", 2, 1, (("across", 2, 0), ("across", 1, 1))),
    ("down", 3, 1, (("along", 3, 0),)),
    ("along", 3, 1, (("along", 2, 1),)),
)


def norm_project_kernel(
    x_hbm, gain_ref, key_hbm, value_hbm, scale_ref, kv_ref,
    x_scr, weight_scr, acc_scr, x_sem, key_sem, value_sem,
):
    rows, features = x_scr.shape
    loads = LOADS
    tall = rows // loads
    chunks, chunk = weight_scr.shape[:2]
    width = weight_scr.shape[2] // 2
    lanes = 128

    def span(c):
        return pl.ds(pl.multiple_of(c * chunk, chunk), chunk)

    def load_x(c):
        row = pl.ds(pl.multiple_of(c * tall, tall), tall)
        return pltpu.make_async_copy(x_hbm.at[row], x_scr.at[row], x_sem.at[c])

    def load_weights(c):
        head = pl.ds(0, width)
        return [
            pltpu.make_async_copy(
                key_hbm.at[span(c), head], weight_scr.at[c, :, pl.ds(0, width)], key_sem.at[c]
            ),
            pltpu.make_async_copy(
                value_hbm.at[span(c), head], weight_scr.at[c, :, pl.ds(width, width)], value_sem.at[c]
            ),
        ]

    for c in range(loads):
        load_x(c).start()

    def square(c, carry):
        load_x(c).wait()

        @pl.when(c == loads - 4)
        def _():
            for copy in load_weights(0):
                copy.start()

        row = pl.ds(pl.multiple_of(c * tall, tall), tall)
        total = jnp.zeros((tall, lanes), jnp.float32)
        for lane in range(0, features, lanes):
            x = x_scr[row, lane : lane + lanes].astype(jnp.float32)
            total += x * x
        scale_ref[row, :] = total
        return carry

    lax.fori_loop(0, loads, square, 0)
    for c in range(1, chunks):
        for copy in load_weights(c):
            copy.start()
    mean_sq = jnp.sum(scale_ref[...], axis=-1, keepdims=True) / features
    scale_ref[...] = jnp.broadcast_to(lax.rsqrt(mean_sq + EPS), scale_ref.shape)

    acc_scr[...] = jnp.zeros_like(acc_scr)

    def multiply(c, carry):
        for copy in load_weights(c):
            copy.wait()
        inverse = scale_ref[...]
        parts = []
        for lane in range(0, chunk, lanes):
            cols = pl.ds(pl.multiple_of(c * chunk + lane, lanes), lanes)
            x = x_scr[:, cols].astype(jnp.float32)
            parts.append((x * inverse * gain_ref[:, cols]).astype(jnp.bfloat16))
        normed = jnp.concatenate(parts, axis=1)
        acc_scr[...] += jnp.dot(normed, weight_scr[c], preferred_element_type=jnp.float32)
        return carry

    lax.fori_loop(0, chunks, multiply, 0)
    write_heads(kv_ref, acc_scr)


def write_heads(kv_ref, acc_scr):
    heads = kv_ref.shape[0]
    for head in range(heads):
        for part in range(2):
            first = (part * heads + head) * HEAD_DIM
            source = acc_scr[:, first : first + HEAD_DIM]
            kv_ref[head, :, part * HEAD_DIM : (part + 1) * HEAD_DIM] = source.astype(jnp.bfloat16)


def norm_project(hidden, gain, key_weight, value_weight):
    rows, features = hidden.shape
    width = key_weight.shape[1] // UNITS
    chunk = features // CHUNKS
    whole = pl.BlockSpec(memory_space=pltpu.VMEM)
    held = pl.BlockSpec(memory_space=pltpu.HBM)
    return pl.pallas_call(
        norm_project_kernel,
        in_specs=[held, whole, held, held],
        out_specs=[whole, whole],
        out_shape=[
            jax.ShapeDtypeStruct((rows, 128), jnp.float32),
            jax.ShapeDtypeStruct((width // HEAD_DIM, rows, 2 * HEAD_DIM), jnp.bfloat16),
        ],
        scratch_shapes=[
            pltpu.VMEM((rows, features), jnp.bfloat16),
            pltpu.VMEM((CHUNKS, chunk, 2 * width), jnp.bfloat16),
            pltpu.VMEM((rows, 2 * width), jnp.float32),
            pltpu.SemaphoreType.DMA((LOADS,)),
            pltpu.SemaphoreType.DMA((CHUNKS,)),
            pltpu.SemaphoreType.DMA((CHUNKS,)),
        ],
        compiler_params=pltpu.CompilerParams(vmem_limit_bytes=57 * MIB),
        cost_estimate=pl.CostEstimate(
            flops=4 * rows * features * width, bytes_accessed=16 * MIB, transcendentals=0
        ),
        name="norm_project",
    )(hidden, gain.reshape(1, features), key_weight, value_weight)


def project_kernel(x_ref, scale_ref, gain_ref, key_ref, value_ref, kv_ref, acc_scr):
    step = pl.program_id(0)
    rows, chunk = x_ref.shape
    width = key_ref.shape[1]
    lanes = 128
    inverse = scale_ref[...]
    parts = []
    for lane in range(0, chunk, lanes):
        cols = slice(lane, lane + lanes)
        x = x_ref[:, cols].astype(jnp.float32)
        parts.append((x * inverse * gain_ref[:, cols]).astype(jnp.bfloat16))
    normed = jnp.concatenate(parts, axis=1)
    for part, weight in enumerate((key_ref, value_ref)):
        cols = slice(part * width, (part + 1) * width)
        term = jnp.dot(normed, weight[...], preferred_element_type=jnp.float32)
        acc_scr[:, cols] = jnp.where(step == 0, term, acc_scr[:, cols] + term)

    @pl.when(step == CHUNKS - 1)
    def _():
        write_heads(kv_ref, acc_scr)


def project(hidden, scale, gain, key_weight, value_weight, unit):
    rows, features = hidden.shape
    chunk = features // CHUNKS
    width = key_weight.shape[1] // UNITS
    weight = pl.BlockSpec((chunk, width), lambda i: (i, unit))
    return pl.pallas_call(
        project_kernel,
        grid=(CHUNKS,),
        in_specs=[
            pl.BlockSpec((rows, chunk), lambda i: (0, i)),
            pl.BlockSpec(scale.shape, lambda i: (0, 0)),
            pl.BlockSpec((1, chunk), lambda i: (0, i)),
            weight,
            weight,
        ],
        out_specs=pl.BlockSpec((width // HEAD_DIM, rows, 2 * HEAD_DIM), lambda i: (0, 0, 0)),
        out_shape=jax.ShapeDtypeStruct((width // HEAD_DIM, rows, 2 * HEAD_DIM), jnp.bfloat16),
        scratch_shapes=[pltpu.VMEM((rows, 2 * width), jnp.float32)],
        compiler_params=pltpu.CompilerParams(vmem_limit_bytes=57 * MIB),
        cost_estimate=pl.CostEstimate(
            flops=4 * rows * features * width, bytes_accessed=16 * MIB, transcendentals=0
        ),
        name="project",
    )(hidden, scale, gain.reshape(1, features), key_weight, value_weight)


def attention_kernel(block, unit, near, slot_ref, cut_ref, odd_ref, q_hbm, *refs):
    own_hbm, straight, crossed = refs[0], refs[1 : near + 1], refs[near + 1 : 2 * near + 2]
    out_hbm, kv_scr, q_scr, out_scr, kv_sem, q_sem, out_sem = refs[-7:]
    kv_heads, levels, rows, width = kv_scr.shape
    depth = levels - 1
    steps, tall, wide = q_scr.shape
    per_head = steps // kv_heads
    per_group = wide // HEAD_DIM
    scale = HEAD_DIM**-0.5 * LOG2E

    def load_kv(head):
        def copy(ref, level, number):
            return pltpu.make_async_copy(
                ref.at[head],
                kv_scr.at[head, level],
                kv_sem.at[head, number],
            )

        copies = [copy(own_hbm, depth, 0)]
        for s, ref in enumerate(straight):
            copies.append(copy(ref, 2 * s + 1, s + 1))
        for s, ref in enumerate(crossed):
            level = 2 * lax.rem(s + odd_ref[0] + near, near + 1)
            copies.append(copy(ref, level, near + s + 1))
        return copies

    def place(ref, step):
        head, part = lax.div(step, per_head), lax.rem(step, per_head)
        span = pl.ds(pl.multiple_of(part * tall, tall), tall)
        cols = pl.ds(pl.multiple_of((unit * kv_heads + head) * wide, wide), wide)
        return ref.at[span, cols]

    def load_q(step):
        return pltpu.make_async_copy(place(q_hbm, step), q_scr.at[step], q_sem.at[step])

    def store(step, part):
        span = pl.ds(part * STORED * block, STORED * block)
        return pltpu.make_async_copy(
            out_scr.at[step, span], place(out_hbm, step).at[span], out_sem.at[step, part]
        )

    for head in range(kv_heads):
        for copy in load_kv(head):
            copy.start()
        for step in range(head * per_head, (head + 1) * per_head):
            load_q(step).start()

    token = lax.broadcasted_iota(jnp.int32, (block, HEAD_DIM), 0)
    lane = lax.broadcasted_iota(jnp.int32, (block, HEAD_DIM), 1)
    hidden_later = jnp.where((lane >= block) & (lane - block > token), MASKED, 0.0)
    query_mask = jnp.where(lane == 0, 1.0, hidden_later).astype(jnp.bfloat16)
    query_mask = jnp.concatenate([query_mask] * per_group, axis=0)
    own_mask = jnp.where(lane - block == token, 1.0, 0.0).astype(jnp.bfloat16)

    def score(step, local):
        head = lax.div(step, per_head)
        here = lax.rem(step, per_head) * BLOCKS_PER_STEP + local
        pieces, masks = [], []
        for k in range(depth):
            span = pl.ds(pl.multiple_of(slot_ref[here, k] * block, block), block)
            pieces.append(kv_scr[head, k, span, :])
            unseen = (lane == 0) & (token >= cut_ref[here, k])
            masks.append(jnp.where(unseen, MASKED, 0.0).astype(jnp.bfloat16))
        span = pl.ds(pl.multiple_of(here * block, block), block)
        pieces.append(kv_scr[head, depth, span, :])
        masks.append(own_mask)
        every = jnp.concatenate(pieces, axis=0)
        keys = jnp.concatenate([every[:, :HEAD_DIM], jnp.concatenate(masks, axis=0)], axis=1)
        span = slice(local * block, (local + 1) * block)
        queries = jnp.concatenate(
            [q_scr[step, span, r * HEAD_DIM : (r + 1) * HEAD_DIM] for r in range(per_group)], axis=0
        )
        queries = jnp.concatenate([queries, query_mask], axis=1)
        scores = lax.dot_general(
            queries, keys, (((1,), (1,)), ((), ())), preferred_element_type=jnp.float32
        )
        return scores, every[:, HEAD_DIM:]

    def finish(step, local, scores, values):
        peak = jnp.max(scores, axis=-1, keepdims=True)
        weights = jnp.exp2((scores - peak) * scale).astype(jnp.bfloat16)
        padded = jnp.concatenate([values, jnp.ones_like(values)], axis=1)
        both = jnp.dot(weights, padded, preferred_element_type=jnp.float32)
        context = (both[:, :HEAD_DIM] * (1.0 / both[:, HEAD_DIM:])).astype(jnp.bfloat16)
        span = slice(local * block, (local + 1) * block)
        for r in range(per_group):
            out_scr[step, span, r * HEAD_DIM : (r + 1) * HEAD_DIM] = context[
                r * block : (r + 1) * block
            ]

    def body(step, carry):
        load_q(step).wait()
        for head in range(kv_heads):

            @pl.when(step == head * per_head)
            def _(head=head):
                for copy in load_kv(head):
                    copy.wait()

        def complete(local, scores, values):
            finish(step, local, scores, values)
            if local % STORED == STORED - 1:
                store(step, local // STORED).start()

        waiting = None
        for local in range(BLOCKS_PER_STEP):
            scores, values = score(step, local)
            if waiting is not None:
                complete(*waiting)
            waiting = (local, scores, values)
        complete(*waiting)
        return carry

    lax.fori_loop(0, steps, body, 0)
    for step in range(steps):
        for part in range(BLOCKS_PER_STEP // STORED):
            store(step, part).wait()


def attention(slots, cuts, odd, queries, own, straight, crossed, unit, previous):
    rows, features = queries.shape
    blocks, depth = slots.shape
    block = rows // blocks
    near = len(straight)
    kv_heads = own.shape[0]
    wide = features // UNITS // kv_heads
    steps = kv_heads * blocks // BLOCKS_PER_STEP
    held = pl.BlockSpec(memory_space=pltpu.HBM)
    table = pl.BlockSpec(memory_space=pltpu.SMEM)
    operands = [slots, cuts, odd, queries, own, *straight, *crossed]
    aliases = {}
    if previous is not None:
        aliases = {len(operands): 0}
        operands.append(previous)
    return pl.pallas_call(
        functools.partial(attention_kernel, block, unit, near),
        in_specs=[table] * 3 + [held] * (len(operands) - 3),
        out_specs=held,
        out_shape=jax.ShapeDtypeStruct((rows, features), jnp.bfloat16),
        input_output_aliases=aliases,
        scratch_shapes=[
            pltpu.VMEM((kv_heads, depth + 1, rows, 2 * HEAD_DIM), own.dtype),
            pltpu.VMEM((steps, BLOCKS_PER_STEP * block, wide), jnp.bfloat16),
            pltpu.VMEM((steps, BLOCKS_PER_STEP * block, wide), jnp.bfloat16),
            pltpu.SemaphoreType.DMA((kv_heads, depth + 1)),
            pltpu.SemaphoreType.DMA((steps,)),
            pltpu.SemaphoreType.DMA((steps, BLOCKS_PER_STEP // STORED)),
        ],
        compiler_params=pltpu.CompilerParams(vmem_limit_bytes=57 * MIB),
        cost_estimate=pl.CostEstimate(
            flops=4 * rows * wide * kv_heads * (depth + 1) * block,
            bytes_accessed=8 * MIB,
            transcendentals=rows * wide // HEAD_DIM * kv_heads * (depth + 1) * block,
        ),
        name="attention",
    )(*operands)


def shards(hidden, queries, norm_gain, key_weight, value_weight, anc_ids, anc_cut):
    blocks, depth = anc_ids.shape
    levels = depth + 1
    size = lax.axis_size("node")
    chains = size // levels
    near = depth // 2
    half = [index // chains // 2 for index in range(size)]
    even = [index // chains % 2 == 0 for index in range(size)]
    other = [index + chains if even[index] else index - chains for index in range(size)]
    odd = (lax.axis_index("node") // chains % 2).astype(jnp.int32).reshape(1)
    slots = jnp.where(anc_ids >= 0, anc_ids % blocks, 0)

    scale, first = norm_project(hidden, norm_gain, key_weight, value_weight)
    own = [first, project(hidden, scale, norm_gain, key_weight, value_weight, 1)]
    def after(array, *earlier):
        return lax.optimization_barrier((array, *earlier))[0]

    column = 2 * chains
    moved = {("own", 0, 0): own[0], ("own", 0, 1): own[1]}

    def step(kind, s, unit, waits):
        if kind == "across":
            source = ("along", s, unit) if s else ("own", 0, unit)
            exchange = s > 0 or unit == UNITS - 1
            pairs = [
                (i, other[i])
                for i in range(size)
                if half[i] >= s and (even[i] or (exchange and half[i] == 0) or s > 0)
            ]
        elif kind == "along":
            source = ("along", s - 1, unit) if s > 1 else ("own", 0, unit)
            pairs = [(i, i + column) for i in range(size - column) if half[i] >= s - 1]
        else:
            source = ("across" if kind == "down" else "own", 0, unit)
            pairs = [(i, i + s * column) for i in range(size - s * column)]
        array = lax.optimization_barrier((moved[source], *[moved[w] for w in waits]))[0]
        key = "along" if kind == "direct" else kind
        moved[key, s, unit] = lax.ppermute(array, "node", pairs)

    for kind, s, unit, waits in PLAN:
        step(kind, s, unit, waits)
    result = None
    for unit in range(UNITS):
        result = attention(
            slots,
            anc_cut,
            odd,
            queries,
            own[unit],
            [moved["along", s, unit] for s in range(1, near + 1)],
            [moved["across", s, unit] for s in range(near)]
            + [moved["across" if unit == 0 else "down", near, unit]],
            unit,
            result,
        )
    return result


def solution(mesh):
    placed = (
        P(("groups", "node"), None),
        P(("groups", "node"), None),
        P(),
        P(),
        P(),
        P(("groups", "node"), None),
        P(("groups", "node"), None),
    )
    return jax.shard_map(
        shards, mesh=mesh, in_specs=placed, out_specs=P(("groups", "node"), None), check_vma=False
    )
```

```python
import functools
import jax
import jax.numpy as jnp
from jax import lax
from jax.experimental import pallas as pl
from jax.experimental.pallas import tpu as pltpu
from jax.sharding import PartitionSpec as P

HEAD_DIM = 128
EPS = 1e-05
LOG2E = 1.4426950408889634
MASKED = -1e30
MIB = 1024 * 1024
CHUNKS = 4
LOADS = 16
UNITS = 2
BLOCKS_PER_STEP = 8
STORED = 2


PLAN = (
    ("across", 0, 0, ()),
    ("along", 1, 0, ()),
    ("across", 0, 1, ()),
    ("along", 1, 1, ()),
    ("across", 1, 0, (("across", 0, 0),)),
    ("along", 2, 0, (("along", 1, 0),)),
    ("across", 1, 1, (("across", 0, 1),)),
    ("along", 3, 0, (("along", 1, 1),)),
    ("across", 2, 0, (("across", 1, 0),)),
    ("along", 2, 1, (("along", 2, 0),)),
    ("across", 3, 0, (("across", 1, 1),)),
    ("across", 2, 1, (("across", 2, 0), ("across", 1, 1))),
    ("down", 3, 1, (("along", 3, 0),)),
    ("along", 3, 1, (("along", 2, 1),)),
)


def norm_project_kernel(
    x_hbm, gain_ref, key_hbm, value_hbm, scale_ref, kv_ref,
    x_scr, weight_scr, acc_scr, x_sem, key_sem, value_sem,
):
    rows, features = x_scr.shape
    loads = LOADS
    tall = rows // loads
    chunks, chunk = weight_scr.shape[:2]
    width = weight_scr.shape[2] // 2
    lanes = 128

    def span(c):
        return pl.ds(pl.multiple_of(c * chunk, chunk), chunk)

    def load_x(c):
        row = pl.ds(pl.multiple_of(c * tall, tall), tall)
        return pltpu.make_async_copy(x_hbm.at[row], x_scr.at[row], x_sem.at[c])

    def load_weights(c):
        head = pl.ds(0, width)
        return [
            pltpu.make_async_copy(
                key_hbm.at[span(c), head], weight_scr.at[c, :, pl.ds(0, width)], key_sem.at[c]
            ),
            pltpu.make_async_copy(
                value_hbm.at[span(c), head], weight_scr.at[c, :, pl.ds(width, width)], value_sem.at[c]
            ),
        ]

    for c in range(loads):
        load_x(c).start()
    acc_scr[...] = jnp.zeros_like(acc_scr)

    def square(c, carry):
        load_x(c).wait()

        for early in range(2):

            @pl.when(c == loads - 4 + 2 * early)
            def _(early=early):
                for copy in load_weights(early):
                    copy.start()

        row = pl.ds(pl.multiple_of(c * tall, tall), tall)
        total = jnp.zeros((tall, lanes), jnp.float32)
        for lane in range(0, features, lanes):
            x = x_scr[row, lane : lane + lanes].astype(jnp.float32)
            total += x * x
        scale_ref[row, :] = total
        return carry

    lax.fori_loop(0, loads, square, 0)
    for c in range(2, chunks):
        for copy in load_weights(c):
            copy.start()
    mean_sq = jnp.sum(scale_ref[...], axis=-1, keepdims=True) / features
    scale_ref[...] = jnp.broadcast_to(lax.rsqrt(mean_sq + EPS), scale_ref.shape)

    def multiply(c, carry):
        for copy in load_weights(c):
            copy.wait()
        inverse = scale_ref[...]
        parts = []
        for lane in range(0, chunk, lanes):
            cols = pl.ds(pl.multiple_of(c * chunk + lane, lanes), lanes)
            x = x_scr[:, cols].astype(jnp.float32)
            parts.append((x * inverse * gain_ref[:, cols]).astype(jnp.bfloat16))
        normed = jnp.concatenate(parts, axis=1)
        acc_scr[...] += jnp.dot(normed, weight_scr[c], preferred_element_type=jnp.float32)
        return carry

    lax.fori_loop(0, chunks, multiply, 0)
    write_heads(kv_ref, acc_scr)


def write_heads(kv_ref, acc_scr):
    heads = kv_ref.shape[0]
    for head in range(heads):
        for part in range(2):
            first = (part * heads + head) * HEAD_DIM
            source = acc_scr[:, first : first + HEAD_DIM]
            kv_ref[head, :, part * HEAD_DIM : (part + 1) * HEAD_DIM] = source.astype(jnp.bfloat16)


def norm_project(hidden, gain, key_weight, value_weight):
    rows, features = hidden.shape
    width = key_weight.shape[1] // UNITS
    chunk = features // CHUNKS
    whole = pl.BlockSpec(memory_space=pltpu.VMEM)
    held = pl.BlockSpec(memory_space=pltpu.HBM)
    return pl.pallas_call(
        norm_project_kernel,
        in_specs=[held, whole, held, held],
        out_specs=[whole, whole],
        out_shape=[
            jax.ShapeDtypeStruct((rows, 128), jnp.float32),
            jax.ShapeDtypeStruct((width // HEAD_DIM, rows, 2 * HEAD_DIM), jnp.bfloat16),
        ],
        scratch_shapes=[
            pltpu.VMEM((rows, features), jnp.bfloat16),
            pltpu.VMEM((CHUNKS, chunk, 2 * width), jnp.bfloat16),
            pltpu.VMEM((rows, 2 * width), jnp.float32),
            pltpu.SemaphoreType.DMA((LOADS,)),
            pltpu.SemaphoreType.DMA((CHUNKS,)),
            pltpu.SemaphoreType.DMA((CHUNKS,)),
        ],
        compiler_params=pltpu.CompilerParams(vmem_limit_bytes=57 * MIB),
        cost_estimate=pl.CostEstimate(
            flops=4 * rows * features * width, bytes_accessed=16 * MIB, transcendentals=0
        ),
        name="norm_project",
    )(hidden, gain.reshape(1, features), key_weight, value_weight)


def project_kernel(x_ref, scale_ref, gain_ref, key_ref, value_ref, kv_ref, acc_scr):
    step = pl.program_id(0)
    rows, chunk = x_ref.shape
    width = key_ref.shape[1]
    lanes = 128
    inverse = scale_ref[...]
    parts = []
    for lane in range(0, chunk, lanes):
        cols = slice(lane, lane + lanes)
        x = x_ref[:, cols].astype(jnp.float32)
        parts.append((x * inverse * gain_ref[:, cols]).astype(jnp.bfloat16))
    normed = jnp.concatenate(parts, axis=1)
    for part, weight in enumerate((key_ref, value_ref)):
        cols = slice(part * width, (part + 1) * width)
        term = jnp.dot(normed, weight[...], preferred_element_type=jnp.float32)
        acc_scr[:, cols] = jnp.where(step == 0, term, acc_scr[:, cols] + term)

    @pl.when(step == CHUNKS - 1)
    def _():
        write_heads(kv_ref, acc_scr)


def project(hidden, scale, gain, key_weight, value_weight, unit):
    rows, features = hidden.shape
    chunk = features // CHUNKS
    width = key_weight.shape[1] // UNITS
    weight = pl.BlockSpec((chunk, width), lambda i: (i, unit))
    return pl.pallas_call(
        project_kernel,
        grid=(CHUNKS,),
        in_specs=[
            pl.BlockSpec((rows, chunk), lambda i: (0, i)),
            pl.BlockSpec(scale.shape, lambda i: (0, 0)),
            pl.BlockSpec((1, chunk), lambda i: (0, i)),
            weight,
            weight,
        ],
        out_specs=pl.BlockSpec((width // HEAD_DIM, rows, 2 * HEAD_DIM), lambda i: (0, 0, 0)),
        out_shape=jax.ShapeDtypeStruct((width // HEAD_DIM, rows, 2 * HEAD_DIM), jnp.bfloat16),
        scratch_shapes=[pltpu.VMEM((rows, 2 * width), jnp.float32)],
        compiler_params=pltpu.CompilerParams(vmem_limit_bytes=57 * MIB),
        cost_estimate=pl.CostEstimate(
            flops=4 * rows * features * width, bytes_accessed=16 * MIB, transcendentals=0
        ),
        name="project",
    )(hidden, scale, gain.reshape(1, features), key_weight, value_weight)


def attention_kernel(block, unit, near, slot_ref, cut_ref, odd_ref, q_hbm, *refs):
    own_hbm, straight, crossed = refs[0], refs[1 : near + 1], refs[near + 1 : 2 * near + 2]
    out_hbm, kv_scr, q_scr, out_scr, kv_sem, q_sem, out_sem = refs[-7:]
    kv_heads, levels, rows, width = kv_scr.shape
    depth = levels - 1
    steps, tall, wide = q_scr.shape
    per_head = steps // kv_heads
    per_group = wide // HEAD_DIM
    scale = HEAD_DIM**-0.5 * LOG2E

    def load_kv(head):
        def copy(ref, level, number):
            return pltpu.make_async_copy(
                ref.at[head],
                kv_scr.at[head, level],
                kv_sem.at[head, number],
            )

        copies = [copy(own_hbm, depth, 0)]
        for s, ref in enumerate(straight):
            copies.append(copy(ref, 2 * s + 1, s + 1))
        for s, ref in enumerate(crossed):
            level = 2 * lax.rem(s + odd_ref[0] + near, near + 1)
            copies.append(copy(ref, level, near + s + 1))
        return copies

    def place(ref, step):
        head, part = lax.div(step, per_head), lax.rem(step, per_head)
        span = pl.ds(pl.multiple_of(part * tall, tall), tall)
        cols = pl.ds(pl.multiple_of((unit * kv_heads + head) * wide, wide), wide)
        return ref.at[span, cols]

    def load_q(step):
        return pltpu.make_async_copy(place(q_hbm, step), q_scr.at[step], q_sem.at[step])

    def store(step, part):
        span = pl.ds(part * STORED * block, STORED * block)
        return pltpu.make_async_copy(
            out_scr.at[step, span], place(out_hbm, step).at[span], out_sem.at[step, part]
        )

    for head in range(kv_heads):
        for copy in load_kv(head):
            copy.start()
        for step in range(head * per_head, (head + 1) * per_head):
            load_q(step).start()

    token = lax.broadcasted_iota(jnp.int32, (block, HEAD_DIM), 0)
    lane = lax.broadcasted_iota(jnp.int32, (block, HEAD_DIM), 1)
    hidden_later = jnp.where((lane >= block) & (lane - block > token), MASKED, 0.0)
    query_mask = jnp.where(lane == 0, 1.0, hidden_later).astype(jnp.bfloat16)
    query_mask = jnp.concatenate([query_mask] * per_group, axis=0)
    own_mask = jnp.where(lane - block == token, 1.0, 0.0).astype(jnp.bfloat16)

    def score(step, local):
        head = lax.div(step, per_head)
        here = lax.rem(step, per_head) * BLOCKS_PER_STEP + local
        pieces, masks = [], []
        for k in range(depth):
            span = pl.ds(pl.multiple_of(slot_ref[here, k] * block, block), block)
            pieces.append(kv_scr[head, k, span, :])
            unseen = (lane == 0) & (token >= cut_ref[here, k])
            masks.append(jnp.where(unseen, MASKED, 0.0).astype(jnp.bfloat16))
        span = pl.ds(pl.multiple_of(here * block, block), block)
        pieces.append(kv_scr[head, depth, span, :])
        masks.append(own_mask)
        every = jnp.concatenate(pieces, axis=0)
        keys = jnp.concatenate([every[:, :HEAD_DIM], jnp.concatenate(masks, axis=0)], axis=1)
        span = slice(local * block, (local + 1) * block)
        queries = jnp.concatenate(
            [q_scr[step, span, r * HEAD_DIM : (r + 1) * HEAD_DIM] for r in range(per_group)], axis=0
        )
        queries = jnp.concatenate([queries, query_mask], axis=1)
        scores = lax.dot_general(
            queries, keys, (((1,), (1,)), ((), ())), preferred_element_type=jnp.float32
        )
        return scores, every[:, HEAD_DIM:]

    def finish(step, local, scores, values):
        peak = jnp.max(scores, axis=-1, keepdims=True)
        weights = jnp.exp2((scores - peak) * scale).astype(jnp.bfloat16)
        padded = jnp.concatenate([values, jnp.ones_like(values)], axis=1)
        both = jnp.dot(weights, padded, preferred_element_type=jnp.float32)
        context = (both[:, :HEAD_DIM] * (1.0 / both[:, HEAD_DIM:])).astype(jnp.bfloat16)
        span = slice(local * block, (local + 1) * block)
        for r in range(per_group):
            out_scr[step, span, r * HEAD_DIM : (r + 1) * HEAD_DIM] = context[
                r * block : (r + 1) * block
            ]

    def body(step, carry):
        load_q(step).wait()
        for head in range(kv_heads):

            @pl.when(step == head * per_head)
            def _(head=head):
                for copy in load_kv(head):
                    copy.wait()

        def complete(local, scores, values):
            finish(step, local, scores, values)
            if local % STORED == STORED - 1:
                store(step, local // STORED).start()

        waiting = None
        for local in range(BLOCKS_PER_STEP):
            scores, values = score(step, local)
            if waiting is not None:
                complete(*waiting)
            waiting = (local, scores, values)
        complete(*waiting)
        return carry

    lax.fori_loop(0, steps, body, 0)
    for step in range(steps):
        for part in range(BLOCKS_PER_STEP // STORED):
            store(step, part).wait()


def attention(slots, cuts, odd, queries, own, straight, crossed, unit, previous):
    rows, features = queries.shape
    blocks, depth = slots.shape
    block = rows // blocks
    near = len(straight)
    kv_heads = own.shape[0]
    wide = features // UNITS // kv_heads
    steps = kv_heads * blocks // BLOCKS_PER_STEP
    held = pl.BlockSpec(memory_space=pltpu.HBM)
    table = pl.BlockSpec(memory_space=pltpu.SMEM)
    operands = [slots, cuts, odd, queries, own, *straight, *crossed]
    aliases = {}
    if previous is not None:
        aliases = {len(operands): 0}
        operands.append(previous)
    return pl.pallas_call(
        functools.partial(attention_kernel, block, unit, near),
        in_specs=[table] * 3 + [held] * (len(operands) - 3),
        out_specs=held,
        out_shape=jax.ShapeDtypeStruct((rows, features), jnp.bfloat16),
        input_output_aliases=aliases,
        scratch_shapes=[
            pltpu.VMEM((kv_heads, depth + 1, rows, 2 * HEAD_DIM), own.dtype),
            pltpu.VMEM((steps, BLOCKS_PER_STEP * block, wide), jnp.bfloat16),
            pltpu.VMEM((steps, BLOCKS_PER_STEP * block, wide), jnp.bfloat16),
            pltpu.SemaphoreType.DMA((kv_heads, depth + 1)),
            pltpu.SemaphoreType.DMA((steps,)),
            pltpu.SemaphoreType.DMA((steps, BLOCKS_PER_STEP // STORED)),
        ],
        compiler_params=pltpu.CompilerParams(vmem_limit_bytes=57 * MIB),
        cost_estimate=pl.CostEstimate(
            flops=4 * rows * wide * kv_heads * (depth + 1) * block,
            bytes_accessed=8 * MIB,
            transcendentals=rows * wide // HEAD_DIM * kv_heads * (depth + 1) * block,
        ),
        name="attention",
    )(*operands)


def shards(hidden, queries, norm_gain, key_weight, value_weight, anc_ids, anc_cut):
    blocks, depth = anc_ids.shape
    levels = depth + 1
    size = lax.axis_size("node")
    chains = size // levels
    near = depth // 2
    half = [index // chains // 2 for index in range(size)]
    even = [index // chains % 2 == 0 for index in range(size)]
    other = [index + chains if even[index] else index - chains for index in range(size)]
    odd = (lax.axis_index("node") // chains % 2).astype(jnp.int32).reshape(1)
    slots = jnp.where(anc_ids >= 0, anc_ids % blocks, 0)

    scale, first = norm_project(hidden, norm_gain, key_weight, value_weight)
    own = [first, project(hidden, scale, norm_gain, key_weight, value_weight, 1)]
    def after(array, *earlier):
        return lax.optimization_barrier((array, *earlier))[0]

    column = 2 * chains
    moved = {("own", 0, 0): own[0], ("own", 0, 1): own[1]}

    def step(kind, s, unit, waits):
        if kind == "across":
            source = ("along", s, unit) if s else ("own", 0, unit)
            exchange = s > 0 or unit == UNITS - 1
            pairs = [
                (i, other[i])
                for i in range(size)
                if half[i] >= s and (even[i] or (exchange and half[i] == 0) or s > 0)
            ]
        elif kind == "along":
            source = ("along", s - 1, unit) if s > 1 else ("own", 0, unit)
            pairs = [(i, i + column) for i in range(size - column) if half[i] >= s - 1]
        else:
            source = ("across" if kind == "down" else "own", 0, unit)
            pairs = [(i, i + s * column) for i in range(size - s * column)]
        array = lax.optimization_barrier((moved[source], *[moved[w] for w in waits]))[0]
        key = "along" if kind == "direct" else kind
        moved[key, s, unit] = lax.ppermute(array, "node", pairs)

    for kind, s, unit, waits in PLAN:
        step(kind, s, unit, waits)
    result = None
    for unit in range(UNITS):
        result = attention(
            slots,
            anc_cut,
            odd,
            queries,
            own[unit],
            [moved["along", s, unit] for s in range(1, near + 1)],
            [moved["across", s, unit] for s in range(near)]
            + [moved["across" if unit == 0 else "down", near, unit]],
            unit,
            result,
        )
    return result


def solution(mesh):
    placed = (
        P(("groups", "node"), None),
        P(("groups", "node"), None),
        P(),
        P(),
        P(),
        P(("groups", "node"), None),
        P(("groups", "node"), None),
    )
    return jax.shard_map(
        shards, mesh=mesh, in_specs=placed, out_specs=P(("groups", "node"), None), check_vma=False
    )
```
